32 devices in a mesh: pipe: 2 (over x), dp: 16 (over z, y, core).
Axes of the slice: x: 2, y: 2, z: 4, core: 2. Of those that a mesh axis runs over, the one named last changes fastest.
Arguments:
- fields: float32 [32, 48, 16, 128], P('dp', 'pipe'), may hold values from -13 to 13
- item_weights: int32 [32], P('dp'), may hold values from 1 to 96, as said below
- live_counts: int32 [16], P('dp'), may hold values from 0 to 2
- running_stats: float32 [2, 48], P(None, 'pipe'), may hold values from 0.5 to 2
- embed_weight: bfloat16 [48, 4, 1024], replicated, may hold values from -3 to 3
- variable_embed: bfloat16 [48, 1024], replicated, may hold values from -3 to 3
- variable_query: bfloat16 [1024], replicated, may hold values from -6 to 6
- attend_weight: bfloat16 [2, 3, 1024, 1024], P('pipe'), may hold values from -0.1875 to 0.1875
- merge_weight: bfloat16 [2, 1024, 1024], P('pipe'), may hold values from -1 to 1
- position_embed: bfloat16 [512, 1024], replicated, may hold values from -3 to 3
- norm_gain: float32 [2, 1024], replicated, may hold values from 0.5 to 1.5
- norm_bias: float32 [2, 1024], replicated, may hold values from -2 to 2
- up_weight: bfloat16 [1024, 4096], replicated, may hold values from -0.1875 to 0.1875
- hidden_bias: float32 [4096], replicated, may hold values from -3 to 3
- down_weight: bfloat16 [4096, 1024], replicated, may hold values from -0.09375 to 0.09375
- output_bias: float32 [1024], replicated, may hold values from -4 to 4
- cotangent: bfloat16 [32, 512, 1024], P('dp'), may hold values from -6 to 6
Outputs:
- statistics: float32 [2, 48], P(None, 'pipe')
- section_outputs: bfloat16 [2, 32, 512, 1024], P('pipe', 'dp')
- field_grads: float32 [32, 48, 16, 128], P('dp', 'pipe')
- embed_grads: float32 [48, 4, 1024], replicated
- variable_grads: float32 [48, 1024], replicated
- query_grads: float32 [1024], replicated
- attend_grads: float32 [2, 3, 1024, 1024], P('pipe', None, 'dp')
- merge_grads: float32 [2, 1024, 1024], P('pipe', 'dp')
- position_grads: float32 [512, 1024], replicated
- gain_grads: float32 [2, 1024], replicated
- bias_grads: float32 [2, 1024], replicated
- up_grads: float32 [1024, 4096], P(None, ('pipe', 'dp'))
- hidden_grads: float32 [4096], P(('pipe', 'dp'))
- down_grads: float32 [4096, 1024], P(('pipe', 'dp'))
- output_grads: float32 [1024], replicated
The draws below stay inside these ranges and needn't reach their ends.
Inputs may be any that keep to these rules, and one draw needn't show every extreme that they name: `item_weights`: whole numbers.
All inputs are finite; a program needn't handle non-finite values.
Results may differ from the reference program's by a relative error of at most 0.015.
The reference program's roundings to bfloat16 on the way count: a program that leaves them out, or rounds other values in their place, can miss the bound.
Values may be sent and summed in bfloat16 or wider, within the bound.
No kernel may reach another device: no remote copies, remote signals or barrier semaphores. Data moves between devices by JAX's collectives and lax.ppermute only.
A program may use at most 448 MiB of HBM per device.

```python
import math
from functools import partial
import jax
import jax.numpy as jnp
from jax import lax

D = 1024
HEADS = 16
HDIM = 64
FF = 4096
VARS = 48
PATCH = 2
COLS = 128
ROWS = 16
MICRO = 2
PATCHES = 512
REPLICAS = 16
ITEMS = 32


def draw_fields(key, part):
    keys = jax.random.split(key, 3)
    offsets = jax.random.uniform(keys[0], (1, VARS, 1, 1), minval=-2.0, maxval=2.0)
    scales = jnp.exp(jax.random.uniform(keys[1], (1, VARS, 1, 1), minval=math.log(0.3), maxval=math.log(2.0)))
    noise = jnp.clip(jax.random.normal(keys[2], (ITEMS, VARS, ROWS, COLS)), -4.0, 4.0)
    return (offsets + scales * noise).astype(jnp.float32)


def draw_item_weights(key, part):
    keys = jax.random.split(key, 2)
    power = jax.random.randint(keys[0], (ITEMS,), 0, 5)
    base = jax.random.randint(keys[1], (ITEMS,), 1, 3)
    index = jnp.arange(ITEMS, dtype=jnp.int32)
    ramp = 1 + 3 * index // ITEMS
    weights = base * 2 ** power * ramp
    weights = jnp.where(index == ITEMS - 1, 96, weights)
    return weights.astype(jnp.int32)


def draw_live_counts(key, part):
    keys = jax.random.split(key, 3)
    counts = jax.random.randint(keys[0], (REPLICAS,), 0, MICRO + 1)
    fullest = jax.random.randint(keys[1], (), 0, REPLICAS)
    offset = jax.random.randint(keys[2], (), 1, REPLICAS)
    emptiest = (fullest + offset) % REPLICAS
    index = jnp.arange(REPLICAS, dtype=jnp.int32)
    counts = jnp.where(index == fullest, MICRO, counts)
    counts = jnp.where(index == emptiest, 0, counts)
    return counts.astype(jnp.int32)


def levels(own_key, shape, cuts, smallest, top_value):
    level, own = 1.0, jax.random.fold_in(own_key, 6)
    for dim, blocks in cuts:
        steps = jnp.exp(jax.random.uniform(jax.random.fold_in(own, dim), (blocks,), jnp.float32, smallest / len(cuts), top_value / len(cuts)))
        level = level * jnp.repeat(steps, shape[dim] // blocks).reshape([-1 if axis == dim else 1 for axis in range(len(shape))])
    return level


def centred(own_key, extent, deviation, reach, cuts=(), kind=jnp.bfloat16):
    level = levels(own_key, extent, cuts, -0.22, 0.18) if cuts else 1.0
    array = jax.random.normal(own_key, extent, jnp.float32) * deviation * level
    return jnp.minimum(jnp.maximum(array, -reach), reach).astype(kind)


def setup_inputs(seed: int = 0) -> dict:
    key_list = jax.random.split(jax.random.key(seed), 18)
    return {
        "fields": draw_fields(jax.random.fold_in(key_list[17], 71), 0),
        "item_weights": draw_item_weights(jax.random.fold_in(key_list[17], 71), 0),
        "live_counts": draw_live_counts(jax.random.fold_in(key_list[17], 71), 0),
        "running_stats": jnp.clip(jnp.exp(math.log(2.0) - 1.3862944 * jax.random.uniform(key_list[3], (2, VARS), jnp.float32) ** levels(key_list[3], (2, VARS), ((1, 2),), -0.2, 0.2)), 0.5, 2.0),
        "embed_weight": centred(key_list[4], (VARS, PATCH * PATCH, D), (PATCH * PATCH) ** -0.5, 3.0),
        "variable_embed": centred(key_list[5], (VARS, D), 0.5, 3.0),
        "variable_query": centred(key_list[6], (D,), 1.0, 6.0),
        "attend_weight": centred(key_list[7], (2, 3, D, D), D ** -0.5, 0.1875, ((0, 2),)),
        "merge_weight": centred(key_list[8], (2, D, D), (D // 32) ** -0.5, 1.0, ((0, 2),)),
        "position_embed": centred(key_list[9], (PATCHES, D), 0.5, 3.0),
        "norm_gain": jnp.clip(1.0 + 0.1 * jax.random.normal(key_list[10], (2, D), jnp.float32), 0.5, 1.5),
        "norm_bias": centred(key_list[11], (2, D), 0.3, 2.0, (), jnp.float32),
        "up_weight": centred(key_list[12], (D, FF), D ** -0.5, 0.1875),
        "hidden_bias": centred(key_list[13], (FF,), 0.5, 3.0, (), jnp.float32),
        "down_weight": centred(key_list[14], (FF, D), FF ** -0.5, 0.09375),
        "output_bias": centred(key_list[15], (D,), 1.0, 4.0, (), jnp.float32),
        "cotangent": centred(key_list[16], (ITEMS, PATCHES, D), 1.0, 6.0, ((0, 16),)),
    }


PRECISE = lax.Precision.HIGHEST
EPSILON = 1e-05
MOMENTUM = 0.1

@jax.custom_vjp
def low(v):
    return lax.optimization_barrier(v.astype(jnp.bfloat16)).astype(jnp.float32)

@jax.custom_vjp
def low_back(v):
    return v

def low_keep(v):
    return (low(v), None)

def low_pass(kept, grad):
    return (grad,)

def back_keep(v):
    return (v, None)

def back_low(kept, grad):
    return (low(grad),)
low.defvjp(low_keep, low_pass)
low_back.defvjp(back_keep, back_low)

def product(spec, left, right):
    return jnp.einsum(spec, left, right, precision=PRECISE)

def layer_norm(values, gain, bias):
    center = values - lax.optimization_barrier(jnp.mean(values, axis=-1, keepdims=True))
    spread = lax.optimization_barrier(jnp.mean(center * center, axis=-1, keepdims=True))
    return center * lax.rsqrt(spread + EPSILON) * gain + bias

def to_patches(grid):
    count, rows, cols = grid.shape
    split = grid.reshape(count, rows // PATCH, PATCH, cols // PATCH, PATCH)
    return split.transpose(0, 2, 4, 1, 3).reshape(count, PATCH * PATCH, rows // PATCH * (cols // PATCH))

def first_section(field, flag, center, scale, embed, variable_embed, variable_query, attend, merge, position):
    normed = low((field - center[:, None, None]) * scale[:, None, None])
    pixels = to_patches(normed)
    query = low_back(low(product('d,de->e', variable_query, attend[0, 0])))
    key_weight = attend[0, 1].reshape(D, HEADS, HDIM)
    key_query = low_back(low(product('dhe,he->dh', key_weight, query.reshape(HEADS, HDIM)) * HDIM ** (-0.5)))
    pixel_keys = product('vkd,dh->vkh', embed, key_query)
    variable_keys = product('vd,dh->vh', variable_embed, key_query)
    scores = product('vkp,vkh->vhp', pixels, pixel_keys) + variable_keys[:, :, None]
    shares = jax.nn.softmax(scores, axis=0)
    mixed = low(shares[:, None, :, :] * pixels[:, :, None, :])
    mixed_var = low(shares)
    pooled = product('vkhp,vkd->hpd', mixed, embed) + product('vhp,vd->hpd', mixed_var, variable_embed)
    pooled = low_back(low(pooled))
    heads = product('hpd,dhe->phe', pooled, attend[0, 2].reshape(D, HEADS, HDIM)).reshape(-1, D)
    heads = low_back(low(heads))
    return low(flag * (product('pd,de->pe', heads, merge[0]) + position))

def second_section(tokens, attend, merge, gain, bias, up_weight, hidden_bias, down_weight, output_bias):
    inputs = low_back(tokens)
    first_norm = low(layer_norm(inputs, gain[0], bias[0]))
    projected = low_back(low(product('pd,jde->jpe', first_norm, attend[1])))
    triple = projected.reshape(3, -1, HEADS, HDIM)
    scores = low_back(product('phe,qhe->hpq', triple[0], triple[1]) * HDIM ** (-0.5))
    shares = low(jax.nn.softmax(scores, axis=-1))
    context = low_back(low(product('hpq,qhe->phe', shares, triple[2]).reshape(-1, D)))
    middle = inputs + low_back(product('pd,de->pe', context, merge[1]))
    second_norm = low(layer_norm(middle, gain[1], bias[1]))
    hidden = low_back(product('pd,df->pf', second_norm, up_weight) + hidden_bias)
    activation = low(jax.nn.gelu(hidden, approximate=False))
    return middle + low_back(product('pf,fd->pd', activation, down_weight)) + output_bias

def whole_model(alive, center, scale, fields, embed, variable_embed, variable_query, attend, merge, position, gain, bias, up_weight, hidden_bias, down_weight, output_bias):

    def one_item(pair):
        field, flag = pair
        tokens = first_section(field, flag, center, scale, embed, variable_embed, variable_query, attend, merge, position)
        result = second_section(tokens, attend, merge, gain, bias, up_weight, hidden_bias, down_weight, output_bias)
        return (tokens, result)
    return lax.map(jax.checkpoint(one_item), (fields, alive))

def reference(fields, item_weights, live_counts, running_stats, embed_weight, variable_embed, variable_query, attend_weight, merge_weight, position_embed, norm_gain, norm_bias, up_weight, hidden_bias, down_weight, output_bias, cotangent):
    index = jnp.arange(ITEMS, dtype=jnp.int32)
    alive = (index % MICRO < live_counts[index // MICRO]).astype(jnp.float32)
    omega = item_weights.astype(jnp.float32) * alive
    total = jnp.sum(omega)
    live_total = jnp.sum(alive)
    first_moment = lax.optimization_barrier(jnp.sum(omega[:, None] * lax.optimization_barrier(jnp.sum(fields, axis=(2, 3))), axis=0)) / (total * ROWS * COLS)
    second_moment = lax.optimization_barrier(jnp.sum(omega[:, None] * lax.optimization_barrier(jnp.sum(fields * fields, axis=(2, 3))), axis=0)) / (total * ROWS * COLS)
    center_new = (1.0 - MOMENTUM) * running_stats[0] + MOMENTUM * first_moment
    spread_new = (1.0 - MOMENTUM) * running_stats[1] + MOMENTUM * (second_moment - first_moment * first_moment)
    statistics = jnp.stack([center_new, spread_new])
    scale = lax.rsqrt(spread_new + EPSILON)
    grad_scale = omega * live_total / total
    out_grads = cotangent.astype(jnp.float32) * grad_scale[:, None, None]
    floats = [fields, embed_weight, variable_embed, variable_query, attend_weight, merge_weight, position_embed, norm_gain, norm_bias, up_weight, hidden_bias, down_weight, output_bias]
    floats = [entry.astype(jnp.float32) for entry in floats]
    outputs, pull = jax.vjp(partial(whole_model, alive, center_new, scale), *floats)
    tokens, results = outputs
    grads = pull((jnp.zeros_like(tokens), out_grads))
    section_outputs = jnp.stack([tokens, low(alive[:, None, None] * results)]).astype(jnp.bfloat16)
    return (statistics, section_outputs, grads[0], grads[1], grads[2], grads[3], grads[4], grads[5], grads[6], grads[7], grads[8], grads[9], grads[10], grads[11], grads[12])
```

```python
import functools

import jax
import jax.numpy as jnp
from jax import lax
from jax.experimental import pallas as pl
from jax.experimental.pallas import tpu as pltpu
from jax.sharding import PartitionSpec as P

D = 1024
HEADS = 16
HDIM = 64
FF = 4096
VARS = 48
PATCH = 2
PATCHES = 512
PIECES = PATCH * PATCH
ROWS_TABLE = VARS * (PIECES + 1)
HALF = D // 2
QUARTER = D // 4
TABLE_PAD = 256
FF_TILE = 512
FF_STEPS = FF // FF_TILE
PAIRS = HEADS // 2
LANES = 2 * HDIM
CHUNK = 64
TOKENS_BACK = 2

PRECISE = lax.Precision.HIGHEST
EPSILON = 1e-05
MOMENTUM = 0.1
BF = jnp.bfloat16
F32 = jnp.float32
VMEM_LIMIT = 56 * 1024 * 1024


def dot(left, right, left_dim, right_dim):
    return lax.dot_general(
        left, right, (((left_dim,), (right_dim,)), ((), ())), preferred_element_type=F32
    )


VMEM = pl.BlockSpec(memory_space=pltpu.VMEM)
SMEM = pl.BlockSpec(memory_space=pltpu.SMEM)
ANYWHERE = pl.BlockSpec(memory_space=pl.ANY)


def shape(dims, kind):
    return jax.ShapeDtypeStruct(dims, kind)


def params(grid=0):
    semantics = ("arbitrary",) * grid if grid else None
    return pltpu.CompilerParams(vmem_limit_bytes=VMEM_LIMIT, dimension_semantics=semantics)


def cost():
    return pl.CostEstimate(flops=1000, bytes_accessed=1000, transcendentals=0)


def section_copies(place_ref, section, own, brought, targets, sems):
    core, side = place_ref[1], place_ref[2]

    def rows(core, side):
        return pl.ds(pl.multiple_of((2 * core + side) * QUARTER, QUARTER), QUARTER)

    @pl.when(place_ref[0] == section)
    def _():
        for n, target in enumerate(targets):
            for quarter in range(4):
                part = pl.ds(quarter * QUARTER, QUARTER)
                pltpu.make_async_copy(
                    own[n].at[part], target.at[part], sems.at[n, quarter]
                ).start()

    @pl.when(place_ref[0] != section)
    def _():
        for n, target in enumerate(targets):
            for other in range(2):
                for turn in range(2):
                    place = rows(core + other - 2 * core * other, side + turn - 2 * side * turn)
                    pltpu.make_async_copy(
                        brought[n][other].at[turn], target.at[place], sems.at[n, 2 * other + turn]
                    ).start()

    def wait(n):
        for quarter in range(4):
            part = pl.ds(quarter * QUARTER, QUARTER)
            pltpu.make_async_copy(
                brought[n][0].at[0], targets[n].at[part], sems.at[n, quarter]
            ).wait()

    return wait


def normalized(values):
    center = values - jnp.mean(values, axis=-1, keepdims=True)
    spread = jnp.mean(center * center, axis=-1, keepdims=True)
    inverse = lax.rsqrt(spread + EPSILON)
    return center * inverse, inverse


def norm_back(xhat, inverse, gain, grad):
    scaled = grad * gain
    first = jnp.mean(scaled, axis=-1, keepdims=True)
    second = jnp.mean(scaled * xhat, axis=-1, keepdims=True)
    return (scaled - first - xhat * second) * inverse


def row_chunks(body):
    def step(i, carry):
        body(pl.ds(pl.multiple_of(i * CHUNK, CHUNK), CHUNK))
        return carry

    lax.fori_loop(0, PATCHES // CHUNK, step, 0)


def column_tiles(width, body):
    def step(i, carry):
        body(pl.ds(pl.multiple_of(i * width, width), width))
        return carry

    lax.fori_loop(0, D // width, step, 0)


def head_rows(width):
    row = lax.broadcasted_iota(jnp.int32, (HEADS, width), 0)
    column = lax.broadcasted_iota(jnp.int32, (HEADS, width), 1)
    start = row * HDIM
    return (column >= start) & (column < start + HDIM)


def tables_kernel(query_ref, table_ref, weight_ref, low_ref, keys_ref, value_ref):
    given = jnp.broadcast_to(query_ref[...], (HEADS, D)).astype(BF)
    query = dot(given, weight_ref[0], 1, 0).astype(BF).astype(F32)
    low_ref[...] = query
    spread = jnp.where(head_rows(D), query, 0.0).astype(BF)
    key_query = (dot(spread, weight_ref[1], 1, 1) * HDIM ** (-0.5)).astype(BF)
    keys_ref[...] = dot(table_ref[...], key_query, 1, 1)
    values = dot(table_ref[...], weight_ref[2], 1, 0)
    value_ref[...] = jnp.concatenate([values, key_query.astype(F32)], axis=0).T


def tables(query, table, weights):
    return pl.pallas_call(
        tables_kernel,
        out_shape=(
            shape((HEADS, D), F32),
            shape((ROWS_TABLE, HEADS), F32),
            shape((D, TABLE_PAD), F32),
        ),
        in_specs=[VMEM] * 3,
        out_specs=(VMEM,) * 3,
        compiler_params=params(),
        cost_estimate=cost(),
        name="tables",
    )(query, table, weights)


COLS = 128
STRIPES = 16


def column_order():
    row = lax.broadcasted_iota(jnp.int32, (COLS, COLS), 0)
    column = lax.broadcasted_iota(jnp.int32, (COLS, COLS), 1)
    place = jnp.where(column < COLS // 2, 2 * column, 2 * column - COLS + 1)
    return (row == place).astype(F32)


def exact(left, right, right_dim):
    return lax.dot_general(
        left,
        right,
        (((1,), (right_dim,)), ((), ())),
        precision=PRECISE,
        preferred_element_type=F32,
    )


def head_keys(keys_ref, h):
    keys = keys_ref[...]
    lane = lax.broadcasted_iota(jnp.int32, keys.shape, 1)
    return jnp.sum(jnp.where(lane == h, keys, 0.0), axis=1, keepdims=True)


def mixed_rows(shares, pixels_ref):
    return jnp.concatenate(
        [(shares * pixels_ref[k]).astype(BF) for k in range(PIECES)]
        + [shares.astype(BF), jnp.zeros((TABLE_PAD - ROWS_TABLE, PATCHES), BF)],
        axis=0,
    )


def aggregate_kernel(
    place_ref,
    alive_ref,
    own_field_ref,
    other_field_ref,
    center_ref,
    scale_ref,
    keys_ref,
    tvt_ref,
    position_ref,
    own_ref,
    brought_ref,
    beside_ref,
    tokens_ref,
    heads_ref,
    shares_ref,
    pixels_ref,
    merge_ref,
    grid_ref,
    sems,
):
    wait = section_copies(
        place_ref, 0, [own_ref], [(brought_ref, beside_ref)], [merge_ref], sems
    )
    alive = alive_ref[0]
    order = column_order()
    half = VARS // 2 * STRIPES
    own, other = own_field_ref[...], other_field_ref[...]
    grid_ref[:half] = exact(jnp.where(place_ref[0] == 0, own, other), order, 0)
    grid_ref[half:] = exact(jnp.where(place_ref[0] == 0, other, own), order, 0)
    center, scale = center_ref[...], scale_ref[...]
    low_lane = lax.broadcasted_iota(jnp.int32, (VARS, COLS), 1) < COLS // 2

    def stripe(r):
        values = grid_ref[pl.ds(r, VARS, stride=STRIPES), :]
        return ((values - center) * scale).astype(BF).astype(F32)

    for a in range(PATCH):
        for j in range(PATCHES // COLS):
            even, odd = stripe(4 * j + a), stripe(4 * j + 2 + a)
            columns = slice(j * COLS, (j + 1) * COLS)
            pixels_ref[2 * a, :, columns] = jnp.where(
                low_lane, even, pltpu.roll(odd, COLS // 2, 1)
            )
            pixels_ref[2 * a + 1, :, columns] = jnp.where(
                low_lane, pltpu.roll(even, COLS // 2, 1), odd
            )

    def head(h, carry):
        keys = head_keys(keys_ref, h)
        scores = keys[PIECES * VARS :]
        for k in range(PIECES):
            scores = scores + keys[k * VARS : (k + 1) * VARS] * pixels_ref[k]
        top = jnp.max(scores, axis=0, keepdims=True)
        powers = jnp.exp(scores - top)
        shares = powers / jnp.sum(powers, axis=0, keepdims=True)
        shares_ref[h] = shares
        rows = pl.ds(pl.multiple_of(h * HDIM, HDIM), HDIM)
        heads_ref[rows, :] = dot(tvt_ref[rows, :], mixed_rows(shares, pixels_ref), 1, 0).astype(
            BF
        )
        return carry

    lax.fori_loop(0, HEADS, head, 0)
    wait(0)
    heads = heads_ref[...]

    def tile(columns):
        merged = dot(heads, merge_ref[:, columns], 0, 0)
        tokens_ref[:, columns] = (alive * (merged + position_ref[:, columns].astype(F32))).astype(
            BF
        )

    column_tiles(256, tile)


def aggregate(place, alive, own_field, other_field, center, scale, keys, tvt, position, merge):
    return pl.pallas_call(
        aggregate_kernel,
        out_shape=(
            shape((PATCHES, D), BF),
            shape((D, PATCHES), BF),
            shape((HEADS, VARS, PATCHES), F32),
            shape((PIECES, VARS, PATCHES), F32),
        ),
        in_specs=[SMEM, SMEM] + [VMEM] * 7 + [ANYWHERE] * 3,
        out_specs=(VMEM,) * 4,
        scratch_shapes=[
            pltpu.VMEM((D, D), BF),
            pltpu.VMEM((VARS * STRIPES, COLS), F32),
            pltpu.SemaphoreType.DMA((1, 4)),
        ],
        compiler_params=params(),
        cost_estimate=cost(),
        name="aggregate",
    )(place, alive, own_field, other_field, center, scale, keys, tvt, position, *merge)


def attend_kernel(place_ref, tokens_ref, gain_ref, bias_ref, attend_ref, *refs):
    brought = [(refs[2 * n], refs[2 * n + 1]) for n in range(3)]
    pack_ref, proj_ref, lse_ref, weight_ref, first_ref, sems = refs[6:]
    wait = section_copies(
        place_ref,
        1,
        [attend_ref.at[j] for j in range(3)],
        brought,
        [weight_ref.at[j] for j in range(3)],
        sems,
    )

    def first_norm(rows):
        xhat, _ = normalized(tokens_ref[rows, :].astype(F32))
        first_ref[rows, :] = (xhat * gain_ref[0:1, :] + bias_ref[0:1, :]).astype(BF)

    row_chunks(first_norm)
    pack_ref[:D, :] = first_ref[...].T
    for j in range(3):
        wait(j)
        column_tiles(
            256,
            lambda columns: proj_ref.__setitem__(
                (j, slice(None), columns),
                dot(first_ref[...], weight_ref[j, :, columns], 1, 0).astype(BF),
            ),
        )

    lane = lax.broadcasted_iota(jnp.int32, (PATCHES, LANES), 1)

    def pair(i, carry):
        columns = pl.ds(pl.multiple_of(i * LANES, LANES), LANES)
        queries = proj_ref[0, :, columns]
        keys = proj_ref[1, :, columns]
        values = proj_ref[2, :, columns].T
        for side in range(2):
            inside = (lane < HDIM) if side == 0 else (lane >= HDIM)
            key = jnp.where(inside, keys * HDIM ** (-0.5), jnp.zeros_like(keys)).astype(BF)
            scores = dot(key, queries, 1, 1)
            top = jnp.max(scores, axis=0, keepdims=True)
            powers = jnp.exp(scores - top)
            whole = jnp.sum(powers, axis=0, keepdims=True)
            probs = (powers * (1.0 / whole)).astype(BF)
            lse_ref[i, side : side + 1, :] = top + jnp.log(whole)
            value = values[side * HDIM : (side + 1) * HDIM]
            rows = pl.ds(pl.multiple_of(D + i * LANES + side * HDIM, HDIM), HDIM)
            pack_ref[rows, :] = dot(value, probs, 1, 0).astype(BF)
        return carry

    lax.fori_loop(0, PAIRS, pair, 0)


def attend(place, tokens, gain, bias, own_attend, brought):
    return pl.pallas_call(
        attend_kernel,
        out_shape=(
            shape((2 * D, PATCHES), BF),
            shape((3, PATCHES, D), BF),
            shape((PAIRS, 2, PATCHES), F32),
        ),
        in_specs=[SMEM] + [VMEM] * 3 + [ANYWHERE] * 7,
        out_specs=(VMEM,) * 3,
        scratch_shapes=[
            pltpu.VMEM((3, D, D), BF),
            pltpu.VMEM((PATCHES, D), BF),
            pltpu.SemaphoreType.DMA((3, 4)),
        ],
        compiler_params=params(),
        cost_estimate=cost(),
        name="attend",
    )(place, tokens, gain, bias, own_attend, *brought)


def merge_kernel(
    place_ref,
    tokens_ref,
    pack_ref,
    gain_ref,
    bias_ref,
    own_ref,
    brought_ref,
    beside_ref,
    middle_ref,
    second_ref,
    merge_ref,
    sems,
):
    wait = section_copies(
        place_ref, 1, [own_ref], [(brought_ref, beside_ref)], [merge_ref], sems
    )
    wait(0)
    context = pack_ref[...]
    column_tiles(
        256,
        lambda columns: middle_ref.__setitem__(
            (slice(None), columns),
            tokens_ref[:, columns].astype(F32) + dot(context, merge_ref[:, columns], 0, 0),
        ),
    )

    def second_norm(rows):
        xhat, _ = normalized(middle_ref[rows, :])
        second_ref[rows, :] = (xhat * gain_ref[1:2, :] + bias_ref[1:2, :]).astype(BF)

    row_chunks(second_norm)


def merge(place, tokens, pack, gain, bias, weights):
    return pl.pallas_call(
        merge_kernel,
        grid=(1,),
        out_shape=(shape((PATCHES, D), F32), shape((PATCHES, D), BF)),
        in_specs=[SMEM, VMEM, pl.BlockSpec((D, PATCHES), lambda i: (1, 0)), VMEM, VMEM]
        + [ANYWHERE] * 3,
        out_specs=(VMEM,) * 2,
        scratch_shapes=[pltpu.VMEM((D, D), BF), pltpu.SemaphoreType.DMA((1, 4))],
        compiler_params=params(1),
        cost_estimate=cost(),
        name="merge",
    )(place, tokens, pack, gain, bias, *weights)


def gelu_parts(hidden):
    inverse = 1.0 / (1.0 + 0.23164190 * jnp.abs(hidden))
    decay = jnp.exp2(hidden * hidden * (-0.72134752))
    series = 0.5 * 1.061405429
    for factor in (-1.453152027, 1.421413741, -0.284496736, 0.254829592):
        series = series * inverse + 0.5 * factor
    tail = series * inverse * decay
    cdf = jnp.where(hidden >= 0.0, 1.0 - tail, tail)
    return cdf, decay * 0.3989422804014327


FF_PART = 256
UNITS = FF + HALF


def copy(source, target, sem):
    return pltpu.make_async_copy(source, target, sem)


def aligned(index, size):
    return pl.ds(pl.multiple_of(index * size, size), size)


def start_either(choice, source, if_true, if_false, sem):
    @pl.when(choice)
    def _():
        copy(source, if_true, sem).start()

    @pl.when(jnp.logical_not(choice))
    def _():
        copy(source, if_false, sem).start()


def expand_kernel(
    place_ref,
    second_ref,
    out_ref,
    bias_ref,
    up_any,
    down_any,
    after_any,
    units_any,
    sum_ref,
    up_ref,
    down_ref,
    tile_ref,
    in_sems,
    out_sems,
):
    def fetch(j):
        part = aligned(j, FF_TILE)
        return (
            copy(up_any.at[:, part], up_ref.at[:, part], in_sems.at[j, 0]),
            copy(down_any.at[part], down_ref.at[part], in_sems.at[j, 1]),
        )

    def put(j, slot):
        return copy(
            tile_ref.at[slot], units_any.at[:, :, aligned(j, FF_TILE)], out_sems.at[slot]
        )

    for j in range(FF_STEPS):
        for one in fetch(j):
            one.start()

    def step(j, carry):
        slot = lax.rem(j, 2)

        @pl.when(j >= 2)
        def _():
            put(j - 2, slot).wait()

        for one in fetch(j):
            one.wait()
        for part in range(FF_TILE // FF_PART):
            inner = slice(part * FF_PART, (part + 1) * FF_PART)
            start = pl.multiple_of(j * FF_TILE + part * FF_PART, FF_PART)
            columns = pl.ds(start, FF_PART)
            hidden = dot(second_ref[...], up_ref[:, columns], 1, 0) + bias_ref[:, columns]
            grad = dot(out_ref[...], down_ref[columns, :], 1, 1)
            cdf, density = gelu_parts(hidden)
            tile_ref[slot, 0, :, inner] = (hidden * cdf).astype(BF)
            low = (grad * (cdf + hidden * density)).astype(BF)
            tile_ref[slot, 1, :, inner] = low
            sum_ref[:, columns] = jnp.sum(low.astype(F32), axis=0, keepdims=True)
        put(j, slot).start()
        return carry

    lax.fori_loop(0, FF_STEPS, step, 0)
    others = aligned(1 - place_ref[1], HALF)
    put(FF_STEPS - 2, 0).wait()
    tile_ref[0, 0] = out_ref[:, others]
    tile_ref[0, 1] = second_ref[:, others]
    put(FF_STEPS, 0).start()
    put(FF_STEPS - 1, 1).wait()
    put(FF_STEPS, 0).wait()


def expand(place, second, out_low, up, bias, down, after):
    return pl.pallas_call(
        expand_kernel,
        out_shape=(shape((2, PATCHES, UNITS), BF), shape((1, FF), F32)),
        in_specs=[SMEM, VMEM, VMEM, VMEM, ANYWHERE, ANYWHERE, ANYWHERE],
        out_specs=(ANYWHERE, VMEM),
        scratch_shapes=[
            pltpu.VMEM((D, FF), BF),
            pltpu.VMEM((FF, D), BF),
            pltpu.VMEM((2, 2, PATCHES, FF_TILE), BF),
            pltpu.SemaphoreType.DMA((FF_STEPS, 2)),
            pltpu.SemaphoreType.DMA((2,)),
        ],
        compiler_params=params(),
        cost_estimate=cost(),
        name="expand",
    )(place, second, out_low, bias.reshape(1, FF), up, down, after)


DEPTHS = 4
DEPTH = FF // DEPTHS


def contract_kernel(
    place_ref,
    scalars_ref,
    gain_ref,
    bias_ref,
    units_any,
    up_any,
    down_any,
    middle_any,
    cotangent_any,
    result_ref,
    grad_ref,
    branch_ref,
    gain_grad_ref,
    bias_grad_ref,
    out_grad_ref,
    units_ref,
    up_ref,
    down_ref,
    middle_ref,
    cotangent_ref,
    total_ref,
    second_ref,
    sems,
):
    def fetch(n):
        which, c = divmod(n, DEPTHS)
        part = slice(c * DEPTH, (c + 1) * DEPTH)
        if which == 0:
            weight = copy(down_any.at[part], down_ref.at[part], sems.at[n, 1])
        else:
            weight = copy(up_any.at[:, part], up_ref.at[:, part], sems.at[n, 1])
        return (
            copy(units_any.at[which, :, part], units_ref.at[which, :, part], sems.at[n, 0]),
            weight,
        )

    rest = (
        copy(middle_any, middle_ref, sems.at[2 * DEPTHS, 0]),
        copy(cotangent_any.at[place_ref[0]], cotangent_ref, sems.at[2 * DEPTHS, 1]),
    )
    for n in range(2 * DEPTHS):
        for one in fetch(n):
            one.start()
    for one in rest:
        one.start()
    for n in range(2 * DEPTHS):
        which, c = divmod(n, DEPTHS)
        part = slice(c * DEPTH, (c + 1) * DEPTH)
        for one in fetch(n):
            one.wait()
        ref = second_ref if which else total_ref
        if which:
            product = dot(units_ref[1, :, part], up_ref[:, part], 1, 1)
        else:
            product = dot(units_ref[0, :, part], down_ref[part, :], 1, 0)
        if c:
            ref[...] += product
        else:
            ref[...] = product
    for one in rest:
        one.wait()
    alive, hat = scalars_ref[0], scalars_ref[1]
    gain_grad_ref[...] = jnp.zeros_like(gain_grad_ref)
    bias_grad_ref[...] = jnp.zeros_like(bias_grad_ref)
    out_grad_ref[...] = jnp.zeros_like(out_grad_ref)

    def chunk(rows):
        middle = middle_ref[rows, :]
        result_ref[rows, :] = (alive * (middle + total_ref[rows, :] + bias_ref[...])).astype(BF)
        xhat, inverse = normalized(middle)
        grad = second_ref[rows, :]
        gain_grad_ref[...] += jnp.sum(grad * xhat, axis=0, keepdims=True)
        bias_grad_ref[...] += jnp.sum(grad, axis=0, keepdims=True)
        out = cotangent_ref[rows, :].astype(F32) * hat
        out_grad_ref[...] += jnp.sum(out, axis=0, keepdims=True)
        whole = out + norm_back(xhat, inverse, gain_ref[...], grad)
        grad_ref[rows, :] = whole
        branch_ref[rows, :] = whole.astype(BF)

    row_chunks(chunk)


def contract(place, scalars, units, up, down, middle, cotangent, gain, bias):
    return pl.pallas_call(
        contract_kernel,
        out_shape=(
            shape((PATCHES, D), BF),
            shape((PATCHES, D), F32),
            shape((PATCHES, D), BF),
            shape((1, D), F32),
            shape((1, D), F32),
            shape((1, D), F32),
        ),
        in_specs=[SMEM, SMEM, VMEM, VMEM] + [ANYWHERE] * 5,
        out_specs=(VMEM,) * 6,
        scratch_shapes=[
            pltpu.VMEM((2, PATCHES, FF), BF),
            pltpu.VMEM((D, FF), BF),
            pltpu.VMEM((FF, D), BF),
            pltpu.VMEM((PATCHES, D), F32),
            pltpu.VMEM((PATCHES, D), BF),
            pltpu.VMEM((PATCHES, D), F32),
            pltpu.VMEM((PATCHES, D), F32),
            pltpu.SemaphoreType.DMA((2 * DEPTHS + 1, 2)),
        ],
        compiler_params=params(),
        cost_estimate=cost(),
        name="contract",
    )(place, scalars, gain, bias, units, up, down, middle, cotangent)


def attend_back_kernel(
    place_ref,
    grad_ref,
    branch_ref,
    proj_ref,
    lse_ref,
    tokens_ref,
    gain_ref,
    attend_ref,
    merge_ref,
    *refs,
):
    brought = [(refs[2 * n], refs[2 * n + 1]) for n in range(4)]
    outs = refs[8 + TOKENS_BACK :]
    keep_ref, send_ref, token_grad_ref, gain_grad_ref, bias_grad_ref = outs[:5]
    weight_ref, context_ref, first_ref, proj_grad_ref, sems = outs[5:]
    wait = section_copies(
        place_ref,
        1,
        [merge_ref] + [attend_ref.at[j] for j in range(3)],
        brought[3:] + brought[:3],
        [weight_ref.at[j] for j in range(4)],
        sems,
    )
    wait(0)
    branch = branch_ref[...]

    def context_tile(columns):
        context_ref[:, columns] = dot(branch, weight_ref[0, columns, :], 1, 1).astype(BF)

    column_tiles(256, context_tile)
    lane = lax.broadcasted_iota(jnp.int32, (PATCHES, LANES), 1)

    def pair(i, carry):
        columns = pl.ds(pl.multiple_of(i * LANES, LANES), LANES)
        queries = proj_ref[0, :, columns]
        keys = proj_ref[1, :, columns]
        values = proj_ref[2, :, columns]
        grads = context_ref[:, columns]
        keys_turned = keys.T
        blank = jnp.zeros_like(keys)
        query_grads, key_grads, value_grads = [], [], []
        for side in range(2):
            inside = (lane < HDIM) if side == 0 else (lane >= HDIM)
            key = jnp.where(inside, keys * HDIM ** (-0.5), blank).astype(BF)
            value = jnp.where(inside, values, blank)
            probs = jnp.exp(dot(key, queries, 1, 1) - lse_ref[i, side : side + 1, :])
            share_grad = dot(value, grads, 1, 1)
            weighted = probs * share_grad
            inner = jnp.sum(weighted, axis=0, keepdims=True)
            score_low = (weighted - probs * inner).astype(BF)
            value_grads.append(dot(probs.astype(BF), grads, 1, 0))
            key_grads.append(dot(score_low, queries, 1, 0))
            query_grads.append(
                dot(keys_turned[side * HDIM : (side + 1) * HDIM], score_low, 1, 0)
            )
        low = lane < HDIM
        query_grad = jnp.concatenate(query_grads, axis=0) * HDIM ** (-0.5)
        proj_grad_ref[0, :, columns] = query_grad.T.astype(BF)
        proj_grad_ref[1, :, columns] = (
            jnp.where(low, key_grads[0], key_grads[1]) * HDIM ** (-0.5)
        ).astype(BF)
        proj_grad_ref[2, :, columns] = jnp.where(low, value_grads[0], value_grads[1]).astype(BF)
        return carry

    lax.fori_loop(0, PAIRS, pair, 0)
    core = place_ref[1]
    owns = pl.ds(pl.multiple_of(core * HALF, HALF), HALF)
    others = pl.ds(pl.multiple_of((1 - core) * HALF, HALF), HALF)
    for j in range(3):
        keep_ref[j] = proj_grad_ref[j, :, owns]
        send_ref[j] = proj_grad_ref[j, :, others]
    keep_ref[3] = branch_ref[:, owns]
    send_ref[3] = branch_ref[:, others]
    for j in range(3):
        wait(j + 1)

    def first_tile(columns):
        total = dot(proj_grad_ref[0], weight_ref[1, columns, :], 1, 1)
        for j in range(1, 3):
            total = total + dot(proj_grad_ref[j], weight_ref[j + 1, columns, :], 1, 1)
        first_ref[:, columns] = total

    column_tiles(256, first_tile)
    gain_grad_ref[...] = jnp.zeros_like(gain_grad_ref)
    bias_grad_ref[...] = jnp.zeros_like(bias_grad_ref)

    def chunk(rows):
        xhat, inverse = normalized(tokens_ref[rows, :].astype(F32))
        grad = first_ref[rows, :]
        gain_grad_ref[...] += jnp.sum(grad * xhat, axis=0, keepdims=True)
        bias_grad_ref[...] += jnp.sum(grad, axis=0, keepdims=True)
        token_grad_ref[rows, :] = (
            grad_ref[rows, :] + norm_back(xhat, inverse, gain_ref[0:1, :], grad)
        ).astype(BF)

    row_chunks(chunk)


def attend_back(
    place, grad, branch, proj, lse, tokens, gain, own_attend, own_merge, brought, after
):
    return pl.pallas_call(
        attend_back_kernel,
        out_shape=(
            shape((4, PATCHES, HALF), BF),
            shape((4, PATCHES, HALF), BF),
            shape((PATCHES, D), BF),
            shape((1, D), F32),
            shape((1, D), F32),
        ),
        in_specs=[SMEM] + [VMEM] * 6 + [ANYWHERE] * (10 + TOKENS_BACK),
        out_specs=(VMEM,) * 5,
        scratch_shapes=[
            pltpu.VMEM((4, D, D), BF),
            pltpu.VMEM((PATCHES, D), BF),
            pltpu.VMEM((PATCHES, D), F32),
            pltpu.VMEM((3, PATCHES, D), BF),
            pltpu.SemaphoreType.DMA((4, 4)),
        ],
        compiler_params=params(),
        cost_estimate=cost(),
        name="attend_back",
    )(place, grad, branch, proj, lse, tokens, gain, own_attend, own_merge, *brought, *after)


MIX_AT = PATCHES
SMALL_AT = PATCHES + TABLE_PAD
KEYS_AT = SMALL_AT + 16
TAIL = KEYS_AT + ROWS_TABLE


def aggregate_back_kernel(
    place_ref,
    alive_ref,
    token_grad_ref,
    pixels_ref,
    keys_ref,
    tvt_ref,
    shares_ref,
    gain_first_ref,
    gain_second_ref,
    bias_first_ref,
    bias_second_ref,
    output_ref,
    hidden_ref,
    own_ref,
    brought_ref,
    beside_ref,
    keep_ref,
    send_ref,
    field_ref,
    key_grad_ref,
    head_ref,
    merge_ref,
    mix_ref,
    pixel_grad_ref,
    grid_ref,
    sems,
):
    wait = section_copies(
        place_ref, 0, [own_ref], [(brought_ref, beside_ref)], [merge_ref], sems
    )
    core = place_ref[1]
    owns = pl.ds(pl.multiple_of(core * HALF, HALF), HALF)
    others = pl.ds(pl.multiple_of((1 - core) * HALF, HALF), HALF)
    alive = alive_ref[0]
    pre = (token_grad_ref[...].astype(F32) * alive).astype(BF)
    keep_ref[:PATCHES, :] = (token_grad_ref[:, owns].astype(F32) * alive).astype(BF)
    send_ref[:PATCHES, :] = (token_grad_ref[:, others].astype(F32) * alive).astype(BF)
    wait(0)

    def head_tile(rows):
        head_ref[rows, :] = dot(merge_ref[rows, :], pre, 1, 1).astype(BF)

    column_tiles(256, head_tile)
    pixel_grad_ref[...] = jnp.zeros_like(pixel_grad_ref)
    key_grad_ref[...] = jnp.zeros_like(key_grad_ref)
    lane = lax.broadcasted_iota(jnp.int32, (VARS, HEADS), 1)

    def head(h, carry):
        rows = pl.ds(pl.multiple_of(h * HDIM, HDIM), HDIM)
        keys = head_keys(keys_ref, h)
        grads = head_ref[rows, :]
        shares = shares_ref[h]
        mix_ref[rows, :] = dot(grads, mixed_rows(shares, pixels_ref), 1, 1)
        row_grads = dot(tvt_ref[rows, :], grads, 0, 0)
        share_grads = row_grads[PIECES * VARS : ROWS_TABLE]
        for k in range(PIECES):
            share_grads = share_grads + row_grads[k * VARS : (k + 1) * VARS] * pixels_ref[k]
        inner = jnp.sum(shares * share_grads, axis=0, keepdims=True)
        scores = shares * (share_grads - inner)
        for k in range(PIECES + 1):
            piece = slice(k * VARS, (k + 1) * VARS)
            if k < PIECES:
                pixel_grad_ref[k] += shares * row_grads[piece] + scores * keys[piece]
                total = jnp.sum(scores * pixels_ref[k], axis=1, keepdims=True)
            else:
                total = jnp.sum(scores, axis=1, keepdims=True)
            key_grad_ref[piece, :] += jnp.where(lane == h, total, 0.0)
        return carry

    lax.fori_loop(0, HEADS, head, 0)
    for ref, start in ((keep_ref, core * HALF), (send_ref, (1 - core) * HALF)):
        for part in range(2):
            rows = pl.ds(pl.multiple_of(start + part * TABLE_PAD, TABLE_PAD), TABLE_PAD)
            ref[MIX_AT:SMALL_AT, part * TABLE_PAD : (part + 1) * TABLE_PAD] = mix_ref[
                rows, :
            ].astype(BF)
        columns = pl.ds(pl.multiple_of(start, HALF), HALF)
        small = [
            one[:, columns]
            for one in (
                gain_first_ref,
                gain_second_ref,
                bias_first_ref,
                bias_second_ref,
                output_ref,
            )
        ]
        for part in range(FF // D):
            small.append(hidden_ref[:, pl.ds(pl.multiple_of(part * D + start, HALF), HALF)])
        small.append(jnp.zeros((16 - len(small), HALF), F32))
        ref[SMALL_AT:KEYS_AT, :] = jnp.concatenate(small, axis=0).astype(BF)
        ref[KEYS_AT:, :] = jnp.concatenate(
            [key_grad_ref[...], jnp.zeros((ROWS_TABLE, HALF - HEADS), F32)], axis=1
        ).astype(BF)
    low_lane = lax.broadcasted_iota(jnp.int32, (VARS, COLS), 1) < COLS // 2
    for a in range(PATCH):
        for j in range(PATCHES // COLS):
            columns = slice(j * COLS, (j + 1) * COLS)
            low, high = pixel_grad_ref[2 * a, :, columns], pixel_grad_ref[2 * a + 1, :, columns]
            even = jnp.where(low_lane, low, pltpu.roll(high, COLS // 2, 1))
            odd = jnp.where(low_lane, pltpu.roll(low, COLS // 2, 1), high)
            grid_ref[pl.ds(4 * j + a, VARS, stride=STRIPES), :] = even
            grid_ref[pl.ds(4 * j + 2 + a, VARS, stride=STRIPES), :] = odd
    field_ref[...] = exact(grid_ref[...], column_order(), 1)


def aggregate_back(place, alive, token_grad, pixels, keys, tvt, shares, small, merge):
    return pl.pallas_call(
        aggregate_back_kernel,
        out_shape=(
            shape((TAIL, HALF), BF),
            shape((TAIL, HALF), BF),
            shape((VARS * STRIPES, COLS), F32),
        ),
        in_specs=[SMEM, SMEM] + [VMEM] * 11 + [ANYWHERE] * 3,
        out_specs=(VMEM,) * 3,
        scratch_shapes=[
            pltpu.VMEM((ROWS_TABLE, HEADS), F32),
            pltpu.VMEM((D, PATCHES), BF),
            pltpu.VMEM((D, D), BF),
            pltpu.VMEM((D, TABLE_PAD), F32),
            pltpu.VMEM((PIECES, VARS, PATCHES), F32),
            pltpu.VMEM((VARS * STRIPES, COLS), F32),
            pltpu.SemaphoreType.DMA((1, 4)),
        ],
        compiler_params=params(),
        cost_estimate=cost(),
        name="aggregate_back",
    )(place, alive, token_grad, pixels, keys, tvt, shares, *small, *merge)


BLOCKS = 16
BLOCK = FF // BLOCKS
SPANS = BLOCKS // 2
SPAN = 4 * BLOCK


def wide_kernel(which, by_pipe, place_ref, left_any, own_any, beside_any, *refs):
    send_any, keep_any, left_ref, turned_ref, right_ref, product_ref, sems, out_sems = refs[-8:]
    place, core = place_ref[0], place_ref[1]
    side, z_low = jnp.bitwise_and(place, 1), jnp.bitwise_and(lax.shift_right_logical(place, 1), 1)

    def fetch(i):
        columns = aligned(jnp.bitwise_xor(3 - i, lax.shift_right_logical(place, 2)), SPAN)
        return [
            copy(
                source.at[which, :, columns],
                right_ref.at[i, pl.ds(n * PATCHES, PATCHES)],
                sems.at[i, n],
            )
            for n, source in enumerate((own_any, beside_any))
        ]

    lefts = (
        copy(left_any.at[:, aligned(core, HALF)], left_ref.at[0], sems.at[4, 0]),
        copy(beside_any.at[which, :, pl.ds(FF, HALF)], left_ref.at[1], sems.at[4, 1]),
    )
    for one in lefts:
        one.start()
    for i in range(4):
        for one in fetch(i):
            one.start()
    for n, one in enumerate(lefts):
        one.wait()
        turned_ref[:, n * PATCHES : (n + 1) * PATCHES] = left_ref[n].T

    def put(i, block):
        source = product_ref.at[i % 2, :, pl.ds(block * BLOCK, BLOCK)]
        return source, out_sems.at[i % 2, block]

    def wait(i):
        for block in range(4):
            source, sem = put(i, block)
            copy(source, send_any.at[0, 0, 0], sem).wait()

    for i in range(4):
        for one in fetch(i):
            one.wait()
        if i >= 2:
            wait(i - 2)
        product_ref[i % 2] = dot(turned_ref[...], right_ref[i], 1, 0).astype(BF)
        pipe, z_high = divmod(3 - i, 2)
        for block in range(4):
            source, sem = put(i, block)
            to_side = jnp.bitwise_xor(block % 2, side)
            to_z = jnp.bitwise_xor(block // 2, z_low)
            if by_pipe:
                target = send_any if pipe else keep_any
                copy(source, target.at[to_side, z_high, to_z], sem).start()
            else:
                start_either(
                    to_side == 1,
                    source,
                    send_any.at[pipe, z_high, to_z],
                    keep_any.at[pipe, z_high, to_z],
                    sem,
                )
    wait(2)
    wait(3)


def wide_grads(place, left, right, which, by_pipe, after, name):
    return pl.pallas_call(
        functools.partial(wide_kernel, which, by_pipe),
        in_specs=[SMEM] + [ANYWHERE] * (3 + len(after)),
        out_specs=(ANYWHERE, ANYWHERE),
        out_shape=(shape((2, 2, 2, HALF, BLOCK), BF), shape((2, 2, 2, HALF, BLOCK), BF)),
        scratch_shapes=[
            pltpu.VMEM((2, PATCHES, HALF), BF),
            pltpu.VMEM((HALF, 2 * PATCHES), BF),
            pltpu.VMEM((4, 2 * PATCHES, SPAN), BF),
            pltpu.VMEM((2, HALF, SPAN), BF),
            pltpu.SemaphoreType.DMA((5, 2)),
            pltpu.SemaphoreType.DMA((2, 4)),
        ],
        compiler_params=params(),
        cost_estimate=cost(),
        name=name,
    )(place, left, *right, *after)


ROWS = D // SPANS
PARTS = 2 * ROWS


def square_kernel(
    place_ref,
    tail_own,
    tail_beside,
    heads_own,
    heads_beside,
    pack_own,
    pack_beside,
    right_own,
    right_beside,
    *refs,
):
    send_any, keep_any, cross_send_any, cross_keep_any = refs[-9:-5]
    left_ref, right_ref, product_ref, sems, out_sems = refs[-5:]
    pipe, place = place_ref[0], place_ref[1]
    side, z = jnp.bitwise_and(place, 1), lax.shift_right_logical(place, 1)
    lefts = [
        (pack_own.at[pl.ds(0, D)], pack_beside.at[pl.ds(0, D)]),
        (pack_own.at[pl.ds(D, D)], pack_beside.at[pl.ds(D, D)]),
        (heads_own, heads_beside),
    ]
    left_copies = [
        [
            copy(one, left_ref.at[n, :, pl.ds(m * PATCHES, PATCHES)], sems.at[n, m])
            for m, one in enumerate(pair)
        ]
        for n, pair in enumerate(lefts)
    ]
    right_copies = [
        [
            copy(one.at[n], right_ref.at[n, pl.ds(m * PATCHES, PATCHES)], sems.at[3 + n, m])
            for m, one in enumerate((right_own, right_beside))
        ]
        for n in range(4)
    ]
    for n in (0, 3, 1, 2):
        for one in (left_copies[n] if n < 3 else []) + right_copies[n]:
            one.start()
    right_ref[4, :PATCHES] = tail_own[:PATCHES]
    right_ref[4, PATCHES:] = tail_beside[:PATCHES]

    def put(slot, block):
        return product_ref.at[slot, pl.ds(block * ROWS, ROWS)], out_sems.at[slot, block]

    def wait(slot):
        for block in range(SPANS):
            source, sem = put(slot, block)
            copy(source, send_any.at[0, pl.ds(0, ROWS)], sem).wait()

    def share(slot, part):
        rows = pl.ds(part * ROWS, ROWS)
        for block in range(SPANS):
            source, sem = put(slot, block)
            to_z = jnp.bitwise_xor(block // 2, z)
            start_either(
                side != block % 2, source, send_any.at[to_z, rows], keep_any.at[to_z, rows], sem
            )

    def cross(slot, part, goal):
        rows = pl.ds(part * ROWS, ROWS)
        for block in range(SPANS):
            source, sem = put(slot, block)
            to_side = jnp.bitwise_xor(block % 2, side)
            to_z = jnp.bitwise_xor(block // 2, z)
            start_either(
                pipe != goal,
                source,
                cross_send_any.at[to_side, to_z, rows],
                cross_keep_any.at[to_side, to_z, rows],
                sem,
            )

    product_ref[0] = (tail_own[...].astype(F32) + tail_beside[...].astype(F32)).astype(BF)
    share(0, 1)
    for step, (left, right) in enumerate(((0, 0), (1, 3), (2, 4), (0, 1), (0, 2))):
        slot = (step + 1) % 2
        if step in (0, 1, 2):
            for one in left_copies[left]:
                one.wait()
        if right < 4:
            for one in right_copies[right]:
                one.wait()
        if step >= 1:
            wait(slot)
        for tile in range(2):
            rows = slice(tile * HALF, (tile + 1) * HALF)
            product_ref[slot, rows] = dot(left_ref[left, rows], right_ref[right], 1, 0).astype(BF)
        if step == 0:
            share(slot, 0)
        elif step == 1:
            cross(slot, 0, 1)
        elif step == 2:
            cross(slot, 0, 0)
        else:
            cross(slot, 1, step - 3)
    wait(0)
    wait(1)


def square_grads(place, tail, heads, pack, right, after):
    return pl.pallas_call(
        square_kernel,
        in_specs=[SMEM, VMEM, VMEM] + [ANYWHERE] * (6 + len(after)),
        out_specs=(ANYWHERE,) * 4,
        out_shape=(
            shape((4, PARTS, HALF), BF),
            shape((4, PARTS, HALF), BF),
            shape((2, 4, PARTS, HALF), BF),
            shape((2, 4, PARTS, HALF), BF),
        ),
        scratch_shapes=[
            pltpu.VMEM((3, D, 2 * PATCHES), BF),
            pltpu.VMEM((5, 2 * PATCHES, HALF), BF),
            pltpu.VMEM((2, D, HALF), BF),
            pltpu.SemaphoreType.DMA((7, 2)),
            pltpu.SemaphoreType.DMA((2, SPANS)),
        ],
        compiler_params=params(),
        cost_estimate=cost(),
        name="square_grads",
    )(place, *tail, *heads, *pack, *right, *after)


def finish_kernel(
    chips,
    place_ref,
    tail_ref,
    table_ref,
    weight_ref,
    position_ref,
    mix_ref,
    small_ref,
    keys_ref,
    key_query_ref,
    low_ref,
    query_ref,
    whole_ref,
):
    pipe, core, chip = place_ref[0], place_ref[1], place_ref[2]
    part = TAIL // (2 * chips)
    for c in range(2):
        for n in range(chips):
            for p in range(2):
                start = (2 * n + p) * part
                whole_ref[c, start : start + part, :] = tail_ref[
                    jnp.bitwise_xor(c, core), jnp.bitwise_xor(n, chip), jnp.bitwise_xor(p, pipe)
                ].astype(F32)
    for c in range(2):
        columns = slice(c * HALF, (c + 1) * HALF)
        position_ref[:, columns] = whole_ref[c, :PATCHES, :]
        small_ref[:, columns] = whole_ref[c, SMALL_AT:KEYS_AT, :]
        for n in range(2):
            start = c * HALF + n * TABLE_PAD
            mix_ref[start : start + TABLE_PAD, :] = whole_ref[
                c, MIX_AT:SMALL_AT, n * TABLE_PAD : (n + 1) * TABLE_PAD
            ]
    keys = whole_ref[0, KEYS_AT:, :HEADS]
    keys_ref[...] = keys
    grads = lax.dot_general(
        keys,
        table_ref[...].astype(F32),
        (((0,), (0,)), ((), ())),
        precision=PRECISE,
        preferred_element_type=F32,
    ).astype(BF)
    key_query_ref[...] = grads.astype(F32)
    low = jnp.where(head_rows(D), dot(grads, weight_ref[1], 1, 0), 0.0)
    low = jnp.sum(low, axis=0, keepdims=True) * HDIM ** (-0.5)
    low = jnp.broadcast_to(low, (HEADS, D)).astype(BF)
    low_ref[...] = low.astype(F32)
    query_ref[...] = dot(low, weight_ref[0], 1, 1)


def finish(place, tail, table, weights, chips):
    return pl.pallas_call(
        functools.partial(finish_kernel, chips),
        out_shape=(
            shape((PATCHES, D), F32),
            shape((D, TABLE_PAD), F32),
            shape((16, D), F32),
            shape((ROWS_TABLE, HEADS), F32),
            shape((HEADS, D), F32),
            shape((HEADS, D), F32),
            shape((HEADS, D), F32),
        ),
        in_specs=[SMEM] + [VMEM] * 3,
        out_specs=(VMEM,) * 7,
        scratch_shapes=[pltpu.VMEM((2, TAIL, HALF), F32)],
        compiler_params=params(),
        cost_estimate=cost(),
        name="finish",
    )(place, tail, table, weights)


def partner(block, axis, distance):
    size = lax.axis_size(axis)
    return lax.ppermute(block, axis, [(i, i ^ distance) for i in range(size)])


def swap(block):
    return partner(block, "pipe", 1)


def pick(array, index, axis=0):
    return lax.dynamic_index_in_dim(array, index, axis, keepdims=False)


def tree_sum(terms):
    while len(terms) > 1:
        terms = [terms[2 * i] + terms[2 * i + 1] for i in range(len(terms) // 2)]
    return terms[0]


class Places:
    def __init__(self):
        self.pipe = lax.axis_index("pipe")
        self.dp = lax.axis_index("dp")
        self.size = lax.axis_size("dp")
        self.core = self.dp % 2
        self.chips = self.size // 2
        bits = self.size.bit_length() - 2
        low = bits % 2 if bits % 2 else 2
        self.groups = []
        at = 1
        while bits > 0:
            width = low if at == 1 else 2
            self.groups.append((at, width))
            at += width
            bits -= width

    def relative(self, array, place):
        for bit in range(array.shape[0].bit_length() - 1):
            paired = array.reshape(-1, 2, 2**bit, *array.shape[1:])
            flipped = jnp.where((place // 2**bit) % 2 == 1, paired[:, ::-1], paired)
            array = flipped.reshape(array.shape)
        return array

    def grouped(self, array):
        counts = [2**width for _, width in reversed(self.groups)]
        dims = array.shape[1:]
        array = array.reshape(*counts, *dims)
        order = list(range(len(counts)))[::-1] + list(range(len(counts), array.ndim))
        return array.transpose(order)

    def reduced(self, array, groups):
        for n, (at, width) in enumerate(groups):
            terms = [array[0].astype(F32)]
            for distance in range(1, 2**width):
                terms.append(partner(array[distance], "dp", distance * 2**at).astype(F32))
            array = tree_sum(terms)
            if n < len(groups) - 1:
                array = array.astype(BF)
        return array

    def over_cores(self, array):
        brought = partner(pick(array, 1 - self.core).astype(BF), "dp", 1).astype(F32)
        own = pick(array, self.core)
        return jnp.concatenate(
            [jnp.where(self.core == 0, own, brought), jnp.where(self.core == 0, brought, own)],
            axis=-1,
        )

    def gather(self, block):
        blocks = block[None]
        for at, width in reversed(self.groups):
            parts = [partner(blocks, "dp", m * 2**at) for m in range(1, 2**width)]
            blocks = jnp.stack([blocks] + parts, axis=1).reshape(-1, *block.shape)
        return blocks

    def total(self, block):
        for bit in range(self.size.bit_length() - 1):
            block = block + partner(block, "dp", 2**bit)
        return block


def on_device(
    fields,
    item_weights,
    live_counts,
    running_stats,
    embed_weight,
    variable_embed,
    variable_query,
    attend_weight,
    merge_weight,
    position_embed,
    norm_gain,
    norm_bias,
    up_weight,
    hidden_bias,
    down_weight,
    output_bias,
    cotangent,
):
    at = Places()
    pipe, core = at.pipe, at.core
    first = pipe == 0
    side = (at.dp // 2) % 2
    chip = at.dp // 2
    place = jnp.stack([pipe, core, side]).astype(jnp.int32)
    micro, half_vars, rows, cols = fields.shape
    scale_heads = HDIM ** (-0.5)

    own_attend, own_merge = attend_weight[0], merge_weight[0]

    def quarter(weight):
        return lax.dynamic_slice_in_dim(weight, (2 * core + side) * QUARTER, QUARTER, 0)

    def quarter_of(j):
        start = (jnp.int32(j), (2 * core + side) * QUARTER, jnp.int32(0))
        return lax.dynamic_slice(own_attend, start, (1, QUARTER, D))[0]

    def passed_on(block):
        pair = jnp.stack([block, partner(block, "dp", 2)])
        return pair, partner(pair, "dp", 1)

    def after(value, *others):
        return lax.optimization_barrier((value, others))[0]

    chunk_first = swap(jnp.where(first, quarter(own_merge), quarter_of(0)))

    flat_fields = fields.reshape(micro, half_vars * rows, cols)
    other_fields = swap(pick(flat_fields, 1 - pipe))
    own_fields = pick(flat_fields, pipe)
    slots = jnp.arange(micro, dtype=jnp.int32)
    alive = (slots < live_counts[0]).astype(F32)
    omega = item_weights.astype(F32) * alive
    plain_sums = jnp.sum(fields, axis=(2, 3))
    square_sums = jnp.sum(fields * fields, axis=(2, 3))
    sums = jnp.concatenate(
        [
            jnp.sum(omega[:, None] * plain_sums, axis=0),
            jnp.sum(omega[:, None] * square_sums, axis=0),
            jnp.sum(omega)[None],
            jnp.sum(alive)[None],
        ]
    )
    sums = at.total(sums)
    total, live_total = sums[2 * half_vars], sums[2 * half_vars + 1]
    first_moment = sums[:half_vars] / (total * rows * cols)
    second_moment = sums[half_vars : 2 * half_vars] / (total * rows * cols)
    center_new = (1.0 - MOMENTUM) * running_stats[0] + MOMENTUM * first_moment
    spread_new = (1.0 - MOMENTUM) * running_stats[1] + MOMENTUM * (
        second_moment - first_moment * first_moment
    )
    statistics = jnp.stack([center_new, spread_new])
    other_statistics = swap(statistics)
    all_statistics = jnp.concatenate(
        [
            jnp.where(first, statistics, other_statistics),
            jnp.where(first, other_statistics, statistics),
        ],
        axis=1,
    )
    center = all_statistics[0].reshape(VARS, 1)
    scale = lax.rsqrt(all_statistics[1] + EPSILON).reshape(VARS, 1)
    weight_hat = pick(omega, pipe) * live_total / total
    alive_own = pick(alive, pipe)[None]
    out_low = (pick(cotangent, pipe).astype(F32) * weight_hat).astype(BF)

    table = jnp.concatenate(
        [embed_weight.transpose(1, 0, 2).reshape(VARS * PIECES, D), variable_embed], axis=0
    )
    query, table_keys, table_value = tables(
        variable_query.astype(F32).reshape(1, D), table, own_attend
    )

    def from_first(block):
        return jnp.where(first, block, lax.ppermute(block, "pipe", [(0, 1)]))

    tvt = from_first(table_value.astype(BF))
    keys = from_first(table_keys)

    chunk = chunk_first
    passed = [passed_on(chunk)]
    chunks = [chunk]
    chunk = swap(after(jnp.where(first, quarter_of(2), quarter_of(1)), chunk))
    passed.append(passed_on(chunk))
    chunk = lax.ppermute(after(quarter_of(2), chunk, passed[0][0]), "pipe", [(1, 0)])
    passed.append(passed_on(chunk))
    chunk = lax.ppermute(after(quarter(own_merge), chunk, passed[1][0]), "pipe", [(1, 0)])
    passed.append(passed_on(chunk))
    brought = [block for pair in passed for block in pair]

    tokens, heads, shares, pixels = aggregate(
        place,
        alive_own,
        own_fields,
        other_fields,
        center,
        scale,
        keys,
        tvt,
        position_embed,
        (own_merge, *passed[0]),
    )
    heads_beside = partner(heads, "dp", 1)
    pack, proj, lse = attend(place, tokens, norm_gain, norm_bias, own_attend, brought[:6])
    middle, second_low = merge(
        place, tokens, pack, norm_gain, norm_bias, (own_merge, *brought[6:])
    )
    pack_beside = partner(pack, "dp", 1)
    units, hidden_sum = expand(
        place, second_low, out_low, up_weight, hidden_bias, down_weight, heads_beside
    )
    units_beside = partner(units, "dp", 1)
    scalars = jnp.stack([alive_own[0], weight_hat])
    result, middle_grad, branch_low, gain_second, bias_second, output_sum = contract(
        place,
        scalars,
        units,
        up_weight,
        down_weight,
        middle,
        cotangent,
        norm_gain[1:2],
        output_bias.reshape(1, D),
    )
    ff_width = FF // (2 * at.size)
    d_width = D // at.size
    direct = 2 * at.chips == BLOCKS
    wide_place = jnp.stack([pipe * SPANS + chip if direct else 0 * chip, core]).astype(jnp.int32)
    square_place = jnp.stack([pipe, chip if direct else 0 * chip]).astype(jnp.int32)
    both_units = (units, units_beside)
    down_send, down_keep = wide_grads(
        wide_place,
        out_low,
        both_units,
        0,
        True,
        (branch_low,),
        "down_grads",
    )
    up_send, up_keep = wide_grads(
        wide_place,
        second_low,
        both_units,
        1,
        False,
        (down_keep,),
        "up_grads",
    )
    right_own, right_send, token_grad, gain_first, bias_first = attend_back(
        place,
        middle_grad,
        branch_low,
        proj,
        lse,
        tokens,
        norm_gain,
        own_attend,
        own_merge,
        brought,
        (down_keep, up_keep),
    )
    right_beside = partner(right_send, "dp", 1)
    tail_own, tail_send, field_grads = aggregate_back(
        place,
        alive_own,
        token_grad,
        pixels,
        keys,
        tvt,
        shares,
        (gain_first, gain_second, bias_first, bias_second, output_sum, hidden_sum),
        (own_merge, *passed[0]),
    )
    tail_beside = partner(tail_send, "dp", 1)

    if direct:
        groups = at.groups[1:]
        down_sum = after(down_keep, tail_own).astype(F32) + swap(down_send).astype(F32)
        down_sum = down_sum.astype(BF).reshape(2, 4, HALF, BLOCK)
        up_sum = after(up_keep, tail_own).astype(F32) + partner(up_send, "dp", 2).astype(F32)
        up_sum = up_sum.astype(BF).reshape(2, 4, HALF, BLOCK)
        down_brought = partner(down_sum[1], "dp", 2)
        up_brought = swap(up_sum[1])
        started = (down_sum, up_sum)
    else:
        groups = at.groups
        started = (down_keep, up_keep)

        def spread(array):
            array = array.transpose(4, 0, 1, 2, 3, 5).reshape(HALF, 2 * at.chips, -1)
            array = at.relative(array.transpose(1, 0, 2), pipe * at.chips + chip)
            array = array.reshape(2, at.chips, HALF, -1)
            total = array[0].astype(F32) + swap(array[1]).astype(F32)
            return at.grouped(total.astype(BF))

        down_wide = jnp.stack([down_keep, down_send]).transpose(0, 2, 3, 1, 4, 5)
        wide = [spread(down_wide), spread(jnp.stack([up_keep, up_send], axis=3))]

    send, keep, cross_send, cross_keep = square_grads(
        square_place,
        (tail_own, tail_beside),
        (heads, heads_beside),
        (pack, pack_beside),
        (right_own, right_beside),
        started,
    )
    if direct:
        wide = [
            (down_sum[0].astype(F32) + after(down_brought, send).astype(F32)).astype(BF),
            (up_sum[0].astype(F32) + after(up_brought, send).astype(F32)).astype(BF),
        ]
        wide = jnp.stack(wide, axis=1)
        shared = partner(after(send, wide), "dp", 2)
        crossed = swap(after(cross_send, wide))
        cross = (cross_keep.astype(F32) + crossed.astype(F32)).astype(BF)
        cross_brought = partner(cross[1], "dp", 2)
        keep = after(keep, cross)
        square = (keep.astype(F32) + shared.astype(F32)).astype(BF)
        cross = (cross[0].astype(F32) + after(cross_brought, square).astype(F32)).astype(BF)
        square = jnp.concatenate([square, cross], axis=1)
        wide = at.reduced(wide, groups)
        square = at.reduced(after(square, wide), groups)
        field_grads, result = after((field_grads, result), cross_brought)
    else:
        wide = jnp.stack([at.reduced(array, groups) for array in wide])

        def rows_of(array):
            return at.relative(array.reshape(at.chips, -1, HALF), chip)

        whole = jnp.stack([keep, send], axis=1).reshape(SPANS, PARTS, HALF)
        cross = (cross_keep.astype(F32) + swap(cross_send).astype(F32)).astype(BF)
        cross = cross.transpose(1, 0, 2, 3).reshape(SPANS, PARTS, HALF)
        square = [
            rows_of(array[:, n * ROWS : (n + 1) * ROWS]) for array in (whole, cross) for n in (0, 1)
        ]
        square = at.reduced(at.grouped(jnp.concatenate(square, axis=1)), groups)

    wide = wide.reshape(2, HALF, 2, ff_width)
    other = partner(pick(wide, 1 - core, 2).astype(BF), "dp", 1).astype(F32)
    own = pick(wide, core, 2)
    wide = jnp.concatenate(
        [jnp.where(core == 0, own, other), jnp.where(core == 0, other, own)], axis=1
    )
    down_part, up_part = wide[0].T, wide[1]

    lot = 2 * d_width
    part = TAIL // (2 * at.chips)
    query_part = square[:lot]
    tail = square[lot : lot + 2 * part]
    merge_sum = square[lot + 2 * part : 2 * lot + 2 * part]
    cross = square[2 * lot + 2 * part :]
    sent = jnp.concatenate(
        [query_part, cross, jnp.where(first, tail[part:], tail[:part])], axis=0
    ).astype(BF)
    came = swap(sent).astype(F32)
    section_sum = jnp.stack(
        [merge_sum, query_part + came[:lot], came[lot : 2 * lot], cross]
    )
    tail = (jnp.where(first, tail[:part], tail[part:]) + came[2 * lot :]).astype(BF)
    section_sum = section_sum.reshape(4, 2, d_width, HALF).transpose(1, 0, 2, 3)
    section_part = at.over_cores(section_sum)
    merge_part = section_part[0]
    second_attend = section_part[1:]

    tail = at.gather(jnp.stack([tail, swap(tail)]))
    tail = jnp.stack([tail, partner(tail, "dp", 1)])
    spot = jnp.stack([pipe, core, chip]).astype(jnp.int32)
    position_sum, table_mix, small, key_grads, key_query_grads, query_low, query_sum = finish(
        spot, tail, table, own_attend, at.chips
    )
    table_mix = table_mix[:, :ROWS_TABLE].astype(BF)
    hidden_sum = small[5:9].reshape(FF)

    came = swap(jnp.where(first, result, tokens))
    outputs = jnp.stack([jnp.where(first, tokens, came), jnp.where(first, came, result)])
    field_halves = field_grads.reshape(2, half_vars, rows, cols)
    field_came = swap(pick(field_halves, 1 - pipe).astype(BF)).astype(F32)
    field_own = pick(field_halves, pipe)
    own_scale = lax.rsqrt(spread_new + EPSILON)
    field_out = (
        jnp.stack(
            [
                jnp.where(first, field_own, field_came),
                jnp.where(first, field_came, field_own),
            ]
        )
        * own_scale[None, :, None, None]
    )

    query_sum = from_first(query_sum[:1])
    own_rows = at.dp * d_width
    query_rows = lax.dynamic_slice_in_dim(variable_query, own_rows, d_width).astype(F32)
    key_rows = lax.dynamic_slice_in_dim(key_query_grads, own_rows, d_width, 1)
    key_rows = key_rows.T[:, :, None] * query[0].reshape(1, HEADS, HDIM) * scale_heads
    table_rows = lax.dynamic_slice_in_dim(table, own_rows, d_width, 1)
    first_attend = jnp.stack(
        [
            query_rows[:, None] * query_low[:1],
            key_rows.reshape(d_width, D),
            dot(table_rows, table_mix, 0, 1),
        ]
    )
    attend_part = jnp.where(first, first_attend, second_attend)

    value_pair = passed[1][0]
    value_pair = jnp.where(side == 0, value_pair, value_pair[::-1]).reshape(HALF, D)
    value_own = lax.dynamic_slice(own_attend, (jnp.int32(2), core * HALF, jnp.int32(0)), (1, HALF, D))
    value_own = jnp.where(first, value_own[0], value_pair)
    table_half = dot(table_mix, value_own, 0, 1)
    beside = partner(table_half, "dp", 1)
    key_query = tvt[:, ROWS_TABLE:].astype(F32)
    table_sum = jnp.concatenate(
        [jnp.where(core == 0, table_half, beside), jnp.where(core == 0, beside, table_half)],
        axis=1,
    ) + lax.dot_general(
        key_grads, key_query, (((1,), (1,)), ((), ())), precision=PRECISE
    )
    embed_grads = table_sum[: VARS * PIECES].reshape(PIECES, VARS, D).transpose(1, 0, 2)
    variable_grads = table_sum[VARS * PIECES :]
    hidden_part = lax.dynamic_slice_in_dim(
        hidden_sum, (pipe * at.size + at.dp) * ff_width, ff_width
    )
    return (
        statistics,
        outputs[None],
        field_out,
        embed_grads,
        variable_grads,
        query_sum.reshape(D),
        attend_part[None],
        merge_part[None],
        position_sum,
        small[0:2],
        small[2:4],
        up_part,
        hidden_part,
        down_part,
        small[4],
    )


def solution(mesh):
    return jax.shard_map(
        on_device,
        mesh=mesh,
        in_specs=(
            P("dp", "pipe", None, None),
            P("dp"),
            P("dp"),
            P(None, "pipe"),
            P(),
            P(),
            P(),
            P("pipe", None, None, None),
            P("pipe", None, None),
            P(),
            P(),
            P(),
            P(),
            P(),
            P(),
            P(),
            P("dp", None, None),
        ),
        out_specs=(
            P(None, "pipe"),
            P("pipe", "dp", None, None),
            P("dp", "pipe", None, None),
            P(),
            P(),
            P(),
            P("pipe", None, "dp", None),
            P("pipe", "dp", None),
            P(),
            P(),
            P(),
            P(None, ("pipe", "dp")),
            P(("pipe", "dp")),
            P(("pipe", "dp"), None),
            P(),
        ),
        check_vma=False,
    )
```

```python
import functools

import jax
import jax.numpy as jnp
from jax import lax
from jax.experimental import pallas as pl
from jax.experimental.pallas import tpu as pltpu
from jax.sharding import PartitionSpec as P

D = 1024
HEADS = 16
HDIM = 64
FF = 4096
VARS = 48
PATCH = 2
PATCHES = 512
PIECES = PATCH * PATCH
ROWS_TABLE = VARS * (PIECES + 1)
HALF = D // 2
QUARTER = D // 4
TABLE_PAD = 256
FF_TILE = 512
FF_STEPS = FF // FF_TILE
PAIRS = HEADS // 2
LANES = 2 * HDIM
CHUNK = 64
TOKENS_BACK = 2

PRECISE = lax.Precision.HIGHEST
EPSILON = 1e-05
MOMENTUM = 0.1
BF = jnp.bfloat16
F32 = jnp.float32
VMEM_LIMIT = 56 * 1024 * 1024


def dot(left, right, left_dim, right_dim):
    return lax.dot_general(
        left, right, (((left_dim,), (right_dim,)), ((), ())), preferred_element_type=F32
    )


VMEM = pl.BlockSpec(memory_space=pltpu.VMEM)
SMEM = pl.BlockSpec(memory_space=pltpu.SMEM)
ANYWHERE = pl.BlockSpec(memory_space=pl.ANY)


def shape(dims, kind):
    return jax.ShapeDtypeStruct(dims, kind)


def params(grid=0):
    semantics = ("arbitrary",) * grid if grid else None
    return pltpu.CompilerParams(vmem_limit_bytes=VMEM_LIMIT, dimension_semantics=semantics)


def cost():
    return pl.CostEstimate(flops=1000, bytes_accessed=1000, transcendentals=0)


def section_copies(place_ref, section, own, brought, targets, sems):
    core, side = place_ref[1], place_ref[2]

    def rows(core, side):
        return pl.ds(pl.multiple_of((2 * core + side) * QUARTER, QUARTER), QUARTER)

    @pl.when(place_ref[0] == section)
    def _():
        for n, target in enumerate(targets):
            for quarter in range(4):
                part = pl.ds(quarter * QUARTER, QUARTER)
                pltpu.make_async_copy(
                    own[n].at[part], target.at[part], sems.at[n, quarter]
                ).start()

    @pl.when(place_ref[0] != section)
    def _():
        for n, target in enumerate(targets):
            for other in range(2):
                for turn in range(2):
                    place = rows(core + other - 2 * core * other, side + turn - 2 * side * turn)
                    pltpu.make_async_copy(
                        brought[n][other].at[turn], target.at[place], sems.at[n, 2 * other + turn]
                    ).start()

    def wait(n):
        for quarter in range(4):
            part = pl.ds(quarter * QUARTER, QUARTER)
            pltpu.make_async_copy(
                brought[n][0].at[0], targets[n].at[part], sems.at[n, quarter]
            ).wait()

    return wait


def normalized(values):
    center = values - jnp.mean(values, axis=-1, keepdims=True)
    spread = jnp.mean(center * center, axis=-1, keepdims=True)
    inverse = lax.rsqrt(spread + EPSILON)
    return center * inverse, inverse


def norm_back(xhat, inverse, gain, grad):
    scaled = grad * gain
    first = jnp.mean(scaled, axis=-1, keepdims=True)
    second = jnp.mean(scaled * xhat, axis=-1, keepdims=True)
    return (scaled - first - xhat * second) * inverse


def row_chunks(body):
    def step(i, carry):
        body(pl.ds(pl.multiple_of(i * CHUNK, CHUNK), CHUNK))
        return carry

    lax.fori_loop(0, PATCHES // CHUNK, step, 0)


def column_tiles(width, body):
    def step(i, carry):
        body(pl.ds(pl.multiple_of(i * width, width), width))
        return carry

    lax.fori_loop(0, D // width, step, 0)


def head_rows(width):
    row = lax.broadcasted_iota(jnp.int32, (HEADS, width), 0)
    column = lax.broadcasted_iota(jnp.int32, (HEADS, width), 1)
    start = row * HDIM
    return (column >= start) & (column < start + HDIM)


def tables_kernel(query_ref, table_ref, weight_ref, low_ref, keys_ref, value_ref):
    given = jnp.broadcast_to(query_ref[...], (HEADS, D)).astype(BF)
    query = dot(given, weight_ref[0], 1, 0).astype(BF).astype(F32)
    low_ref[...] = query
    spread = jnp.where(head_rows(D), query, 0.0).astype(BF)
    key_query = (dot(spread, weight_ref[1], 1, 1) * HDIM ** (-0.5)).astype(BF)
    keys_ref[...] = dot(table_ref[...], key_query, 1, 1)
    values = dot(table_ref[...], weight_ref[2], 1, 0)
    value_ref[...] = jnp.concatenate([values, key_query.astype(F32)], axis=0).T


def tables(query, table, weights):
    return pl.pallas_call(
        tables_kernel,
        out_shape=(
            shape((HEADS, D), F32),
            shape((ROWS_TABLE, HEADS), F32),
            shape((D, TABLE_PAD), F32),
        ),
        in_specs=[VMEM] * 3,
        out_specs=(VMEM,) * 3,
        compiler_params=params(),
        cost_estimate=cost(),
        name="tables",
    )(query, table, weights)


COLS = 128
STRIPES = 16


def column_order():
    row = lax.broadcasted_iota(jnp.int32, (COLS, COLS), 0)
    column = lax.broadcasted_iota(jnp.int32, (COLS, COLS), 1)
    place = jnp.where(column < COLS // 2, 2 * column, 2 * column - COLS + 1)
    return (row == place).astype(F32)


def exact(left, right, right_dim):
    return lax.dot_general(
        left,
        right,
        (((1,), (right_dim,)), ((), ())),
        precision=PRECISE,
        preferred_element_type=F32,
    )


def head_keys(keys_ref, h):
    keys = keys_ref[...]
    lane = lax.broadcasted_iota(jnp.int32, keys.shape, 1)
    return jnp.sum(jnp.where(lane == h, keys, 0.0), axis=1, keepdims=True)


def mixed_rows(shares, pixels_ref):
    return jnp.concatenate(
        [(shares * pixels_ref[k]).astype(BF) for k in range(PIECES)]
        + [shares.astype(BF), jnp.zeros((TABLE_PAD - ROWS_TABLE, PATCHES), BF)],
        axis=0,
    )


def aggregate_kernel(
    place_ref,
    alive_ref,
    own_field_ref,
    other_field_ref,
    center_ref,
    scale_ref,
    keys_ref,
    tvt_ref,
    position_ref,
    own_ref,
    brought_ref,
    beside_ref,
    tokens_ref,
    heads_ref,
    shares_ref,
    pixels_ref,
    merge_ref,
    grid_ref,
    sems,
):
    wait = section_copies(
        place_ref, 0, [own_ref], [(brought_ref, beside_ref)], [merge_ref], sems
    )
    alive = alive_ref[0]
    order = column_order()
    half = VARS // 2 * STRIPES
    own, other = own_field_ref[...], other_field_ref[...]
    grid_ref[:half] = exact(jnp.where(place_ref[0] == 0, own, other), order, 0)
    grid_ref[half:] = exact(jnp.where(place_ref[0] == 0, other, own), order, 0)
    center, scale = center_ref[...], scale_ref[...]
    low_lane = lax.broadcasted_iota(jnp.int32, (VARS, COLS), 1) < COLS // 2

    def stripe(r):
        values = grid_ref[pl.ds(r, VARS, stride=STRIPES), :]
        return ((values - center) * scale).astype(BF).astype(F32)

    for a in range(PATCH):
        for j in range(PATCHES // COLS):
            even, odd = stripe(4 * j + a), stripe(4 * j + 2 + a)
            columns = slice(j * COLS, (j + 1) * COLS)
            pixels_ref[2 * a, :, columns] = jnp.where(
                low_lane, even, pltpu.roll(odd, COLS // 2, 1)
            )
            pixels_ref[2 * a + 1, :, columns] = jnp.where(
                low_lane, pltpu.roll(even, COLS // 2, 1), odd
            )

    def head(h, carry):
        keys = head_keys(keys_ref, h)
        scores = keys[PIECES * VARS :]
        for k in range(PIECES):
            scores = scores + keys[k * VARS : (k + 1) * VARS] * pixels_ref[k]
        top = jnp.max(scores, axis=0, keepdims=True)
        powers = jnp.exp(scores - top)
        shares = powers / jnp.sum(powers, axis=0, keepdims=True)
        shares_ref[h] = shares
        rows = pl.ds(pl.multiple_of(h * HDIM, HDIM), HDIM)
        heads_ref[rows, :] = dot(tvt_ref[rows, :], mixed_rows(shares, pixels_ref), 1, 0).astype(
            BF
        )
        return carry

    lax.fori_loop(0, HEADS, head, 0)
    wait(0)
    heads = heads_ref[...]

    def tile(columns):
        merged = dot(heads, merge_ref[:, columns], 0, 0)
        tokens_ref[:, columns] = (alive * (merged + position_ref[:, columns].astype(F32))).astype(
            BF
        )

    column_tiles(256, tile)


def aggregate(place, alive, own_field, other_field, center, scale, keys, tvt, position, merge):
    return pl.pallas_call(
        aggregate_kernel,
        out_shape=(
            shape((PATCHES, D), BF),
            shape((D, PATCHES), BF),
            shape((HEADS, VARS, PATCHES), F32),
            shape((PIECES, VARS, PATCHES), F32),
        ),
        in_specs=[SMEM, SMEM] + [VMEM] * 7 + [ANYWHERE] * 3,
        out_specs=(VMEM,) * 4,
        scratch_shapes=[
            pltpu.VMEM((D, D), BF),
            pltpu.VMEM((VARS * STRIPES, COLS), F32),
            pltpu.SemaphoreType.DMA((1, 4)),
        ],
        compiler_params=params(),
        cost_estimate=cost(),
        name="aggregate",
    )(place, alive, own_field, other_field, center, scale, keys, tvt, position, *merge)


def attend_kernel(place_ref, tokens_ref, gain_ref, bias_ref, attend_ref, *refs):
    brought = [(refs[2 * n], refs[2 * n + 1]) for n in range(3)]
    pack_ref, proj_ref, lse_ref, weight_ref, first_ref, sems = refs[6:]
    wait = section_copies(
        place_ref,
        1,
        [attend_ref.at[j] for j in range(3)],
        brought,
        [weight_ref.at[j] for j in range(3)],
        sems,
    )

    def first_norm(rows):
        xhat, _ = normalized(tokens_ref[rows, :].astype(F32))
        first_ref[rows, :] = (xhat * gain_ref[0:1, :] + bias_ref[0:1, :]).astype(BF)

    row_chunks(first_norm)
    pack_ref[:D, :] = first_ref[...].T
    for j in range(3):
        wait(j)
        column_tiles(
            256,
            lambda columns: proj_ref.__setitem__(
                (j, slice(None), columns),
                dot(first_ref[...], weight_ref[j, :, columns], 1, 0).astype(BF),
            ),
        )

    lane = lax.broadcasted_iota(jnp.int32, (PATCHES, LANES), 1)

    def pair(i, carry):
        columns = pl.ds(pl.multiple_of(i * LANES, LANES), LANES)
        queries = proj_ref[0, :, columns]
        keys = proj_ref[1, :, columns]
        values = proj_ref[2, :, columns].T
        for side in range(2):
            inside = (lane < HDIM) if side == 0 else (lane >= HDIM)
            key = jnp.where(inside, keys * HDIM ** (-0.5), jnp.zeros_like(keys)).astype(BF)
            scores = dot(key, queries, 1, 1)
            top = jnp.max(scores, axis=0, keepdims=True)
            powers = jnp.exp(scores - top)
            whole = jnp.sum(powers, axis=0, keepdims=True)
            probs = (powers * (1.0 / whole)).astype(BF)
            lse_ref[i, side : side + 1, :] = top + jnp.log(whole)
            value = values[side * HDIM : (side + 1) * HDIM]
            rows = pl.ds(pl.multiple_of(D + i * LANES + side * HDIM, HDIM), HDIM)
            pack_ref[rows, :] = dot(value, probs, 1, 0).astype(BF)
        return carry

    lax.fori_loop(0, PAIRS, pair, 0)


def attend(place, tokens, gain, bias, own_attend, brought):
    return pl.pallas_call(
        attend_kernel,
        out_shape=(
            shape((2 * D, PATCHES), BF),
            shape((3, PATCHES, D), BF),
            shape((PAIRS, 2, PATCHES), F32),
        ),
        in_specs=[SMEM] + [VMEM] * 3 + [ANYWHERE] * 7,
        out_specs=(VMEM,) * 3,
        scratch_shapes=[
            pltpu.VMEM((3, D, D), BF),
            pltpu.VMEM((PATCHES, D), BF),
            pltpu.SemaphoreType.DMA((3, 4)),
        ],
        compiler_params=params(),
        cost_estimate=cost(),
        name="attend",
    )(place, tokens, gain, bias, own_attend, *brought)


def merge_kernel(
    place_ref,
    tokens_ref,
    pack_ref,
    gain_ref,
    bias_ref,
    own_ref,
    brought_ref,
    beside_ref,
    middle_ref,
    second_ref,
    merge_ref,
    sems,
):
    wait = section_copies(
        place_ref, 1, [own_ref], [(brought_ref, beside_ref)], [merge_ref], sems
    )
    wait(0)
    context = pack_ref[...]
    column_tiles(
        256,
        lambda columns: middle_ref.__setitem__(
            (slice(None), columns),
            tokens_ref[:, columns].astype(F32) + dot(context, merge_ref[:, columns], 0, 0),
        ),
    )

    def second_norm(rows):
        xhat, _ = normalized(middle_ref[rows, :])
        second_ref[rows, :] = (xhat * gain_ref[1:2, :] + bias_ref[1:2, :]).astype(BF)

    row_chunks(second_norm)


def merge(place, tokens, pack, gain, bias, weights):
    return pl.pallas_call(
        merge_kernel,
        grid=(1,),
        out_shape=(shape((PATCHES, D), F32), shape((PATCHES, D), BF)),
        in_specs=[SMEM, VMEM, pl.BlockSpec((D, PATCHES), lambda i: (1, 0)), VMEM, VMEM]
        + [ANYWHERE] * 3,
        out_specs=(VMEM,) * 2,
        scratch_shapes=[pltpu.VMEM((D, D), BF), pltpu.SemaphoreType.DMA((1, 4))],
        compiler_params=params(1),
        cost_estimate=cost(),
        name="merge",
    )(place, tokens, pack, gain, bias, *weights)


def gelu_parts(hidden):
    inverse = 1.0 / (1.0 + 0.23164190 * jnp.abs(hidden))
    decay = jnp.exp2(hidden * hidden * (-0.72134752))
    series = 0.5 * 1.061405429
    for factor in (-1.453152027, 1.421413741, -0.284496736, 0.254829592):
        series = series * inverse + 0.5 * factor
    tail = series * inverse * decay
    cdf = jnp.where(hidden >= 0.0, 1.0 - tail, tail)
    return cdf, decay * 0.3989422804014327


FF_PART = 256
UNITS = FF + HALF


def copy(source, target, sem):
    return pltpu.make_async_copy(source, target, sem)


def aligned(index, size):
    return pl.ds(pl.multiple_of(index * size, size), size)


def start_either(choice, source, if_true, if_false, sem):
    @pl.when(choice)
    def _():
        copy(source, if_true, sem).start()

    @pl.when(jnp.logical_not(choice))
    def _():
        copy(source, if_false, sem).start()


def expand_kernel(
    place_ref,
    second_ref,
    out_ref,
    bias_ref,
    up_any,
    down_any,
    after_any,
    units_any,
    sum_ref,
    up_ref,
    down_ref,
    tile_ref,
    in_sems,
    out_sems,
):
    def fetch(j):
        part = aligned(j, FF_TILE)
        return (
            copy(up_any.at[:, part], up_ref.at[:, part], in_sems.at[j, 0]),
            copy(down_any.at[part], down_ref.at[part], in_sems.at[j, 1]),
        )

    def put(j, slot):
        return copy(
            tile_ref.at[slot], units_any.at[:, :, aligned(j, FF_TILE)], out_sems.at[slot]
        )

    for j in range(FF_STEPS):
        for one in fetch(j):
            one.start()

    def step(j, carry):
        slot = lax.rem(j, 2)

        @pl.when(j >= 2)
        def _():
            put(j - 2, slot).wait()

        for one in fetch(j):
            one.wait()
        for part in range(FF_TILE // FF_PART):
            inner = slice(part * FF_PART, (part + 1) * FF_PART)
            start = pl.multiple_of(j * FF_TILE + part * FF_PART, FF_PART)
            columns = pl.ds(start, FF_PART)
            hidden = dot(second_ref[...], up_ref[:, columns], 1, 0) + bias_ref[:, columns]
            grad = dot(out_ref[...], down_ref[columns, :], 1, 1)
            cdf, density = gelu_parts(hidden)
            tile_ref[slot, 0, :, inner] = (hidden * cdf).astype(BF)
            low = (grad * (cdf + hidden * density)).astype(BF)
            tile_ref[slot, 1, :, inner] = low
            sum_ref[:, columns] = jnp.sum(low.astype(F32), axis=0, keepdims=True)
        put(j, slot).start()
        return carry

    lax.fori_loop(0, FF_STEPS, step, 0)
    others = aligned(1 - place_ref[1], HALF)
    put(FF_STEPS - 2, 0).wait()
    tile_ref[0, 0] = out_ref[:, others]
    tile_ref[0, 1] = second_ref[:, others]
    put(FF_STEPS, 0).start()
    put(FF_STEPS - 1, 1).wait()
    put(FF_STEPS, 0).wait()


def expand(place, second, out_low, up, bias, down, after):
    return pl.pallas_call(
        expand_kernel,
        out_shape=(shape((2, PATCHES, UNITS), BF), shape((1, FF), F32)),
        in_specs=[SMEM, VMEM, VMEM, VMEM, ANYWHERE, ANYWHERE, ANYWHERE],
        out_specs=(ANYWHERE, VMEM),
        scratch_shapes=[
            pltpu.VMEM((D, FF), BF),
            pltpu.VMEM((FF, D), BF),
            pltpu.VMEM((2, 2, PATCHES, FF_TILE), BF),
            pltpu.SemaphoreType.DMA((FF_STEPS, 2)),
            pltpu.SemaphoreType.DMA((2,)),
        ],
        compiler_params=params(),
        cost_estimate=cost(),
        name="expand",
    )(place, second, out_low, bias.reshape(1, FF), up, down, after)


DEPTHS = 4
DEPTH = FF // DEPTHS


def contract_kernel(
    place_ref,
    scalars_ref,
    gain_ref,
    bias_ref,
    units_any,
    up_any,
    down_any,
    middle_any,
    cotangent_any,
    result_ref,
    grad_ref,
    branch_ref,
    gain_grad_ref,
    bias_grad_ref,
    out_grad_ref,
    units_ref,
    up_ref,
    down_ref,
    middle_ref,
    cotangent_ref,
    total_ref,
    second_ref,
    sems,
):
    def fetch(n):
        which, c = divmod(n, DEPTHS)
        part = slice(c * DEPTH, (c + 1) * DEPTH)
        if which == 0:
            weight = copy(down_any.at[part], down_ref.at[part], sems.at[n, 1])
        else:
            weight = copy(up_any.at[:, part], up_ref.at[:, part], sems.at[n, 1])
        return (
            copy(units_any.at[which, :, part], units_ref.at[which, :, part], sems.at[n, 0]),
            weight,
        )

    rest = (
        copy(middle_any, middle_ref, sems.at[2 * DEPTHS, 0]),
        copy(cotangent_any.at[place_ref[0]], cotangent_ref, sems.at[2 * DEPTHS, 1]),
    )
    for n in range(2 * DEPTHS):
        for one in fetch(n):
            one.start()
    for one in rest:
        one.start()
    for n in range(2 * DEPTHS):
        which, c = divmod(n, DEPTHS)
        part = slice(c * DEPTH, (c + 1) * DEPTH)
        for one in fetch(n):
            one.wait()
        ref = second_ref if which else total_ref
        if which:
            product = dot(units_ref[1, :, part], up_ref[:, part], 1, 1)
        else:
            product = dot(units_ref[0, :, part], down_ref[part, :], 1, 0)
        if c:
            ref[...] += product
        else:
            ref[...] = product
    for one in rest:
        one.wait()
    alive, hat = scalars_ref[0], scalars_ref[1]
    gain_grad_ref[...] = jnp.zeros_like(gain_grad_ref)
    bias_grad_ref[...] = jnp.zeros_like(bias_grad_ref)
    out_grad_ref[...] = jnp.zeros_like(out_grad_ref)

    def chunk(rows):
        middle = middle_ref[rows, :]
        result_ref[rows, :] = (alive * (middle + total_ref[rows, :] + bias_ref[...])).astype(BF)
        xhat, inverse = normalized(middle)
        grad = second_ref[rows, :]
        gain_grad_ref[...] += jnp.sum(grad * xhat, axis=0, keepdims=True)
        bias_grad_ref[...] += jnp.sum(grad, axis=0, keepdims=True)
        out = cotangent_ref[rows, :].astype(F32) * hat
        out_grad_ref[...] += jnp.sum(out, axis=0, keepdims=True)
        whole = out + norm_back(xhat, inverse, gain_ref[...], grad)
        grad_ref[rows, :] = whole
        branch_ref[rows, :] = whole.astype(BF)

    row_chunks(chunk)


def contract(place, scalars, units, up, down, middle, cotangent, gain, bias):
    return pl.pallas_call(
        contract_kernel,
        out_shape=(
            shape((PATCHES, D), BF),
            shape((PATCHES, D), F32),
            shape((PATCHES, D), BF),
            shape((1, D), F32),
            shape((1, D), F32),
            shape((1, D), F32),
        ),
        in_specs=[SMEM, SMEM, VMEM, VMEM] + [ANYWHERE] * 5,
        out_specs=(VMEM,) * 6,
        scratch_shapes=[
            pltpu.VMEM((2, PATCHES, FF), BF),
            pltpu.VMEM((D, FF), BF),
            pltpu.VMEM((FF, D), BF),
            pltpu.VMEM((PATCHES, D), F32),
            pltpu.VMEM((PATCHES, D), BF),
            pltpu.VMEM((PATCHES, D), F32),
            pltpu.VMEM((PATCHES, D), F32),
            pltpu.SemaphoreType.DMA((2 * DEPTHS + 1, 2)),
        ],
        compiler_params=params(),
        cost_estimate=cost(),
        name="contract",
    )(place, scalars, gain, bias, units, up, down, middle, cotangent)


def attend_back_kernel(
    place_ref,
    grad_ref,
    branch_ref,
    proj_ref,
    lse_ref,
    tokens_ref,
    gain_ref,
    attend_ref,
    merge_ref,
    *refs,
):
    brought = [(refs[2 * n], refs[2 * n + 1]) for n in range(4)]
    outs = refs[8 + TOKENS_BACK :]
    keep_ref, send_ref, token_grad_ref, gain_grad_ref, bias_grad_ref = outs[:5]
    weight_ref, context_ref, first_ref, proj_grad_ref, sems = outs[5:]
    wait = section_copies(
        place_ref,
        1,
        [merge_ref] + [attend_ref.at[j] for j in range(3)],
        brought[3:] + brought[:3],
        [weight_ref.at[j] for j in range(4)],
        sems,
    )
    wait(0)
    branch = branch_ref[...]

    def context_tile(columns):
        context_ref[:, columns] = dot(branch, weight_ref[0, columns, :], 1, 1).astype(BF)

    column_tiles(256, context_tile)
    lane = lax.broadcasted_iota(jnp.int32, (PATCHES, LANES), 1)

    def pair(i, carry):
        columns = pl.ds(pl.multiple_of(i * LANES, LANES), LANES)
        queries = proj_ref[0, :, columns]
        keys = proj_ref[1, :, columns]
        values = proj_ref[2, :, columns]
        grads = context_ref[:, columns]
        keys_turned = keys.T
        blank = jnp.zeros_like(keys)
        query_grads, key_grads, value_grads = [], [], []
        for side in range(2):
            inside = (lane < HDIM) if side == 0 else (lane >= HDIM)
            key = jnp.where(inside, keys * HDIM ** (-0.5), blank).astype(BF)
            value = jnp.where(inside, values, blank)
            probs = jnp.exp(dot(key, queries, 1, 1) - lse_ref[i, side : side + 1, :])
            share_grad = dot(value, grads, 1, 1)
            weighted = probs * share_grad
            inner = jnp.sum(weighted, axis=0, keepdims=True)
            score_low = (weighted - probs * inner).astype(BF)
            value_grads.append(dot(probs.astype(BF), grads, 1, 0))
            key_grads.append(dot(score_low, queries, 1, 0))
            query_grads.append(
                dot(keys_turned[side * HDIM : (side + 1) * HDIM], score_low, 1, 0)
            )
        low = lane < HDIM
        query_grad = jnp.concatenate(query_grads, axis=0) * HDIM ** (-0.5)
        proj_grad_ref[0, :, columns] = query_grad.T.astype(BF)
        proj_grad_ref[1, :, columns] = (
            jnp.where(low, key_grads[0], key_grads[1]) * HDIM ** (-0.5)
        ).astype(BF)
        proj_grad_ref[2, :, columns] = jnp.where(low, value_grads[0], value_grads[1]).astype(BF)
        return carry

    lax.fori_loop(0, PAIRS, pair, 0)
    core = place_ref[1]
    owns = pl.ds(pl.multiple_of(core * HALF, HALF), HALF)
    others = pl.ds(pl.multiple_of((1 - core) * HALF, HALF), HALF)
    for j in range(3):
        keep_ref[j] = proj_grad_ref[j, :, owns]
        send_ref[j] = proj_grad_ref[j, :, others]
    keep_ref[3] = branch_ref[:, owns]
    send_ref[3] = branch_ref[:, others]
    for j in range(3):
        wait(j + 1)

    def first_tile(columns):
        total = dot(proj_grad_ref[0], weight_ref[1, columns, :], 1, 1)
        for j in range(1, 3):
            total = total + dot(proj_grad_ref[j], weight_ref[j + 1, columns, :], 1, 1)
        first_ref[:, columns] = total

    column_tiles(256, first_tile)
    gain_grad_ref[...] = jnp.zeros_like(gain_grad_ref)
    bias_grad_ref[...] = jnp.zeros_like(bias_grad_ref)

    def chunk(rows):
        xhat, inverse = normalized(tokens_ref[rows, :].astype(F32))
        grad = first_ref[rows, :]
        gain_grad_ref[...] += jnp.sum(grad * xhat, axis=0, keepdims=True)
        bias_grad_ref[...] += jnp.sum(grad, axis=0, keepdims=True)
        token_grad_ref[rows, :] = (
            grad_ref[rows, :] + norm_back(xhat, inverse, gain_ref[0:1, :], grad)
        ).astype(BF)

    row_chunks(chunk)


def attend_back(
    place, grad, branch, proj, lse, tokens, gain, own_attend, own_merge, brought, after
):
    return pl.pallas_call(
        attend_back_kernel,
        out_shape=(
            shape((4, PATCHES, HALF), BF),
            shape((4, PATCHES, HALF), BF),
            shape((PATCHES, D), BF),
            shape((1, D), F32),
            shape((1, D), F32),
        ),
        in_specs=[SMEM] + [VMEM] * 6 + [ANYWHERE] * (10 + TOKENS_BACK),
        out_specs=(VMEM,) * 5,
        scratch_shapes=[
            pltpu.VMEM((4, D, D), BF),
            pltpu.VMEM((PATCHES, D), BF),
            pltpu.VMEM((PATCHES, D), F32),
            pltpu.VMEM((3, PATCHES, D), BF),
            pltpu.SemaphoreType.DMA((4, 4)),
        ],
        compiler_params=params(),
        cost_estimate=cost(),
        name="attend_back",
    )(place, grad, branch, proj, lse, tokens, gain, own_attend, own_merge, *brought, *after)


MIX_AT = PATCHES
SMALL_AT = PATCHES + TABLE_PAD
KEYS_AT = SMALL_AT + 16
TAIL = KEYS_AT + ROWS_TABLE


def aggregate_back_kernel(
    place_ref,
    alive_ref,
    token_grad_ref,
    pixels_ref,
    keys_ref,
    tvt_ref,
    shares_ref,
    gain_first_ref,
    gain_second_ref,
    bias_first_ref,
    bias_second_ref,
    output_ref,
    hidden_ref,
    own_ref,
    brought_ref,
    beside_ref,
    keep_ref,
    send_ref,
    field_ref,
    key_grad_ref,
    head_ref,
    merge_ref,
    mix_ref,
    pixel_grad_ref,
    grid_ref,
    sems,
):
    wait = section_copies(
        place_ref, 0, [own_ref], [(brought_ref, beside_ref)], [merge_ref], sems
    )
    core = place_ref[1]
    owns = pl.ds(pl.multiple_of(core * HALF, HALF), HALF)
    others = pl.ds(pl.multiple_of((1 - core) * HALF, HALF), HALF)
    alive = alive_ref[0]
    pre = (token_grad_ref[...].astype(F32) * alive).astype(BF)
    keep_ref[:PATCHES, :] = (token_grad_ref[:, owns].astype(F32) * alive).astype(BF)
    send_ref[:PATCHES, :] = (token_grad_ref[:, others].astype(F32) * alive).astype(BF)
    wait(0)

    def head_tile(rows):
        head_ref[rows, :] = dot(merge_ref[rows, :], pre, 1, 1).astype(BF)

    column_tiles(256, head_tile)
    pixel_grad_ref[...] = jnp.zeros_like(pixel_grad_ref)
    key_grad_ref[...] = jnp.zeros_like(key_grad_ref)
    lane = lax.broadcasted_iota(jnp.int32, (VARS, HEADS), 1)

    def head(h, carry):
        rows = pl.ds(pl.multiple_of(h * HDIM, HDIM), HDIM)
        keys = head_keys(keys_ref, h)
        grads = head_ref[rows, :]
        shares = shares_ref[h]
        mix_ref[rows, :] = dot(grads, mixed_rows(shares, pixels_ref), 1, 1)
        row_grads = dot(tvt_ref[rows, :], grads, 0, 0)
        share_grads = row_grads[PIECES * VARS : ROWS_TABLE]
        for k in range(PIECES):
            share_grads = share_grads + row_grads[k * VARS : (k + 1) * VARS] * pixels_ref[k]
        inner = jnp.sum(shares * share_grads, axis=0, keepdims=True)
        scores = shares * (share_grads - inner)
        for k in range(PIECES + 1):
            piece = slice(k * VARS, (k + 1) * VARS)
            if k < PIECES:
                pixel_grad_ref[k] += shares * row_grads[piece] + scores * keys[piece]
                total = jnp.sum(scores * pixels_ref[k], axis=1, keepdims=True)
            else:
                total = jnp.sum(scores, axis=1, keepdims=True)
            key_grad_ref[piece, :] += jnp.where(lane == h, total, 0.0)
        return carry

    lax.fori_loop(0, HEADS, head, 0)
    for ref, start in ((keep_ref, core * HALF), (send_ref, (1 - core) * HALF)):
        for part in range(2):
            rows = pl.ds(pl.multiple_of(start + part * TABLE_PAD, TABLE_PAD), TABLE_PAD)
            ref[MIX_AT:SMALL_AT, part * TABLE_PAD : (part + 1) * TABLE_PAD] = mix_ref[
                rows, :
            ].astype(BF)
        columns = pl.ds(pl.multiple_of(start, HALF), HALF)
        small = [
            one[:, columns]
            for one in (
                gain_first_ref,
                gain_second_ref,
                bias_first_ref,
                bias_second_ref,
                output_ref,
            )
        ]
        for part in range(FF // D):
            small.append(hidden_ref[:, pl.ds(pl.multiple_of(part * D + start, HALF), HALF)])
        small.append(jnp.zeros((16 - len(small), HALF), F32))
        ref[SMALL_AT:KEYS_AT, :] = jnp.concatenate(small, axis=0).astype(BF)
        ref[KEYS_AT:, :] = jnp.concatenate(
            [key_grad_ref[...], jnp.zeros((ROWS_TABLE, HALF - HEADS), F32)], axis=1
        ).astype(BF)
    low_lane = lax.broadcasted_iota(jnp.int32, (VARS, COLS), 1) < COLS // 2
    for a in range(PATCH):
        for j in range(PATCHES // COLS):
            columns = slice(j * COLS, (j + 1) * COLS)
            low, high = pixel_grad_ref[2 * a, :, columns], pixel_grad_ref[2 * a + 1, :, columns]
            even = jnp.where(low_lane, low, pltpu.roll(high, COLS // 2, 1))
            odd = jnp.where(low_lane, pltpu.roll(low, COLS // 2, 1), high)
            grid_ref[pl.ds(4 * j + a, VARS, stride=STRIPES), :] = even
            grid_ref[pl.ds(4 * j + 2 + a, VARS, stride=STRIPES), :] = odd
    field_ref[...] = exact(grid_ref[...], column_order(), 1)


def aggregate_back(place, alive, token_grad, pixels, keys, tvt, shares, small, merge):
    return pl.pallas_call(
        aggregate_back_kernel,
        out_shape=(
            shape((TAIL, HALF), BF),
            shape((TAIL, HALF), BF),
            shape((VARS * STRIPES, COLS), F32),
        ),
        in_specs=[SMEM, SMEM] + [VMEM] * 11 + [ANYWHERE] * 3,
        out_specs=(VMEM,) * 3,
        scratch_shapes=[
            pltpu.VMEM((ROWS_TABLE, HEADS), F32),
            pltpu.VMEM((D, PATCHES), BF),
            pltpu.VMEM((D, D), BF),
            pltpu.VMEM((D, TABLE_PAD), F32),
            pltpu.VMEM((PIECES, VARS, PATCHES), F32),
            pltpu.VMEM((VARS * STRIPES, COLS), F32),
            pltpu.SemaphoreType.DMA((1, 4)),
        ],
        compiler_params=params(),
        cost_estimate=cost(),
        name="aggregate_back",
    )(place, alive, token_grad, pixels, keys, tvt, shares, *small, *merge)


BLOCKS = 16
BLOCK = FF // BLOCKS
SPANS = BLOCKS // 2
SPAN = 4 * BLOCK


def wide_kernel(which, by_pipe, place_ref, left_any, own_any, beside_any, *refs):
    send_any, keep_any, left_ref, turned_ref, right_ref, product_ref, sems, out_sems = refs[-8:]
    place, core = place_ref[0], place_ref[1]
    side, z_low = jnp.bitwise_and(place, 1), jnp.bitwise_and(lax.shift_right_logical(place, 1), 1)

    def fetch(i):
        columns = aligned(jnp.bitwise_xor(3 - i, lax.shift_right_logical(place, 2)), SPAN)
        return [
            copy(
                source.at[which, :, columns],
                right_ref.at[i, pl.ds(n * PATCHES, PATCHES)],
                sems.at[i, n],
            )
            for n, source in enumerate((own_any, beside_any))
        ]

    lefts = (
        copy(left_any.at[:, aligned(core, HALF)], left_ref.at[0], sems.at[4, 0]),
        copy(beside_any.at[which, :, pl.ds(FF, HALF)], left_ref.at[1], sems.at[4, 1]),
    )
    for one in lefts:
        one.start()
    for i in range(4):
        for one in fetch(i):
            one.start()
    for n, one in enumerate(lefts):
        one.wait()
        turned_ref[:, n * PATCHES : (n + 1) * PATCHES] = left_ref[n].T

    def put(i, block):
        source = product_ref.at[i % 2, :, pl.ds(block * BLOCK, BLOCK)]
        return source, out_sems.at[i % 2, block]

    def wait(i):
        for block in range(4):
            source, sem = put(i, block)
            copy(source, send_any.at[0, 0, 0], sem).wait()

    for i in range(4):
        for one in fetch(i):
            one.wait()
        if i >= 2:
            wait(i - 2)
        product_ref[i % 2] = dot(turned_ref[...], right_ref[i], 1, 0).astype(BF)
        pipe, z_high = divmod(3 - i, 2)
        for block in range(4):
            source, sem = put(i, block)
            to_side = jnp.bitwise_xor(block % 2, side)
            to_z = jnp.bitwise_xor(block // 2, z_low)
            if by_pipe:
                target = send_any if pipe else keep_any
                copy(source, target.at[to_side, z_high, to_z], sem).start()
            else:
                start_either(
                    to_side == 1,
                    source,
                    send_any.at[pipe, z_high, to_z],
                    keep_any.at[pipe, z_high, to_z],
                    sem,
                )
    wait(2)
    wait(3)


def wide_grads(place, left, right, which, by_pipe, after, name):
    return pl.pallas_call(
        functools.partial(wide_kernel, which, by_pipe),
        in_specs=[SMEM] + [ANYWHERE] * (3 + len(after)),
        out_specs=(ANYWHERE, ANYWHERE),
        out_shape=(shape((2, 2, 2, HALF, BLOCK), BF), shape((2, 2, 2, HALF, BLOCK), BF)),
        scratch_shapes=[
            pltpu.VMEM((2, PATCHES, HALF), BF),
            pltpu.VMEM((HALF, 2 * PATCHES), BF),
            pltpu.VMEM((4, 2 * PATCHES, SPAN), BF),
            pltpu.VMEM((2, HALF, SPAN), BF),
            pltpu.SemaphoreType.DMA((5, 2)),
            pltpu.SemaphoreType.DMA((2, 4)),
        ],
        compiler_params=params(),
        cost_estimate=cost(),
        name=name,
    )(place, left, *right, *after)


ROWS = D // SPANS
PARTS = 2 * ROWS


def square_kernel(
    place_ref,
    tail_own,
    tail_beside,
    heads_own,
    heads_beside,
    pack_own,
    pack_beside,
    right_own,
    right_beside,
    *refs,
):
    send_any, keep_any, cross_send_any, cross_keep_any = refs[-9:-5]
    left_ref, right_ref, product_ref, sems, out_sems = refs[-5:]
    pipe, place = place_ref[0], place_ref[1]
    side, z = jnp.bitwise_and(place, 1), lax.shift_right_logical(place, 1)
    lefts = [
        (pack_own.at[pl.ds(0, D)], pack_beside.at[pl.ds(0, D)]),
        (pack_own.at[pl.ds(D, D)], pack_beside.at[pl.ds(D, D)]),
        (heads_own, heads_beside),
    ]
    left_copies = [
        [
            copy(one, left_ref.at[n, :, pl.ds(m * PATCHES, PATCHES)], sems.at[n, m])
            for m, one in enumerate(pair)
        ]
        for n, pair in enumerate(lefts)
    ]
    right_copies = [
        [
            copy(one.at[n], right_ref.at[n, pl.ds(m * PATCHES, PATCHES)], sems.at[3 + n, m])
            for m, one in enumerate((right_own, right_beside))
        ]
        for n in range(4)
    ]
    for n in (0, 3, 1, 2):
        for one in (left_copies[n] if n < 3 else []) + right_copies[n]:
            one.start()
    right_ref[4, :PATCHES] = tail_own[:PATCHES]
    right_ref[4, PATCHES:] = tail_beside[:PATCHES]

    def put(slot, block):
        return product_ref.at[slot, pl.ds(block * ROWS, ROWS)], out_sems.at[slot, block]

    def wait(slot):
        for block in range(SPANS):
            source, sem = put(slot, block)
            copy(source, send_any.at[0, pl.ds(0, ROWS)], sem).wait()

    def share(slot, part):
        rows = pl.ds(part * ROWS, ROWS)
        for block in range(SPANS):
            source, sem = put(slot, block)
            to_z = jnp.bitwise_xor(block // 2, z)
            start_either(
                side != block % 2, source, send_any.at[to_z, rows], keep_any.at[to_z, rows], sem
            )

    def cross(slot, part, goal):
        rows = pl.ds(part * ROWS, ROWS)
        for block in range(SPANS):
            source, sem = put(slot, block)
            to_side = jnp.bitwise_xor(block % 2, side)
            to_z = jnp.bitwise_xor(block // 2, z)
            start_either(
                pipe != goal,
                source,
                cross_send_any.at[to_side, to_z, rows],
                cross_keep_any.at[to_side, to_z, rows],
                sem,
            )

    product_ref[0] = (tail_own[...].astype(F32) + tail_beside[...].astype(F32)).astype(BF)
    share(0, 1)
    for step, (left, right) in enumerate(((0, 0), (1, 3), (2, 4), (0, 1), (0, 2))):
        slot = (step + 1) % 2
        if step in (0, 1, 2):
            for one in left_copies[left]:
                one.wait()
        if right < 4:
            for one in right_copies[right]:
                one.wait()
        if step >= 1:
            wait(slot)
        for tile in range(2):
            rows = slice(tile * HALF, (tile + 1) * HALF)
            product_ref[slot, rows] = dot(left_ref[left, rows], right_ref[right], 1, 0).astype(BF)
        if step == 0:
            share(slot, 0)
        elif step == 1:
            cross(slot, 0, 1)
        elif step == 2:
            cross(slot, 0, 0)
        else:
            cross(slot, 1, step - 3)
    wait(0)
    wait(1)


def square_grads(place, tail, heads, pack, right, after):
    return pl.pallas_call(
        square_kernel,
        in_specs=[SMEM, VMEM, VMEM] + [ANYWHERE] * (6 + len(after)),
        out_specs=(ANYWHERE,) * 4,
        out_shape=(
            shape((4, PARTS, HALF), BF),
            shape((4, PARTS, HALF), BF),
            shape((2, 4, PARTS, HALF), BF),
            shape((2, 4, PARTS, HALF), BF),
        ),
        scratch_shapes=[
            pltpu.VMEM((3, D, 2 * PATCHES), BF),
            pltpu.VMEM((5, 2 * PATCHES, HALF), BF),
            pltpu.VMEM((2, D, HALF), BF),
            pltpu.SemaphoreType.DMA((7, 2)),
            pltpu.SemaphoreType.DMA((2, SPANS)),
        ],
        compiler_params=params(),
        cost_estimate=cost(),
        name="square_grads",
    )(place, *tail, *heads, *pack, *right, *after)


def first_sums_kernel(down_keep, down_came, up_keep, up_came, after_any, down_ref, up_ref):
    for z in range(4):
        at = (0, z // 2, z % 2)
        down_ref[z] = (down_keep[at].astype(F32) + down_came[at].astype(F32)).astype(BF)
        up_ref[z] = (up_keep[at].astype(F32) + up_came[at].astype(F32)).astype(BF)


def first_sums(down_keep, down_came, up_keep, up_came, after):
    half = pl.BlockSpec((1, 2, 2, HALF, BLOCK), lambda i: (1, 0, 0, 0, 0))
    return pl.pallas_call(
        first_sums_kernel,
        grid=(1,),
        in_specs=[half] * 4 + [ANYWHERE],
        out_specs=(VMEM, VMEM),
        out_shape=(shape((4, HALF, BLOCK), BF), shape((4, HALF, BLOCK), BF)),
        compiler_params=params(1),
        cost_estimate=cost(),
        name="first_sums",
    )(down_keep, down_came, up_keep, up_came, after)


def second_sums_kernel(
    down_keep, down_came, down_brought, up_keep, up_came, up_brought, after_any, *outs
):
    def added(keep, came, brought, z):
        at = (0, z // 2, z % 2)
        one = (keep[at].astype(F32) + came[at].astype(F32)).astype(BF).astype(F32)
        return (one + brought[z].astype(F32)).astype(BF)

    for z in range(4):
        outs[z][0] = added(down_keep, down_came, down_brought, z)
        outs[z][1] = added(up_keep, up_came, up_brought, z)


def second_sums(down_keep, down_came, down_brought, up_keep, up_came, up_brought, after):
    half = pl.BlockSpec((1, 2, 2, HALF, BLOCK), lambda i: (0, 0, 0, 0, 0))
    return pl.pallas_call(
        second_sums_kernel,
        grid=(1,),
        in_specs=[half, half, VMEM] * 2 + [ANYWHERE],
        out_specs=(VMEM,) * 4,
        out_shape=(shape((2, HALF, BLOCK), BF),) * 4,
        compiler_params=params(1),
        cost_estimate=cost(),
        name="second_sums",
    )(down_keep, down_came, down_brought, up_keep, up_came, up_brought, after)


def third_sums_kernel(keep, came, out_ref):
    for z in range(4):
        out_ref[z] = (keep[0, z].astype(F32) + came[0, z].astype(F32)).astype(BF)


def third_sums(keep, came):
    half = pl.BlockSpec((1, 4, PARTS, HALF), lambda i: (1, 0, 0, 0))
    return pl.pallas_call(
        third_sums_kernel,
        grid=(1,),
        in_specs=[half, half],
        out_specs=VMEM,
        out_shape=shape((4, PARTS, HALF), BF),
        compiler_params=params(1),
        cost_estimate=cost(),
        name="third_sums",
    )(keep, came)


def fourth_sums_kernel(keep, came, cross_keep, cross_came, brought, *refs):
    for z in range(4):
        out_ref = refs[len(refs) - 4 + z]
        out_ref[:PARTS] = (keep[z].astype(F32) + came[z].astype(F32)).astype(BF)
        one = (cross_keep[0, z].astype(F32) + cross_came[0, z].astype(F32)).astype(BF)
        out_ref[PARTS:] = (one.astype(F32) + brought[z].astype(F32)).astype(BF)


def fourth_sums(keep, came, cross_keep, cross_came, brought, after):
    half = pl.BlockSpec((1, 4, PARTS, HALF), lambda i: (0, 0, 0, 0))
    return pl.pallas_call(
        fourth_sums_kernel,
        grid=(1,),
        in_specs=[VMEM, VMEM, half, half, VMEM] + [ANYWHERE] * len(after),
        out_specs=(VMEM,) * 4,
        out_shape=(shape((2 * PARTS, HALF), BF),) * 4,
        compiler_params=params(1),
        cost_estimate=cost(),
        name="fourth_sums",
    )(keep, came, cross_keep, cross_came, brought, *after)


def finish_kernel(
    chips,
    place_ref,
    tail_ref,
    table_ref,
    query_ref,
    given_ref,
    value_ref,
    attend_ref,
    *refs,
):
    brought = [(refs[2 * n], refs[2 * n + 1]) for n in range(3)]
    position_ref, gain_ref, bias_ref, output_ref, hidden_ref = refs[6:11]
    embed_ref, variable_ref, attend_grad_ref, query_grad_ref = refs[11:15]
    weight_ref, whole_ref, mix_ref, rows_ref, turned_ref, sems = refs[15:]
    core, chip, spot = place_ref[1], place_ref[3], place_ref[4]
    wait = section_copies(
        place_ref,
        0,
        [attend_ref.at[j] for j in range(3)],
        brought,
        [weight_ref.at[j] for j in range(3)],
        sems,
    )
    part = TAIL // chips
    for c in range(2):
        for n in range(chips):
            whole_ref[c, n * part : (n + 1) * part, :] = tail_ref[
                jnp.bitwise_xor(c, core), jnp.bitwise_xor(n, chip)
            ].astype(F32)
    for c in range(2):
        columns = slice(c * HALF, (c + 1) * HALF)
        position_ref[:, columns] = whole_ref[c, :PATCHES, :]
        small = whole_ref[c, SMALL_AT:KEYS_AT, :]
        gain_ref[:, columns] = small[0:2]
        bias_ref[:, columns] = small[2:4]
        output_ref[:, columns] = small[4:5]
        hidden_ref[:, columns] = small[5:9]
        for n in range(2):
            start = c * HALF + n * TABLE_PAD
            mix_ref[start : start + TABLE_PAD, :] = whole_ref[
                c, MIX_AT:SMALL_AT, n * TABLE_PAD : (n + 1) * TABLE_PAD
            ].astype(BF)
    keys = whole_ref[0, KEYS_AT:, :HEADS]
    table = table_ref[...].astype(F32)
    grads = lax.dot_general(
        keys,
        table,
        (((0,), (0,)), ((), ())),
        precision=PRECISE,
        preferred_element_type=F32,
    ).astype(BF)
    mask = head_rows(D)
    wait(1)
    low = jnp.where(mask, dot(grads, weight_ref[1], 1, 0), 0.0)
    low = jnp.sum(low, axis=0, keepdims=True) * HDIM ** (-0.5)
    low = jnp.broadcast_to(low, (HEADS, D)).astype(BF)
    wait(0)
    query_grad_ref[...] = dot(low, weight_ref[0], 1, 1)[:1]
    mixed = mix_ref[...]
    wait(2)
    key_query = value_ref[...].astype(F32)[:, ROWS_TABLE:]
    table_grad = dot(mixed, weight_ref[2], 0, 1)[:ROWS_TABLE] + lax.dot_general(
        keys,
        key_query,
        (((1,), (1,)), ((), ())),
        precision=PRECISE,
        preferred_element_type=F32,
    )
    for k in range(PIECES):
        embed_ref[:, k, :] = table_grad[k * VARS : (k + 1) * VARS]
    variable_ref[...] = table_grad[PIECES * VARS :]
    size = attend_grad_ref.shape[1]
    rows = pl.ds(pl.multiple_of(spot * size, size), size)
    rows_ref[...] = jnp.concatenate([grads.astype(F32), given_ref[...]], axis=0).T
    turned_ref[...] = table.T
    own = rows_ref[rows, :]
    low = low.astype(F32)
    spread = jnp.where(mask, query_ref[...] * HDIM ** (-0.5), 0.0)
    attend_grad_ref[0] = own[:, HEADS : HEADS + 1] * low[:1]
    attend_grad_ref[1] = lax.dot_general(
        own[:, :HEADS],
        spread,
        (((1,), (0,)), ((), ())),
        precision=PRECISE,
        preferred_element_type=F32,
    )
    left = jnp.concatenate(
        [turned_ref[rows, :], jnp.zeros((size, TABLE_PAD - ROWS_TABLE), F32)], axis=1
    ).astype(BF)
    attend_grad_ref[2] = dot(left, mixed, 1, 1)


def finish(place, tail, table, query, given, value, weights, brought, chips, size):
    return pl.pallas_call(
        functools.partial(finish_kernel, chips),
        out_shape=(
            shape((PATCHES, D), F32),
            shape((2, D), F32),
            shape((2, D), F32),
            shape((1, D), F32),
            shape((FF // D, D), F32),
            shape((VARS, PIECES, D), F32),
            shape((VARS, D), F32),
            shape((3, size, D), F32),
            shape((1, D), F32),
        ),
        in_specs=[SMEM] + [VMEM] * 5 + [ANYWHERE] * 7,
        out_specs=(VMEM,) * 9,
        scratch_shapes=[
            pltpu.VMEM((3, D, D), BF),
            pltpu.VMEM((2, TAIL, HALF), F32),
            pltpu.VMEM((D, TABLE_PAD), BF),
            pltpu.VMEM((D, 2 * HEADS), F32),
            pltpu.VMEM((D, ROWS_TABLE), F32),
            pltpu.SemaphoreType.DMA((3, 4)),
        ],
        compiler_params=params(),
        cost_estimate=cost(),
        name="finish",
    )(place, tail, table, query, given, value, weights, *brought)


def partner(block, axis, distance):
    size = lax.axis_size(axis)
    return lax.ppermute(block, axis, [(i, i ^ distance) for i in range(size)])


def swap(block):
    return partner(block, "pipe", 1)


def pick(array, index, axis=0):
    return lax.dynamic_index_in_dim(array, index, axis, keepdims=False)


def tree_sum(terms):
    while len(terms) > 1:
        terms = [terms[2 * i] + terms[2 * i + 1] for i in range(len(terms) // 2)]
    return terms[0]


class Places:
    def __init__(self):
        self.pipe = lax.axis_index("pipe")
        self.dp = lax.axis_index("dp")
        self.size = lax.axis_size("dp")
        self.core = self.dp % 2
        self.chips = self.size // 2
        bits = self.size.bit_length() - 2
        low = bits % 2 if bits % 2 else 2
        self.groups = []
        at = 1
        while bits > 0:
            width = low if at == 1 else 2
            self.groups.append((at, width))
            at += width
            bits -= width

    def relative(self, array, place):
        for bit in range(array.shape[0].bit_length() - 1):
            paired = array.reshape(-1, 2, 2**bit, *array.shape[1:])
            flipped = jnp.where((place // 2**bit) % 2 == 1, paired[:, ::-1], paired)
            array = flipped.reshape(array.shape)
        return array

    def grouped(self, array):
        counts = [2**width for _, width in reversed(self.groups)]
        dims = array.shape[1:]
        array = array.reshape(*counts, *dims)
        order = list(range(len(counts)))[::-1] + list(range(len(counts), array.ndim))
        return array.transpose(order)

    def reduced(self, array, groups):
        for n, (at, width) in enumerate(groups):
            terms = [array[0].astype(F32)]
            for distance in range(1, 2**width):
                terms.append(partner(array[distance], "dp", distance * 2**at).astype(F32))
            array = tree_sum(terms)
            if n < len(groups) - 1:
                array = array.astype(BF)
        return array

    def over_cores(self, array):
        brought = partner(pick(array, 1 - self.core).astype(BF), "dp", 1).astype(F32)
        own = pick(array, self.core)
        return jnp.concatenate(
            [jnp.where(self.core == 0, own, brought), jnp.where(self.core == 0, brought, own)],
            axis=-1,
        )

    def last(self, parts, group):
        terms = [parts[0].astype(F32)]
        for distance in range(1, 2 ** group[1]):
            terms.append(partner(parts[distance], "dp", distance * 2 ** group[0]).astype(F32))
        return tree_sum(terms)

    def gather(self, block):
        blocks = block[None]
        for at, width in reversed(self.groups):
            parts = [partner(blocks, "dp", m * 2**at) for m in range(1, 2**width)]
            blocks = jnp.stack([blocks] + parts, axis=1).reshape(-1, *block.shape)
        return blocks

    def total(self, block):
        for bit in range(self.size.bit_length() - 1):
            block = block + partner(block, "dp", 2**bit)
        return block


def on_device(
    fields,
    item_weights,
    live_counts,
    running_stats,
    embed_weight,
    variable_embed,
    variable_query,
    attend_weight,
    merge_weight,
    position_embed,
    norm_gain,
    norm_bias,
    up_weight,
    hidden_bias,
    down_weight,
    output_bias,
    cotangent,
):
    at = Places()
    pipe, core = at.pipe, at.core
    first = pipe == 0
    side = (at.dp // 2) % 2
    chip = at.dp // 2
    place = jnp.stack([pipe, core, side]).astype(jnp.int32)
    micro, half_vars, rows, cols = fields.shape
    scale_heads = HDIM ** (-0.5)

    own_attend, own_merge = attend_weight[0], merge_weight[0]

    def quarter(weight):
        return lax.dynamic_slice_in_dim(weight, (2 * core + side) * QUARTER, QUARTER, 0)

    def quarter_of(j):
        start = (jnp.int32(j), (2 * core + side) * QUARTER, jnp.int32(0))
        return lax.dynamic_slice(own_attend, start, (1, QUARTER, D))[0]

    def after(value, *others):
        return lax.optimization_barrier((value, others))[0]

    def passed_on(block, before, behind):
        other = partner(after(block, *before), "dp", 2)
        pair = jnp.stack([block, after(other, *behind)])
        return pair, partner(pair, "dp", 1)

    chunk_first = swap(jnp.where(first, quarter(own_merge), quarter_of(0)))

    table = jnp.concatenate(
        [embed_weight.transpose(1, 0, 2).reshape(VARS * PIECES, D), variable_embed], axis=0
    )
    given = variable_query.astype(F32).reshape(1, D)
    query, table_keys, table_value = tables(given, table, own_attend)

    def from_first(block):
        return jnp.where(first, block, lax.ppermute(block, "pipe", [(0, 1)]))

    keys = from_first(table_keys)
    tvt = from_first(table_value.astype(BF))

    flat_fields = fields.reshape(micro, half_vars * rows, cols)
    other_fields = swap(pick(flat_fields, 1 - pipe))
    own_fields = pick(flat_fields, pipe)
    slots = jnp.arange(micro, dtype=jnp.int32)
    alive = (slots < live_counts[0]).astype(F32)
    omega = item_weights.astype(F32) * alive
    plain_sums = jnp.sum(fields, axis=(2, 3))
    square_sums = jnp.sum(fields * fields, axis=(2, 3))
    sums = jnp.concatenate(
        [
            jnp.sum(omega[:, None] * plain_sums, axis=0),
            jnp.sum(omega[:, None] * square_sums, axis=0),
            jnp.sum(omega)[None],
            jnp.sum(alive)[None],
        ]
    )
    sums = at.total(after(sums, table_value))
    total, live_total = sums[2 * half_vars], sums[2 * half_vars + 1]
    first_moment = after(sums, chunk_first)[:half_vars] / (total * rows * cols)
    second_moment = sums[half_vars : 2 * half_vars] / (total * rows * cols)
    center_new = (1.0 - MOMENTUM) * running_stats[0] + MOMENTUM * first_moment
    spread_new = (1.0 - MOMENTUM) * running_stats[1] + MOMENTUM * (
        second_moment - first_moment * first_moment
    )
    statistics = jnp.stack([center_new, spread_new])
    other_statistics = swap(statistics)
    all_statistics = jnp.concatenate(
        [
            jnp.where(first, statistics, other_statistics),
            jnp.where(first, other_statistics, statistics),
        ],
        axis=1,
    )
    center = all_statistics[0].reshape(VARS, 1)
    scale = lax.rsqrt(all_statistics[1] + EPSILON).reshape(VARS, 1)
    weight_hat = pick(omega, pipe) * live_total / total
    alive_own = pick(alive, pipe)[None]
    out_low = (pick(cotangent, pipe).astype(F32) * weight_hat).astype(BF)

    chunk = chunk_first
    chunks = [chunk]
    passed = [passed_on(chunk, (sums,), ())]
    chunk = swap(after(jnp.where(first, quarter_of(2), quarter_of(1)), chunk))
    passed.append(passed_on(chunk, (), ()))
    chunk = swap(after(jnp.where(first, quarter_of(0), quarter_of(2)), chunk, passed[0][0]))
    third = chunk
    chunk = swap(
        after(jnp.where(first, quarter_of(1), quarter(own_merge)), chunk, passed[1][0])
    )
    fourth = chunk
    alive_own = after(alive_own, third)

    tokens, heads, shares, pixels = aggregate(
        place,
        alive_own,
        own_fields,
        other_fields,
        center,
        scale,
        keys,
        tvt,
        position_embed,
        (own_merge, *passed[0]),
    )
    passed.append(passed_on(third, (), (tokens,)))
    heads_beside = partner(heads, "dp", 1)
    brought = [block for pair in passed for block in pair]
    pack, proj, lse = attend(place, tokens, norm_gain, norm_bias, own_attend, brought)
    passed.append(passed_on(fourth, (tokens,), (lse,)))
    brought = [block for pair in passed for block in pair]
    middle, second_low = merge(
        place, tokens, pack, norm_gain, norm_bias, (own_merge, *brought[6:])
    )
    pack_beside = partner(pack, "dp", 1)
    units, hidden_sum = expand(
        place, second_low, out_low, up_weight, hidden_bias, down_weight, heads_beside
    )
    units_beside = partner(units, "dp", 1)
    scalars = jnp.stack([alive_own[0], weight_hat])
    result, middle_grad, branch_low, gain_second, bias_second, output_sum = contract(
        place,
        scalars,
        units,
        up_weight,
        down_weight,
        middle,
        cotangent,
        norm_gain[1:2],
        output_bias.reshape(1, D),
    )
    ff_width = FF // (2 * at.size)
    d_width = D // at.size
    direct = 2 * at.chips == BLOCKS
    wide_place = jnp.stack([pipe * SPANS + chip if direct else 0 * chip, core]).astype(jnp.int32)
    square_place = jnp.stack([pipe, chip if direct else 0 * chip]).astype(jnp.int32)
    both_units = (units, units_beside)
    down_send, down_keep = wide_grads(
        wide_place,
        out_low,
        both_units,
        0,
        True,
        (branch_low,),
        "down_grads",
    )
    up_send, up_keep = wide_grads(
        wide_place,
        second_low,
        both_units,
        1,
        False,
        (down_keep,),
        "up_grads",
    )
    right_own, right_send, token_grad, gain_first, bias_first = attend_back(
        place,
        middle_grad,
        branch_low,
        proj,
        lse,
        tokens,
        norm_gain,
        own_attend,
        own_merge,
        brought,
        (down_keep, up_keep),
    )
    right_beside = partner(right_send, "dp", 1)
    tail_own, tail_send, field_grads = aggregate_back(
        place,
        alive_own,
        token_grad,
        pixels,
        keys,
        tvt,
        shares,
        (gain_first, gain_second, bias_first, bias_second, output_sum, hidden_sum),
        (own_merge, *passed[0]),
    )
    tail_beside = partner(tail_send, "dp", 1)

    if direct:
        groups = at.groups[1:]
        down_came, up_came = swap(down_send), partner(up_send, "dp", 2)
        down_next, up_next = first_sums(down_keep, down_came, up_keep, up_came, tail_own)
        down_brought = partner(down_next, "dp", 2)
        up_brought = swap(up_next)
        started = (down_next, up_next)
    else:
        groups = at.groups
        started = (down_keep, up_keep)

        def spread(array):
            array = array.transpose(4, 0, 1, 2, 3, 5).reshape(HALF, 2 * at.chips, -1)
            array = at.relative(array.transpose(1, 0, 2), pipe * at.chips + chip)
            array = array.reshape(2, at.chips, HALF, -1)
            total = array[0].astype(F32) + swap(array[1]).astype(F32)
            return at.grouped(total.astype(BF))

        down_wide = jnp.stack([down_keep, down_send]).transpose(0, 2, 3, 1, 4, 5)
        wide = [spread(down_wide), spread(jnp.stack([up_keep, up_send], axis=3))]

    send, keep, cross_send, cross_keep = square_grads(
        square_place,
        (tail_own, tail_beside),
        (heads, heads_beside),
        (pack, pack_beside),
        (right_own, right_beside),
        started,
    )
    if direct:
        wide = second_sums(
            down_keep, down_came, down_brought, up_keep, up_came, up_brought, send
        )
        shared = partner(after(send, wide), "dp", 2)
        crossed = swap(after(cross_send, wide))
        wide = at.last(wide, groups[0])
        cross_next = third_sums(cross_keep, crossed)
        cross_brought = partner(cross_next, "dp", 2)
        field_grads, result = after((field_grads, result), cross_next)
        came = swap(jnp.where(first, result, tokens))
        field_halves = field_grads.reshape(2, half_vars, rows, cols)
        field_came = swap(pick(field_halves, 1 - pipe).astype(BF)).astype(F32)
        square = fourth_sums(
            keep, shared, cross_keep, crossed, cross_brought, (came, field_came, wide)
        )
        square = at.last(square, groups[0])
    else:
        wide = jnp.stack([at.reduced(array, groups) for array in wide])

        def rows_of(array):
            return at.relative(array.reshape(at.chips, -1, HALF), chip)

        whole = jnp.stack([keep, send], axis=1).reshape(SPANS, PARTS, HALF)
        cross = (cross_keep.astype(F32) + swap(cross_send).astype(F32)).astype(BF)
        cross = cross.transpose(1, 0, 2, 3).reshape(SPANS, PARTS, HALF)
        square = [
            rows_of(array[:, n * ROWS : (n + 1) * ROWS]) for array in (whole, cross) for n in (0, 1)
        ]
        square = at.reduced(at.grouped(jnp.concatenate(square, axis=1)), groups)
        came = swap(jnp.where(first, result, tokens))
        field_halves = field_grads.reshape(2, half_vars, rows, cols)
        field_came = swap(pick(field_halves, 1 - pipe).astype(BF)).astype(F32)

    wide = wide.reshape(2, HALF, 2, ff_width)
    other = partner(pick(wide, 1 - core, 2).astype(BF), "dp", 1).astype(F32)
    own = pick(wide, core, 2)
    wide = jnp.concatenate(
        [jnp.where(core == 0, own, other), jnp.where(core == 0, other, own)], axis=1
    )
    down_part, up_part = wide[0].T, wide[1]

    lot = 2 * d_width
    part = TAIL // at.chips
    query_part = square[:lot]
    tail = square[lot : lot + part]
    merge_sum = square[lot + part : 2 * lot + part]
    cross = square[2 * lot + part :]
    tail_came = swap(tail.astype(BF)).astype(F32)
    sent = jnp.concatenate([query_part, cross], axis=0).astype(BF)
    section_came = swap(sent).astype(F32)
    section_sum = jnp.stack(
        [merge_sum, query_part + section_came[:lot], section_came[lot:], cross]
    )
    tail = (tail.astype(BF).astype(F32) + tail_came).astype(BF)
    section_sum = section_sum.reshape(4, 2, d_width, HALF).transpose(1, 0, 2, 3)
    section_part = at.over_cores(section_sum)
    merge_part = section_part[0]
    second_attend = section_part[1:]

    tail = at.gather(tail)
    tail = jnp.stack([tail, partner(tail, "dp", 1)])
    spot = jnp.stack([pipe, core, side, chip, at.dp]).astype(jnp.int32)
    (
        position_sum,
        gain_sum,
        bias_sum,
        output_sum,
        hidden_sum,
        embed_grads,
        variable_grads,
        first_attend,
        query_sum,
    ) = finish(
        spot,
        tail,
        table,
        query,
        jnp.broadcast_to(given, (HEADS, D)),
        tvt,
        own_attend,
        [*passed[2], *passed[3], *passed[1]],
        at.chips,
        d_width,
    )
    attend_part = jnp.where(first, first_attend, second_attend)
    hidden_sum = hidden_sum.reshape(FF)

    outputs = jnp.stack([jnp.where(first, tokens, came), jnp.where(first, came, result)])
    field_own = pick(field_halves, pipe)
    own_scale = lax.rsqrt(spread_new + EPSILON)
    field_out = (
        jnp.stack(
            [
                jnp.where(first, field_own, field_came),
                jnp.where(first, field_came, field_own),
            ]
        )
        * own_scale[None, :, None, None]
    )
    hidden_part = lax.dynamic_slice_in_dim(
        hidden_sum, (pipe * at.size + at.dp) * ff_width, ff_width
    )
    return (
        statistics,
        outputs[None],
        field_out,
        embed_grads,
        variable_grads,
        query_sum.reshape(D),
        attend_part[None],
        merge_part[None],
        position_sum,
        gain_sum,
        bias_sum,
        up_part,
        hidden_part,
        down_part,
        output_sum.reshape(D),
    )


def solution(mesh):
    return jax.shard_map(
        on_device,
        mesh=mesh,
        in_specs=(
            P("dp", "pipe", None, None),
            P("dp"),
            P("dp"),
            P(None, "pipe"),
            P(),
            P(),
            P(),
            P("pipe", None, None, None),
            P("pipe", None, None),
            P(),
            P(),
            P(),
            P(),
            P(),
            P(),
            P(),
            P("dp", None, None),
        ),
        out_specs=(
            P(None, "pipe"),
            P("pipe", "dp", None, None),
            P("dp", "pipe", None, None),
            P(),
            P(),
            P(),
            P("pipe", None, "dp", None),
            P("pipe", "dp", None),
            P(),
            P(),
            P(),
            P(None, ("pipe", "dp")),
            P(("pipe", "dp")),
            P(("pipe", "dp"), None),
            P(),
        ),
        check_vma=False,
    )
```

```python
import functools

import jax
import jax.numpy as jnp
from jax import lax
from jax.experimental import pallas as pl
from jax.experimental.pallas import tpu as pltpu
from jax.sharding import PartitionSpec as P

D = 1024
HEADS = 16
HDIM = 64
FF = 4096
VARS = 48
PATCH = 2
PATCHES = 512
PIECES = PATCH * PATCH
ROWS_TABLE = VARS * (PIECES + 1)
HALF = D // 2
QUARTER = D // 4
TABLE_PAD = 256
FF_TILE = 1024
FF_STEPS = FF // FF_TILE
PAIRS = HEADS // 2
LANES = 2 * HDIM
CHUNK = 128
TOKENS_BACK = 2

PRECISE = lax.Precision.HIGHEST
EPSILON = 1e-05
MOMENTUM = 0.1
BF = jnp.bfloat16
F32 = jnp.float32
VMEM_LIMIT = 56 * 1024 * 1024


def dot(left, right, left_dim, right_dim):
    return lax.dot_general(
        left, right, (((left_dim,), (right_dim,)), ((), ())), preferred_element_type=F32
    )


VMEM = pl.BlockSpec(memory_space=pltpu.VMEM)
SMEM = pl.BlockSpec(memory_space=pltpu.SMEM)
ANYWHERE = pl.BlockSpec(memory_space=pl.ANY)


def shape(dims, kind):
    return jax.ShapeDtypeStruct(dims, kind)


def params(grid=0):
    semantics = ("arbitrary",) * grid if grid else None
    return pltpu.CompilerParams(vmem_limit_bytes=VMEM_LIMIT, dimension_semantics=semantics)


def cost():
    return pl.CostEstimate(flops=1000, bytes_accessed=1000, transcendentals=0)


def section_copies(place_ref, section, own, brought, targets, sems):
    core, side = place_ref[1], place_ref[2]

    def rows(core, side):
        return pl.ds(pl.multiple_of((2 * core + side) * QUARTER, QUARTER), QUARTER)

    @pl.when(place_ref[0] == section)
    def _():
        for n, target in enumerate(targets):
            for quarter in range(4):
                part = pl.ds(quarter * QUARTER, QUARTER)
                pltpu.make_async_copy(
                    own[n].at[part], target.at[part], sems.at[n, quarter]
                ).start()

    @pl.when(place_ref[0] != section)
    def _():
        for n, target in enumerate(targets):
            for other in range(2):
                for turn in range(2):
                    place = rows(core + other - 2 * core * other, side + turn - 2 * side * turn)
                    pltpu.make_async_copy(
                        brought[n][other].at[turn], target.at[place], sems.at[n, 2 * other + turn]
                    ).start()

    def wait(n):
        for quarter in range(4):
            part = pl.ds(quarter * QUARTER, QUARTER)
            pltpu.make_async_copy(
                brought[n][0].at[0], targets[n].at[part], sems.at[n, quarter]
            ).wait()

    return wait


def normalized(values):
    center = values - jnp.mean(values, axis=-1, keepdims=True)
    spread = jnp.mean(center * center, axis=-1, keepdims=True)
    inverse = lax.rsqrt(spread + EPSILON)
    return center * inverse, inverse


def norm_back(xhat, inverse, gain, grad):
    scaled = grad * gain
    first = jnp.mean(scaled, axis=-1, keepdims=True)
    second = jnp.mean(scaled * xhat, axis=-1, keepdims=True)
    return (scaled - first - xhat * second) * inverse


def row_chunks(body):
    def step(i, carry):
        body(pl.ds(pl.multiple_of(i * CHUNK, CHUNK), CHUNK))
        return carry

    lax.fori_loop(0, PATCHES // CHUNK, step, 0)


def column_tiles(width, body):
    def step(i, carry):
        body(pl.ds(pl.multiple_of(i * width, width), width))
        return carry

    lax.fori_loop(0, D // width, step, 0)


def head_rows(width):
    row = lax.broadcasted_iota(jnp.int32, (HEADS, width), 0)
    column = lax.broadcasted_iota(jnp.int32, (HEADS, width), 1)
    start = row * HDIM
    return (column >= start) & (column < start + HDIM)


def tables_kernel(query_ref, table_ref, weight_ref, low_ref, keys_ref, value_ref):
    given = jnp.broadcast_to(query_ref[...], (HEADS, D)).astype(BF)
    query = dot(given, weight_ref[0], 1, 0).astype(BF).astype(F32)
    low_ref[...] = query
    spread = jnp.where(head_rows(D), query, 0.0).astype(BF)
    key_query = (dot(spread, weight_ref[1], 1, 1) * HDIM ** (-0.5)).astype(BF)
    keys_ref[...] = dot(table_ref[...], key_query, 1, 1)
    values = dot(table_ref[...], weight_ref[2], 1, 0)
    value_ref[...] = jnp.concatenate([values, key_query.astype(F32)], axis=0).T


def tables(query, table, weights):
    return pl.pallas_call(
        tables_kernel,
        out_shape=(
            shape((HEADS, D), F32),
            shape((ROWS_TABLE, HEADS), F32),
            shape((D, TABLE_PAD), F32),
        ),
        in_specs=[VMEM] * 3,
        out_specs=(VMEM,) * 3,
        compiler_params=params(),
        cost_estimate=cost(),
        name="tables",
    )(query, table, weights)


COLS = 128
STRIPES = 16


def column_order():
    row = lax.broadcasted_iota(jnp.int32, (COLS, COLS), 0)
    column = lax.broadcasted_iota(jnp.int32, (COLS, COLS), 1)
    place = jnp.where(column < COLS // 2, 2 * column, 2 * column - COLS + 1)
    return (row == place).astype(F32)


def exact(left, right, right_dim):
    return lax.dot_general(
        left,
        right,
        (((1,), (right_dim,)), ((), ())),
        precision=PRECISE,
        preferred_element_type=F32,
    )


def head_keys(keys_ref, h):
    keys = keys_ref[...]
    lane = lax.broadcasted_iota(jnp.int32, keys.shape, 1)
    return jnp.sum(jnp.where(lane == h, keys, 0.0), axis=1, keepdims=True)


def mixed_rows(shares, pixels_ref):
    return jnp.concatenate(
        [(shares * pixels_ref[k]).astype(BF) for k in range(PIECES)]
        + [shares.astype(BF), jnp.zeros((TABLE_PAD - ROWS_TABLE, PATCHES), BF)],
        axis=0,
    )


def aggregate_kernel(
    place_ref,
    alive_ref,
    own_field_ref,
    other_field_ref,
    center_ref,
    scale_ref,
    keys_ref,
    tvt_ref,
    position_ref,
    own_ref,
    brought_ref,
    beside_ref,
    tokens_ref,
    heads_ref,
    shares_ref,
    pixels_ref,
    merge_ref,
    grid_ref,
    sems,
):
    wait = section_copies(
        place_ref, 0, [own_ref], [(brought_ref, beside_ref)], [merge_ref], sems
    )
    alive = alive_ref[0]
    order = column_order()
    half = VARS // 2 * STRIPES
    own, other = own_field_ref[...], other_field_ref[...]
    grid_ref[:half] = exact(jnp.where(place_ref[0] == 0, own, other), order, 0)
    grid_ref[half:] = exact(jnp.where(place_ref[0] == 0, other, own), order, 0)
    center, scale = center_ref[...], scale_ref[...]
    low_lane = lax.broadcasted_iota(jnp.int32, (VARS, COLS), 1) < COLS // 2

    def stripe(r):
        values = grid_ref[pl.ds(r, VARS, stride=STRIPES), :]
        return ((values - center) * scale).astype(BF).astype(F32)

    for a in range(PATCH):
        for j in range(PATCHES // COLS):
            even, odd = stripe(4 * j + a), stripe(4 * j + 2 + a)
            columns = slice(j * COLS, (j + 1) * COLS)
            pixels_ref[2 * a, :, columns] = jnp.where(
                low_lane, even, pltpu.roll(odd, COLS // 2, 1)
            )
            pixels_ref[2 * a + 1, :, columns] = jnp.where(
                low_lane, pltpu.roll(even, COLS // 2, 1), odd
            )

    def head(h, carry):
        keys = head_keys(keys_ref, h)
        scores = keys[PIECES * VARS :]
        for k in range(PIECES):
            scores = scores + keys[k * VARS : (k + 1) * VARS] * pixels_ref[k]
        top = jnp.max(scores, axis=0, keepdims=True)
        powers = jnp.exp(scores - top)
        shares = powers / jnp.sum(powers, axis=0, keepdims=True)
        shares_ref[h] = shares
        rows = pl.ds(pl.multiple_of(h * HDIM, HDIM), HDIM)
        heads_ref[rows, :] = dot(tvt_ref[rows, :], mixed_rows(shares, pixels_ref), 1, 0).astype(
            BF
        )
        return carry

    lax.fori_loop(0, HEADS, head, 0)
    wait(0)
    heads = heads_ref[...].T

    def tile(columns):
        merged = dot(heads, merge_ref[:, columns], 1, 0)
        tokens_ref[:, columns] = (alive * (merged + position_ref[:, columns].astype(F32))).astype(
            BF
        )

    column_tiles(256, tile)


def aggregate(place, alive, own_field, other_field, center, scale, keys, tvt, position, merge):
    return pl.pallas_call(
        aggregate_kernel,
        out_shape=(
            shape((PATCHES, D), BF),
            shape((D, PATCHES), BF),
            shape((HEADS, VARS, PATCHES), F32),
            shape((PIECES, VARS, PATCHES), F32),
        ),
        in_specs=[SMEM, SMEM] + [VMEM] * 7 + [ANYWHERE] * 3,
        out_specs=(VMEM,) * 4,
        scratch_shapes=[
            pltpu.VMEM((D, D), BF),
            pltpu.VMEM((VARS * STRIPES, COLS), F32),
            pltpu.SemaphoreType.DMA((1, 4)),
        ],
        compiler_params=params(),
        cost_estimate=cost(),
        name="aggregate",
    )(place, alive, own_field, other_field, center, scale, keys, tvt, position, *merge)


def attend_kernel(place_ref, tokens_ref, gain_ref, bias_ref, attend_ref, *refs):
    brought = [(refs[2 * n], refs[2 * n + 1]) for n in range(3)]
    pack_ref, proj_ref, lse_ref, weight_ref, first_ref, sems = refs[6:]
    wait = section_copies(
        place_ref,
        1,
        [attend_ref.at[j] for j in range(3)],
        brought,
        [weight_ref.at[j] for j in range(3)],
        sems,
    )

    def first_norm(rows):
        xhat, _ = normalized(tokens_ref[rows, :].astype(F32))
        first_ref[rows, :] = (xhat * gain_ref[0:1, :] + bias_ref[0:1, :]).astype(BF)

    row_chunks(first_norm)
    pack_ref[:D, :] = first_ref[...].T
    for j in range(3):
        wait(j)
        column_tiles(
            256,
            lambda columns: proj_ref.__setitem__(
                (j, slice(None), columns),
                dot(first_ref[...], weight_ref[j, :, columns], 1, 0).astype(BF),
            ),
        )

    lane = lax.broadcasted_iota(jnp.int32, (PATCHES, LANES), 1)

    def pair(i, carry):
        columns = pl.ds(pl.multiple_of(i * LANES, LANES), LANES)
        queries = proj_ref[0, :, columns]
        keys = proj_ref[1, :, columns]
        values = proj_ref[2, :, columns].T
        for side in range(2):
            inside = (lane < HDIM) if side == 0 else (lane >= HDIM)
            key = jnp.where(inside, keys * HDIM ** (-0.5), jnp.zeros_like(keys)).astype(BF)
            scores = dot(key, queries, 1, 1)
            top = jnp.max(scores, axis=0, keepdims=True)
            powers = jnp.exp(scores - top)
            whole = jnp.sum(powers, axis=0, keepdims=True)
            probs = (powers * (1.0 / whole)).astype(BF)
            lse_ref[i, side : side + 1, :] = top + jnp.log(whole)
            value = values[side * HDIM : (side + 1) * HDIM]
            rows = pl.ds(pl.multiple_of(D + i * LANES + side * HDIM, HDIM), HDIM)
            pack_ref[rows, :] = dot(value, probs, 1, 0).astype(BF)
        return carry

    lax.fori_loop(0, PAIRS, pair, 0)


def attend(place, tokens, gain, bias, own_attend, brought):
    return pl.pallas_call(
        attend_kernel,
        out_shape=(
            shape((2 * D, PATCHES), BF),
            shape((3, PATCHES, D), BF),
            shape((PAIRS, 2, PATCHES), F32),
        ),
        in_specs=[SMEM] + [VMEM] * 3 + [ANYWHERE] * 7,
        out_specs=(VMEM,) * 3,
        scratch_shapes=[
            pltpu.VMEM((3, D, D), BF),
            pltpu.VMEM((PATCHES, D), BF),
            pltpu.SemaphoreType.DMA((3, 4)),
        ],
        compiler_params=params(),
        cost_estimate=cost(),
        name="attend",
    )(place, tokens, gain, bias, own_attend, *brought)


def gelu_parts(hidden):
    inverse = 1.0 / (1.0 + 0.23164190 * jnp.abs(hidden))
    decay = jnp.exp2(hidden * hidden * (-0.72134752))
    series = 0.5 * 1.061405429
    for factor in (-1.453152027, 1.421413741, -0.284496736, 0.254829592):
        series = series * inverse + 0.5 * factor
    tail = series * inverse * decay
    cdf = jnp.where(hidden >= 0.0, 1.0 - tail, tail)
    return cdf, decay * 0.3989422804014327


FF_PART = 1024
UNITS = FF + HALF


def copy(source, target, sem):
    return pltpu.make_async_copy(source, target, sem)


def aligned(index, size):
    return pl.ds(pl.multiple_of(index * size, size), size)


def start_either(choice, source, if_true, if_false, sem):
    @pl.when(choice)
    def _():
        copy(source, if_true, sem).start()

    @pl.when(jnp.logical_not(choice))
    def _():
        copy(source, if_false, sem).start()


def expand_kernel(
    place_ref,
    tokens_ref,
    out_ref,
    gain_ref,
    norm_bias_ref,
    bias_ref,
    pack_any,
    own_any,
    brought_any,
    beside_any,
    up_any,
    down_any,
    after_any,
    units_any,
    middle_any,
    second_any,
    sum_ref,
    up_ref,
    down_ref,
    tile_ref,
    merge_ref,
    context_ref,
    middle_ref,
    second_ref,
    merge_sems,
    in_sems,
    out_sems,
):
    def fetch(j):
        part = aligned(j, FF_TILE)
        return (
            copy(up_any.at[:, part], up_ref.at[:, part], in_sems.at[j, 0]),
            copy(down_any.at[part], down_ref.at[part], in_sems.at[j, 1]),
        )

    def start(j):
        for one in fetch(j):
            one.start()

    def put(j, slot):
        return copy(
            tile_ref.at[slot], units_any.at[:, :, aligned(j, FF_TILE)], out_sems.at[slot]
        )

    context = copy(pack_any.at[pl.ds(D, D)], context_ref, in_sems.at[FF_STEPS, 0])
    context.start()
    wait = section_copies(
        place_ref, 1, [own_any], [(brought_any, beside_any)], [merge_ref], merge_sems
    )
    start(0)
    context.wait()
    turned = context_ref[...].T
    wait(0)
    column_tiles(
        512,
        lambda columns: middle_ref.__setitem__(
            (slice(None), columns),
            tokens_ref[:, columns].astype(F32) + dot(turned, merge_ref[:, columns], 1, 0),
        ),
    )
    middle_out = copy(middle_ref, middle_any, in_sems.at[FF_STEPS, 1])
    middle_out.start()
    start(1)

    def second_norm(rows):
        xhat, _ = normalized(middle_ref[rows, :])
        second_ref[rows, :] = (xhat * gain_ref[1:2, :] + norm_bias_ref[1:2, :]).astype(BF)

    row_chunks(second_norm)
    second_out = copy(second_ref, second_any, out_sems.at[2])
    second_out.start()

    def step(j, carry):
        slot = lax.rem(j, 2)

        @pl.when(j + 2 < FF_STEPS)
        def _():
            start(j + 2)

        @pl.when(j >= 2)
        def _():
            put(j - 2, slot).wait()

        for one in fetch(j):
            one.wait()
        for part in range(FF_TILE // FF_PART):
            inner = slice(part * FF_PART, (part + 1) * FF_PART)
            begin = pl.multiple_of(j * FF_TILE + part * FF_PART, FF_PART)
            columns = pl.ds(begin, FF_PART)
            hidden = dot(second_ref[...], up_ref[:, columns], 1, 0) + bias_ref[:, columns]
            grad = dot(out_ref[...], down_ref[columns, :], 1, 1)
            cdf, density = gelu_parts(hidden)
            tile_ref[slot, 0, :, inner] = (hidden * cdf).astype(BF)
            low = (grad * (cdf + hidden * density)).astype(BF)
            tile_ref[slot, 1, :, inner] = low
            sum_ref[:, columns] = jnp.sum(low.astype(F32), axis=0, keepdims=True)
        put(j, slot).start()
        return carry

    lax.fori_loop(0, FF_STEPS, step, 0)
    others = aligned(1 - place_ref[1], HALF)
    put(FF_STEPS - 2, 0).wait()
    tile_ref[0, 0, :, :HALF] = out_ref[:, others]
    tile_ref[0, 1, :, :HALF] = second_ref[:, others]
    end = copy(
        tile_ref.at[0, :, :, pl.ds(0, HALF)], units_any.at[:, :, pl.ds(FF, HALF)], out_sems.at[0]
    )
    end.start()
    middle_out.wait()
    second_out.wait()
    put(FF_STEPS - 1, 1).wait()
    end.wait()


def expand(place, tokens, out_low, gain, norm_bias, pack, merge, up, bias, down, after):
    return pl.pallas_call(
        expand_kernel,
        out_shape=(
            shape((2, PATCHES, UNITS), BF),
            shape((PATCHES, D), F32),
            shape((PATCHES, D), BF),
            shape((1, FF), F32),
        ),
        in_specs=[SMEM] + [VMEM] * 5 + [ANYWHERE] * 7,
        out_specs=(ANYWHERE, ANYWHERE, ANYWHERE, VMEM),
        scratch_shapes=[
            pltpu.VMEM((D, FF), BF),
            pltpu.VMEM((FF, D), BF),
            pltpu.VMEM((2, 2, PATCHES, FF_TILE), BF),
            pltpu.VMEM((D, D), BF),
            pltpu.VMEM((D, PATCHES), BF),
            pltpu.VMEM((PATCHES, D), F32),
            pltpu.VMEM((PATCHES, D), BF),
            pltpu.SemaphoreType.DMA((1, 4)),
            pltpu.SemaphoreType.DMA((FF_STEPS + 1, 2)),
            pltpu.SemaphoreType.DMA((3,)),
        ],
        compiler_params=params(),
        cost_estimate=cost(),
        name="expand",
    )(place, tokens, out_low, gain, norm_bias, bias.reshape(1, FF), pack, *merge, up, down, after)


DEPTHS = 4
DEPTH = FF // DEPTHS


def contract_kernel(
    place_ref,
    scalars_ref,
    gain_ref,
    bias_ref,
    units_any,
    up_any,
    down_any,
    middle_any,
    cotangent_any,
    result_ref,
    grad_ref,
    branch_ref,
    gain_grad_ref,
    bias_grad_ref,
    out_grad_ref,
    units_ref,
    up_ref,
    down_ref,
    middle_ref,
    cotangent_ref,
    total_ref,
    second_ref,
    sems,
):
    def fetch(n):
        which, c = divmod(n, DEPTHS)
        part = slice(c * DEPTH, (c + 1) * DEPTH)
        if which == 0:
            weight = copy(down_any.at[part], down_ref.at[part], sems.at[n, 1])
        else:
            weight = copy(up_any.at[:, part], up_ref.at[:, part], sems.at[n, 1])
        return (
            copy(units_any.at[which, :, part], units_ref.at[which, :, part], sems.at[n, 0]),
            weight,
        )

    rest = (
        copy(middle_any, middle_ref, sems.at[2 * DEPTHS, 0]),
        copy(cotangent_any.at[place_ref[0]], cotangent_ref, sems.at[2 * DEPTHS, 1]),
    )
    for n in range(2):
        for one in fetch(n):
            one.start()
    for n in range(2 * DEPTHS):
        which, c = divmod(n, DEPTHS)
        part = slice(c * DEPTH, (c + 1) * DEPTH)
        for one in fetch(n + 2) if n + 2 < 2 * DEPTHS else rest if n + 2 == 2 * DEPTHS else ():
            one.start()
        for one in fetch(n):
            one.wait()
        ref = second_ref if which else total_ref
        if which:
            product = dot(units_ref[1, :, part], up_ref[:, part], 1, 1)
        else:
            product = dot(units_ref[0, :, part], down_ref[part, :], 1, 0)
        if c:
            ref[...] += product
        else:
            ref[...] = product
    for one in rest:
        one.wait()
    alive, hat = scalars_ref[0], scalars_ref[1]
    gain_grad_ref[...] = jnp.zeros_like(gain_grad_ref)
    bias_grad_ref[...] = jnp.zeros_like(bias_grad_ref)
    out_grad_ref[...] = jnp.zeros_like(out_grad_ref)

    def chunk(rows):
        middle = middle_ref[rows, :]
        result_ref[rows, :] = (alive * (middle + total_ref[rows, :] + bias_ref[...])).astype(BF)
        xhat, inverse = normalized(middle)
        grad = second_ref[rows, :]
        gain_grad_ref[...] += jnp.sum(grad * xhat, axis=0, keepdims=True)
        bias_grad_ref[...] += jnp.sum(grad, axis=0, keepdims=True)
        out = cotangent_ref[rows, :].astype(F32) * hat
        out_grad_ref[...] += jnp.sum(out, axis=0, keepdims=True)
        whole = out + norm_back(xhat, inverse, gain_ref[...], grad)
        grad_ref[rows, :] = whole
        branch_ref[rows, :] = whole.astype(BF)

    row_chunks(chunk)


def contract(place, scalars, units, up, down, middle, cotangent, gain, bias):
    return pl.pallas_call(
        contract_kernel,
        out_shape=(
            shape((PATCHES, D), BF),
            shape((PATCHES, D), F32),
            shape((PATCHES, D), BF),
            shape((1, D), F32),
            shape((1, D), F32),
            shape((1, D), F32),
        ),
        in_specs=[SMEM, SMEM, VMEM, VMEM] + [ANYWHERE] * 5,
        out_specs=(VMEM,) * 6,
        scratch_shapes=[
            pltpu.VMEM((2, PATCHES, FF), BF),
            pltpu.VMEM((D, FF), BF),
            pltpu.VMEM((FF, D), BF),
            pltpu.VMEM((PATCHES, D), F32),
            pltpu.VMEM((PATCHES, D), BF),
            pltpu.VMEM((PATCHES, D), F32),
            pltpu.VMEM((PATCHES, D), F32),
            pltpu.SemaphoreType.DMA((2 * DEPTHS + 1, 2)),
        ],
        compiler_params=params(),
        cost_estimate=cost(),
        name="contract",
    )(place, scalars, gain, bias, units, up, down, middle, cotangent)


def attend_back_kernel(
    place_ref,
    grad_ref,
    branch_ref,
    proj_ref,
    lse_ref,
    tokens_ref,
    gain_ref,
    attend_ref,
    merge_ref,
    *refs,
):
    brought = [(refs[2 * n], refs[2 * n + 1]) for n in range(4)]
    outs = refs[8 + TOKENS_BACK :]
    keep_ref, send_ref, token_grad_ref, gain_grad_ref, bias_grad_ref = outs[:5]
    weight_ref, context_ref, first_ref, proj_grad_ref, sems = outs[5:]
    wait = section_copies(
        place_ref,
        1,
        [merge_ref] + [attend_ref.at[j] for j in range(3)],
        brought[3:] + brought[:3],
        [weight_ref.at[j] for j in range(4)],
        sems,
    )
    wait(0)
    branch = branch_ref[...]

    def context_tile(columns):
        context_ref[:, columns] = dot(branch, weight_ref[0, columns, :], 1, 1).astype(BF)

    column_tiles(256, context_tile)
    lane = lax.broadcasted_iota(jnp.int32, (PATCHES, LANES), 1)

    def pair(i, carry):
        columns = pl.ds(pl.multiple_of(i * LANES, LANES), LANES)
        queries = proj_ref[0, :, columns]
        keys = proj_ref[1, :, columns]
        values = proj_ref[2, :, columns]
        grads = context_ref[:, columns]
        keys_turned = keys.T
        blank = jnp.zeros_like(keys)
        query_grads, key_grads, value_grads = [], [], []
        for side in range(2):
            inside = (lane < HDIM) if side == 0 else (lane >= HDIM)
            key = jnp.where(inside, keys * HDIM ** (-0.5), blank).astype(BF)
            value = jnp.where(inside, values, blank)
            probs = jnp.exp(dot(key, queries, 1, 1) - lse_ref[i, side : side + 1, :])
            share_grad = dot(value, grads, 1, 1)
            weighted = probs * share_grad
            inner = jnp.sum(weighted, axis=0, keepdims=True)
            score_low = (weighted - probs * inner).astype(BF)
            value_grads.append(dot(probs.astype(BF), grads, 1, 0))
            key_grads.append(dot(score_low, queries, 1, 0))
            query_grads.append(
                dot(keys_turned[side * HDIM : (side + 1) * HDIM], score_low, 1, 0)
            )
        low = lane < HDIM
        query_grad = jnp.concatenate(query_grads, axis=0) * HDIM ** (-0.5)
        proj_grad_ref[0, :, columns] = query_grad.T.astype(BF)
        proj_grad_ref[1, :, columns] = (
            jnp.where(low, key_grads[0], key_grads[1]) * HDIM ** (-0.5)
        ).astype(BF)
        proj_grad_ref[2, :, columns] = jnp.where(low, value_grads[0], value_grads[1]).astype(BF)
        return carry

    lax.fori_loop(0, PAIRS, pair, 0)
    core = place_ref[1]
    owns = pl.ds(pl.multiple_of(core * HALF, HALF), HALF)
    others = pl.ds(pl.multiple_of((1 - core) * HALF, HALF), HALF)
    for j in range(3):
        keep_ref[j] = proj_grad_ref[j, :, owns]
        send_ref[j] = proj_grad_ref[j, :, others]
    keep_ref[3] = branch_ref[:, owns]
    send_ref[3] = branch_ref[:, others]
    for j in range(3):
        wait(j + 1)

    def first_tile(columns):
        total = dot(proj_grad_ref[0], weight_ref[1, columns, :], 1, 1)
        for j in range(1, 3):
            total = total + dot(proj_grad_ref[j], weight_ref[j + 1, columns, :], 1, 1)
        first_ref[:, columns] = total

    column_tiles(256, first_tile)
    gain_grad_ref[...] = jnp.zeros_like(gain_grad_ref)
    bias_grad_ref[...] = jnp.zeros_like(bias_grad_ref)

    def chunk(rows):
        xhat, inverse = normalized(tokens_ref[rows, :].astype(F32))
        grad = first_ref[rows, :]
        gain_grad_ref[...] += jnp.sum(grad * xhat, axis=0, keepdims=True)
        bias_grad_ref[...] += jnp.sum(grad, axis=0, keepdims=True)
        token_grad_ref[rows, :] = (
            grad_ref[rows, :] + norm_back(xhat, inverse, gain_ref[0:1, :], grad)
        ).astype(BF)

    row_chunks(chunk)


def attend_back(
    place, grad, branch, proj, lse, tokens, gain, own_attend, own_merge, brought, after
):
    return pl.pallas_call(
        attend_back_kernel,
        out_shape=(
            shape((4, PATCHES, HALF), BF),
            shape((4, PATCHES, HALF), BF),
            shape((PATCHES, D), BF),
            shape((1, D), F32),
            shape((1, D), F32),
        ),
        in_specs=[SMEM] + [VMEM] * 6 + [ANYWHERE] * (10 + TOKENS_BACK),
        out_specs=(VMEM,) * 5,
        scratch_shapes=[
            pltpu.VMEM((4, D, D), BF),
            pltpu.VMEM((PATCHES, D), BF),
            pltpu.VMEM((PATCHES, D), F32),
            pltpu.VMEM((3, PATCHES, D), BF),
            pltpu.SemaphoreType.DMA((4, 4)),
        ],
        compiler_params=params(),
        cost_estimate=cost(),
        name="attend_back",
    )(place, grad, branch, proj, lse, tokens, gain, own_attend, own_merge, *brought, *after)


MIX_AT = PATCHES
SMALL_AT = PATCHES + TABLE_PAD
KEYS_AT = SMALL_AT + 16
TAIL = KEYS_AT + ROWS_TABLE


def aggregate_back_kernel(
    place_ref,
    alive_ref,
    token_grad_ref,
    pixels_ref,
    keys_ref,
    tvt_ref,
    shares_ref,
    gain_first_ref,
    gain_second_ref,
    bias_first_ref,
    bias_second_ref,
    output_ref,
    hidden_ref,
    own_ref,
    brought_ref,
    beside_ref,
    keep_ref,
    send_ref,
    field_ref,
    key_grad_ref,
    head_ref,
    merge_ref,
    mix_ref,
    pixel_grad_ref,
    grid_ref,
    sems,
):
    wait = section_copies(
        place_ref, 0, [own_ref], [(brought_ref, beside_ref)], [merge_ref], sems
    )
    core = place_ref[1]
    owns = pl.ds(pl.multiple_of(core * HALF, HALF), HALF)
    others = pl.ds(pl.multiple_of((1 - core) * HALF, HALF), HALF)
    alive = alive_ref[0]
    pre = (token_grad_ref[...].astype(F32) * alive).astype(BF)
    keep_ref[:PATCHES, :] = (token_grad_ref[:, owns].astype(F32) * alive).astype(BF)
    send_ref[:PATCHES, :] = (token_grad_ref[:, others].astype(F32) * alive).astype(BF)
    wait(0)

    def head_tile(rows):
        head_ref[rows, :] = dot(merge_ref[rows, :], pre, 1, 1).astype(BF)

    column_tiles(256, head_tile)
    pixel_grad_ref[...] = jnp.zeros_like(pixel_grad_ref)
    key_grad_ref[...] = jnp.zeros_like(key_grad_ref)
    lane = lax.broadcasted_iota(jnp.int32, (VARS, HEADS), 1)

    def head(h, carry):
        rows = pl.ds(pl.multiple_of(h * HDIM, HDIM), HDIM)
        keys = head_keys(keys_ref, h)
        grads = head_ref[rows, :]
        shares = shares_ref[h]
        mix_ref[rows, :] = dot(grads, mixed_rows(shares, pixels_ref), 1, 1)
        row_grads = dot(tvt_ref[rows, :], grads, 0, 0)
        share_grads = row_grads[PIECES * VARS : ROWS_TABLE]
        for k in range(PIECES):
            share_grads = share_grads + row_grads[k * VARS : (k + 1) * VARS] * pixels_ref[k]
        inner = jnp.sum(shares * share_grads, axis=0, keepdims=True)
        scores = shares * (share_grads - inner)
        for k in range(PIECES + 1):
            piece = slice(k * VARS, (k + 1) * VARS)
            if k < PIECES:
                pixel_grad_ref[k] += shares * row_grads[piece] + scores * keys[piece]
                total = jnp.sum(scores * pixels_ref[k], axis=1, keepdims=True)
            else:
                total = jnp.sum(scores, axis=1, keepdims=True)
            key_grad_ref[piece, :] += jnp.where(lane == h, total, 0.0)
        return carry

    lax.fori_loop(0, HEADS, head, 0)
    for ref, start in ((keep_ref, core * HALF), (send_ref, (1 - core) * HALF)):
        for part in range(2):
            rows = pl.ds(pl.multiple_of(start + part * TABLE_PAD, TABLE_PAD), TABLE_PAD)
            ref[MIX_AT:SMALL_AT, part * TABLE_PAD : (part + 1) * TABLE_PAD] = mix_ref[
                rows, :
            ].astype(BF)
        columns = pl.ds(pl.multiple_of(start, HALF), HALF)
        small = [
            one[:, columns]
            for one in (
                gain_first_ref,
                gain_second_ref,
                bias_first_ref,
                bias_second_ref,
                output_ref,
            )
        ]
        for part in range(FF // D):
            small.append(hidden_ref[:, pl.ds(pl.multiple_of(part * D + start, HALF), HALF)])
        small.append(jnp.zeros((16 - len(small), HALF), F32))
        ref[SMALL_AT:KEYS_AT, :] = jnp.concatenate(small, axis=0).astype(BF)
        ref[KEYS_AT:, :] = jnp.concatenate(
            [key_grad_ref[...], jnp.zeros((ROWS_TABLE, HALF - HEADS), F32)], axis=1
        ).astype(BF)
    low_lane = lax.broadcasted_iota(jnp.int32, (VARS, COLS), 1) < COLS // 2
    for a in range(PATCH):
        for j in range(PATCHES // COLS):
            columns = slice(j * COLS, (j + 1) * COLS)
            low, high = pixel_grad_ref[2 * a, :, columns], pixel_grad_ref[2 * a + 1, :, columns]
            even = jnp.where(low_lane, low, pltpu.roll(high, COLS // 2, 1))
            odd = jnp.where(low_lane, pltpu.roll(low, COLS // 2, 1), high)
            grid_ref[pl.ds(4 * j + a, VARS, stride=STRIPES), :] = even
            grid_ref[pl.ds(4 * j + 2 + a, VARS, stride=STRIPES), :] = odd
    field_ref[...] = exact(grid_ref[...], column_order(), 1)


def aggregate_back(place, alive, token_grad, pixels, keys, tvt, shares, small, merge):
    return pl.pallas_call(
        aggregate_back_kernel,
        out_shape=(
            shape((TAIL, HALF), BF),
            shape((TAIL, HALF), BF),
            shape((VARS * STRIPES, COLS), F32),
        ),
        in_specs=[SMEM, SMEM] + [VMEM] * 11 + [ANYWHERE] * 3,
        out_specs=(VMEM,) * 3,
        scratch_shapes=[
            pltpu.VMEM((ROWS_TABLE, HEADS), F32),
            pltpu.VMEM((D, PATCHES), BF),
            pltpu.VMEM((D, D), BF),
            pltpu.VMEM((D, TABLE_PAD), F32),
            pltpu.VMEM((PIECES, VARS, PATCHES), F32),
            pltpu.VMEM((VARS * STRIPES, COLS), F32),
            pltpu.SemaphoreType.DMA((1, 4)),
        ],
        compiler_params=params(),
        cost_estimate=cost(),
        name="aggregate_back",
    )(place, alive, token_grad, pixels, keys, tvt, shares, *small, *merge)


BLOCKS = 16
BLOCK = FF // BLOCKS
SPANS = BLOCKS // 2
SPAN = 4 * BLOCK


def wide_kernel(which, by_pipe, place_ref, left_any, own_any, beside_any, *refs):
    send_any, keep_any, left_ref, turned_ref, right_ref, product_ref, sems, out_sems = refs[-8:]
    place, core = place_ref[0], place_ref[1]
    side, z_low = jnp.bitwise_and(place, 1), jnp.bitwise_and(lax.shift_right_logical(place, 1), 1)

    def fetch(i):
        columns = aligned(jnp.bitwise_xor(3 - i, lax.shift_right_logical(place, 2)), SPAN)
        return [
            copy(
                source.at[which, :, columns],
                right_ref.at[i, pl.ds(n * PATCHES, PATCHES)],
                sems.at[i, n],
            )
            for n, source in enumerate((own_any, beside_any))
        ]

    lefts = (
        copy(left_any.at[:, aligned(core, HALF)], left_ref.at[0], sems.at[4, 0]),
        copy(beside_any.at[which, :, pl.ds(FF, HALF)], left_ref.at[1], sems.at[4, 1]),
    )
    for one in lefts:
        one.start()
    for i in range(2):
        for one in fetch(i):
            one.start()
    for n, one in enumerate(lefts):
        one.wait()
        turned_ref[:, n * PATCHES : (n + 1) * PATCHES] = left_ref[n].T

    def put(i, block):
        source = product_ref.at[i % 2, :, pl.ds(block * BLOCK, BLOCK)]
        return source, out_sems.at[i % 2, block]

    def wait(i):
        for block in range(4):
            source, sem = put(i, block)
            copy(source, send_any.at[0, 0, 0], sem).wait()

    for i in range(4):
        for one in fetch(i + 2) if i < 2 else ():
            one.start()
        for one in fetch(i):
            one.wait()
        if i >= 2:
            wait(i - 2)
        product_ref[i % 2] = dot(turned_ref[...], right_ref[i], 1, 0).astype(BF)
        pipe, z_high = divmod(3 - i, 2)
        for block in range(4):
            source, sem = put(i, block)
            to_side = jnp.bitwise_xor(block % 2, side)
            to_z = jnp.bitwise_xor(block // 2, z_low)
            if by_pipe:
                target = send_any if pipe else keep_any
                copy(source, target.at[to_side, z_high, to_z], sem).start()
            else:
                start_either(
                    to_side == 1,
                    source,
                    send_any.at[pipe, z_high, to_z],
                    keep_any.at[pipe, z_high, to_z],
                    sem,
                )
    wait(2)
    wait(3)


def wide_grads(place, left, right, which, by_pipe, after, name):
    return pl.pallas_call(
        functools.partial(wide_kernel, which, by_pipe),
        in_specs=[SMEM] + [ANYWHERE] * (3 + len(after)),
        out_specs=(ANYWHERE, ANYWHERE),
        out_shape=(shape((2, 2, 2, HALF, BLOCK), BF), shape((2, 2, 2, HALF, BLOCK), BF)),
        scratch_shapes=[
            pltpu.VMEM((2, PATCHES, HALF), BF),
            pltpu.VMEM((HALF, 2 * PATCHES), BF),
            pltpu.VMEM((4, 2 * PATCHES, SPAN), BF),
            pltpu.VMEM((2, HALF, SPAN), BF),
            pltpu.SemaphoreType.DMA((5, 2)),
            pltpu.SemaphoreType.DMA((2, 4)),
        ],
        compiler_params=params(),
        cost_estimate=cost(),
        name=name,
    )(place, left, *right, *after)


ROWS = D // SPANS
PARTS = 4 * ROWS
CROSS = ROWS


def square_kernel(
    place_ref,
    tail_own,
    tail_beside,
    heads_own,
    heads_beside,
    pack_own,
    pack_beside,
    right_own,
    right_beside,
    *refs,
):
    send_any, keep_any, cross_send_any, cross_keep_any = refs[-9:-5]
    left_ref, right_ref, product_ref, sems, out_sems = refs[-5:]
    pipe, place = place_ref[0], place_ref[1]
    side, z = jnp.bitwise_and(place, 1), lax.shift_right_logical(place, 1)
    lefts = [
        (pack_own.at[pl.ds(0, D)], pack_beside.at[pl.ds(0, D)]),
        (pack_own.at[pl.ds(D, D)], pack_beside.at[pl.ds(D, D)]),
        (heads_own, heads_beside),
    ]
    left_copies = [
        [
            copy(one, left_ref.at[n, :, pl.ds(m * PATCHES, PATCHES)], sems.at[n, m])
            for m, one in enumerate(pair)
        ]
        for n, pair in enumerate(lefts)
    ]
    right_copies = [
        [
            copy(one.at[n], right_ref.at[n, pl.ds(m * PATCHES, PATCHES)], sems.at[3 + n, m])
            for m, one in enumerate((right_own, right_beside))
        ]
        for n in range(4)
    ]
    for n in (0, 3, 1, 2):
        for one in (left_copies[n] if n < 3 else []) + right_copies[n]:
            one.start()
    right_ref[4, :PATCHES] = tail_own[:PATCHES]
    right_ref[4, PATCHES:] = tail_beside[:PATCHES]

    def put(slot, block):
        return product_ref.at[slot, pl.ds(block * ROWS, ROWS)], out_sems.at[slot, block]

    def wait(slot):
        for block in range(SPANS):
            source, sem = put(slot, block)
            copy(source, send_any.at[0, pl.ds(0, ROWS)], sem).wait()

    def share(slot, part):
        rows = pl.ds(part * ROWS, ROWS)
        for block in range(SPANS):
            source, sem = put(slot, block)
            to_z = jnp.bitwise_xor(block // 2, z)
            start_either(
                side != block % 2, source, send_any.at[to_z, rows], keep_any.at[to_z, rows], sem
            )

    def cross(slot, part, goal):
        rows = pl.ds(part * ROWS, ROWS)
        for block in range(SPANS):
            source, sem = put(slot, block)
            to_side = jnp.bitwise_xor(block % 2, side)
            to_z = jnp.bitwise_xor(block // 2, z)
            start_either(
                pipe != goal,
                source,
                cross_send_any.at[to_side, to_z, rows],
                cross_keep_any.at[to_side, to_z, rows],
                sem,
            )

    product_ref[0] = (tail_own[...].astype(F32) + tail_beside[...].astype(F32)).astype(BF)
    share(0, 1)
    for step, (left, right) in enumerate(((0, 0), (1, 3), (2, 4), (0, 1), (0, 2))):
        slot = (step + 1) % 2
        if step in (0, 1, 2):
            for one in left_copies[left]:
                one.wait()
        if right < 4:
            for one in right_copies[right]:
                one.wait()
        if step >= 1:
            wait(slot)
        for tile in range(2):
            rows = slice(tile * HALF, (tile + 1) * HALF)
            product_ref[slot, rows] = dot(left_ref[left, rows], right_ref[right], 1, 0).astype(BF)
        if step < 3:
            share(slot, (0, 3, 2)[step])
        else:
            cross(slot, 0, step - 3)
    wait(0)
    wait(1)


def square_grads(place, tail, heads, pack, right, after):
    return pl.pallas_call(
        square_kernel,
        in_specs=[SMEM, VMEM, VMEM] + [ANYWHERE] * (6 + len(after)),
        out_specs=(ANYWHERE,) * 4,
        out_shape=(
            shape((4, PARTS, HALF), BF),
            shape((4, PARTS, HALF), BF),
            shape((2, 4, CROSS, HALF), BF),
            shape((2, 4, CROSS, HALF), BF),
        ),
        scratch_shapes=[
            pltpu.VMEM((3, D, 2 * PATCHES), BF),
            pltpu.VMEM((5, 2 * PATCHES, HALF), BF),
            pltpu.VMEM((2, D, HALF), BF),
            pltpu.SemaphoreType.DMA((7, 2)),
            pltpu.SemaphoreType.DMA((2, SPANS)),
        ],
        compiler_params=params(),
        cost_estimate=cost(),
        name="square_grads",
    )(place, *tail, *heads, *pack, *right, *after)


def first_sums_kernel(down_keep, down_came, up_keep, up_came, after_any, down_ref, up_ref):
    for z in range(4):
        at = (0, z // 2, z % 2)
        down_ref[z] = (down_keep[at].astype(F32) + down_came[at].astype(F32)).astype(BF)
        up_ref[z] = (up_keep[at].astype(F32) + up_came[at].astype(F32)).astype(BF)


def first_sums(down_keep, down_came, up_keep, up_came, after):
    half = pl.BlockSpec((1, 2, 2, HALF, BLOCK), lambda i: (1, 0, 0, 0, 0))
    return pl.pallas_call(
        first_sums_kernel,
        grid=(1,),
        in_specs=[half] * 4 + [ANYWHERE],
        out_specs=(VMEM, VMEM),
        out_shape=(shape((4, HALF, BLOCK), BF), shape((4, HALF, BLOCK), BF)),
        compiler_params=params(1),
        cost_estimate=cost(),
        name="first_sums",
    )(down_keep, down_came, up_keep, up_came, after)


def second_sums_kernel(
    down_keep, down_came, down_brought, up_keep, up_came, up_brought, after_any, *outs
):
    def added(keep, came, brought, z):
        at = (0, z // 2, z % 2)
        one = (keep[at].astype(F32) + came[at].astype(F32)).astype(BF).astype(F32)
        return (one + brought[z].astype(F32)).astype(BF)

    for z in range(4):
        outs[z][0] = added(down_keep, down_came, down_brought, z)
        outs[z][1] = added(up_keep, up_came, up_brought, z)


def second_sums(down_keep, down_came, down_brought, up_keep, up_came, up_brought, after):
    half = pl.BlockSpec((1, 2, 2, HALF, BLOCK), lambda i: (0, 0, 0, 0, 0))
    return pl.pallas_call(
        second_sums_kernel,
        grid=(1,),
        in_specs=[half, half, VMEM] * 2 + [ANYWHERE],
        out_specs=(VMEM,) * 4,
        out_shape=(shape((2, HALF, BLOCK), BF),) * 4,
        compiler_params=params(1),
        cost_estimate=cost(),
        name="second_sums",
    )(down_keep, down_came, down_brought, up_keep, up_came, up_brought, after)


def third_sums_kernel(keep, came, out_ref):
    for z in range(4):
        out_ref[z] = (keep[0, z].astype(F32) + came[0, z].astype(F32)).astype(BF)


def third_sums(keep, came):
    half = pl.BlockSpec((1, 4, CROSS, HALF), lambda i: (1, 0, 0, 0))
    return pl.pallas_call(
        third_sums_kernel,
        grid=(1,),
        in_specs=[half, half],
        out_specs=VMEM,
        out_shape=shape((4, CROSS, HALF), BF),
        compiler_params=params(1),
        cost_estimate=cost(),
        name="third_sums",
    )(keep, came)


def fourth_sums_kernel(keep, came, cross_keep, cross_came, brought, *refs):
    for z in range(4):
        out_ref = refs[len(refs) - 4 + z]
        out_ref[:PARTS] = (keep[z].astype(F32) + came[z].astype(F32)).astype(BF)
        one = (cross_keep[0, z].astype(F32) + cross_came[0, z].astype(F32)).astype(BF)
        out_ref[PARTS:] = (one.astype(F32) + brought[z].astype(F32)).astype(BF)


def fourth_sums(keep, came, cross_keep, cross_came, brought, after):
    half = pl.BlockSpec((1, 4, CROSS, HALF), lambda i: (0, 0, 0, 0))
    return pl.pallas_call(
        fourth_sums_kernel,
        grid=(1,),
        in_specs=[VMEM, VMEM, half, half, VMEM] + [ANYWHERE] * len(after),
        out_specs=(VMEM,) * 4,
        out_shape=(shape((PARTS + CROSS, HALF), BF),) * 4,
        compiler_params=params(1),
        cost_estimate=cost(),
        name="fourth_sums",
    )(keep, came, cross_keep, cross_came, brought, *after)


def finish_kernel(
    chips,
    place_ref,
    tail_ref,
    table_ref,
    query_ref,
    given_ref,
    value_ref,
    attend_ref,
    *refs,
):
    brought = [(refs[2 * n], refs[2 * n + 1]) for n in range(3)]
    position_ref, gain_ref, bias_ref, output_ref, hidden_ref = refs[6:11]
    embed_ref, variable_ref, attend_grad_ref, query_grad_ref = refs[11:15]
    weight_ref, whole_ref, mix_ref, rows_ref, turned_ref, sems = refs[15:]
    core, chip, spot = place_ref[1], place_ref[3], place_ref[4]
    wait = section_copies(
        place_ref,
        0,
        [attend_ref.at[j] for j in range(3)],
        brought,
        [weight_ref.at[j] for j in range(3)],
        sems,
    )
    part = TAIL // chips
    for c in range(2):
        for n in range(chips):
            whole_ref[c, n * part : (n + 1) * part, :] = tail_ref[
                jnp.bitwise_xor(c, core), jnp.bitwise_xor(n, chip)
            ].astype(F32)
    for c in range(2):
        columns = slice(c * HALF, (c + 1) * HALF)
        position_ref[:, columns] = whole_ref[c, :PATCHES, :]
        small = whole_ref[c, SMALL_AT:KEYS_AT, :]
        gain_ref[:, columns] = small[0:2]
        bias_ref[:, columns] = small[2:4]
        output_ref[:, columns] = small[4:5]
        hidden_ref[:, columns] = small[5:9]
        for n in range(2):
            start = c * HALF + n * TABLE_PAD
            mix_ref[start : start + TABLE_PAD, :] = whole_ref[
                c, MIX_AT:SMALL_AT, n * TABLE_PAD : (n + 1) * TABLE_PAD
            ].astype(BF)
    keys = whole_ref[0, KEYS_AT:, :HEADS]
    table = table_ref[...].astype(F32)
    grads = lax.dot_general(
        keys,
        table,
        (((0,), (0,)), ((), ())),
        precision=PRECISE,
        preferred_element_type=F32,
    ).astype(BF)
    mask = head_rows(D)
    wait(1)
    low = jnp.where(mask, dot(grads, weight_ref[1], 1, 0), 0.0)
    low = jnp.sum(low, axis=0, keepdims=True) * HDIM ** (-0.5)
    low = jnp.broadcast_to(low, (HEADS, D)).astype(BF)
    wait(0)
    query_grad_ref[...] = dot(low, weight_ref[0], 1, 1)[:1]
    mixed = mix_ref[...]
    wait(2)
    key_query = value_ref[...].astype(F32)[:, ROWS_TABLE:]
    table_grad = dot(mixed, weight_ref[2], 0, 1)[:ROWS_TABLE] + lax.dot_general(
        keys,
        key_query,
        (((1,), (1,)), ((), ())),
        precision=PRECISE,
        preferred_element_type=F32,
    )
    for k in range(PIECES):
        embed_ref[:, k, :] = table_grad[k * VARS : (k + 1) * VARS]
    variable_ref[...] = table_grad[PIECES * VARS :]
    size = attend_grad_ref.shape[1]
    rows = pl.ds(pl.multiple_of(spot * size, size), size)
    rows_ref[...] = jnp.concatenate([grads.astype(F32), given_ref[...]], axis=0).T
    turned_ref[...] = table.T
    own = rows_ref[rows, :]
    low = low.astype(F32)
    spread = jnp.where(mask, query_ref[...] * HDIM ** (-0.5), 0.0)
    attend_grad_ref[0] = own[:, HEADS : HEADS + 1] * low[:1]
    attend_grad_ref[1] = lax.dot_general(
        own[:, :HEADS],
        spread,
        (((1,), (0,)), ((), ())),
        precision=PRECISE,
        preferred_element_type=F32,
    )
    left = jnp.concatenate(
        [turned_ref[rows, :], jnp.zeros((size, TABLE_PAD - ROWS_TABLE), F32)], axis=1
    ).astype(BF)
    attend_grad_ref[2] = dot(left, mixed, 1, 1)


def finish(place, tail, table, query, given, value, weights, brought, chips, size):
    return pl.pallas_call(
        functools.partial(finish_kernel, chips),
        out_shape=(
            shape((PATCHES, D), F32),
            shape((2, D), F32),
            shape((2, D), F32),
            shape((1, D), F32),
            shape((FF // D, D), F32),
            shape((VARS, PIECES, D), F32),
            shape((VARS, D), F32),
            shape((3, size, D), F32),
            shape((1, D), F32),
        ),
        in_specs=[SMEM] + [VMEM] * 5 + [ANYWHERE] * 7,
        out_specs=(VMEM,) * 9,
        scratch_shapes=[
            pltpu.VMEM((3, D, D), BF),
            pltpu.VMEM((2, TAIL, HALF), F32),
            pltpu.VMEM((D, TABLE_PAD), BF),
            pltpu.VMEM((D, 2 * HEADS), F32),
            pltpu.VMEM((D, ROWS_TABLE), F32),
            pltpu.SemaphoreType.DMA((3, 4)),
        ],
        compiler_params=params(),
        cost_estimate=cost(),
        name="finish",
    )(place, tail, table, query, given, value, weights, *brought)


def partner(block, axis, distance):
    size = lax.axis_size(axis)
    return lax.ppermute(block, axis, [(i, i ^ distance) for i in range(size)])


def swap(block):
    return partner(block, "pipe", 1)


def pick(array, index, axis=0):
    return lax.dynamic_index_in_dim(array, index, axis, keepdims=False)


def tree_sum(terms):
    while len(terms) > 1:
        terms = [terms[2 * i] + terms[2 * i + 1] for i in range(len(terms) // 2)]
    return terms[0]


class Places:
    def __init__(self):
        self.pipe = lax.axis_index("pipe")
        self.dp = lax.axis_index("dp")
        self.size = lax.axis_size("dp")
        self.core = self.dp % 2
        self.chips = self.size // 2
        bits = self.size.bit_length() - 2
        low = bits % 2 if bits % 2 else 2
        self.groups = []
        at = 1
        while bits > 0:
            width = low if at == 1 else 2
            self.groups.append((at, width))
            at += width
            bits -= width

    def relative(self, array, place):
        for bit in range(array.shape[0].bit_length() - 1):
            paired = array.reshape(-1, 2, 2**bit, *array.shape[1:])
            flipped = jnp.where((place // 2**bit) % 2 == 1, paired[:, ::-1], paired)
            array = flipped.reshape(array.shape)
        return array

    def grouped(self, array):
        counts = [2**width for _, width in reversed(self.groups)]
        dims = array.shape[1:]
        array = array.reshape(*counts, *dims)
        order = list(range(len(counts)))[::-1] + list(range(len(counts), array.ndim))
        return array.transpose(order)

    def reduced(self, array, groups):
        for n, (at, width) in enumerate(groups):
            terms = [array[0].astype(F32)]
            for distance in range(1, 2**width):
                terms.append(partner(array[distance], "dp", distance * 2**at).astype(F32))
            array = tree_sum(terms)
            if n < len(groups) - 1:
                array = array.astype(BF)
        return array

    def over_cores(self, array):
        brought = partner(pick(array, 1 - self.core).astype(BF), "dp", 1).astype(F32)
        own = pick(array, self.core)
        return jnp.concatenate(
            [jnp.where(self.core == 0, own, brought), jnp.where(self.core == 0, brought, own)],
            axis=-1,
        )

    def last(self, parts, group):
        terms = [parts[0].astype(F32)]
        for distance in range(1, 2 ** group[1]):
            terms.append(partner(parts[distance], "dp", distance * 2 ** group[0]).astype(F32))
        return tree_sum(terms)

    def gather(self, block):
        blocks = block[None]
        for at, width in reversed(self.groups):
            parts = [partner(blocks, "dp", m * 2**at) for m in range(1, 2**width)]
            blocks = jnp.stack([blocks] + parts, axis=1).reshape(-1, *block.shape)
        return blocks

    def round(self, block, bit):
        return block + partner(block, "dp", 2**bit)


def on_device(
    fields,
    item_weights,
    live_counts,
    running_stats,
    embed_weight,
    variable_embed,
    variable_query,
    attend_weight,
    merge_weight,
    position_embed,
    norm_gain,
    norm_bias,
    up_weight,
    hidden_bias,
    down_weight,
    output_bias,
    cotangent,
):
    at = Places()
    pipe, core = at.pipe, at.core
    first = pipe == 0
    side = (at.dp // 2) % 2
    chip = at.dp // 2
    place = jnp.stack([pipe, core, side]).astype(jnp.int32)
    micro, half_vars, rows, cols = fields.shape
    scale_heads = HDIM ** (-0.5)

    own_attend, own_merge = attend_weight[0], merge_weight[0]

    def quarter(weight):
        return lax.dynamic_slice_in_dim(weight, (2 * core + side) * QUARTER, QUARTER, 0)

    def quarter_of(j):
        start = (jnp.int32(j), (2 * core + side) * QUARTER, jnp.int32(0))
        return lax.dynamic_slice(own_attend, start, (1, QUARTER, D))[0]

    def after(value, *others):
        return lax.optimization_barrier((value, others))[0]

    def passed_on(block, before, behind):
        other = partner(after(block, *before), "dp", 2)
        pair = jnp.stack([block, after(other, *behind)])
        return pair, partner(pair, "dp", 1)

    chunk_first = swap(jnp.where(first, quarter(own_merge), quarter_of(0)))

    table = jnp.concatenate(
        [embed_weight.transpose(1, 0, 2).reshape(VARS * PIECES, D), variable_embed], axis=0
    )
    given = variable_query.astype(F32).reshape(1, D)
    query, table_keys, table_value = tables(given, table, own_attend)

    def from_first(block):
        return jnp.where(first, block, lax.ppermute(block, "pipe", [(0, 1)]))

    keys = from_first(table_keys)
    tvt = from_first(table_value.astype(BF))

    flat_fields = fields.reshape(micro, half_vars * rows, cols)
    other_fields = swap(pick(flat_fields, 1 - pipe))
    own_fields = pick(flat_fields, pipe)
    slots = jnp.arange(micro, dtype=jnp.int32)
    alive = (slots < live_counts[0]).astype(F32)
    omega = item_weights.astype(F32) * alive
    plain_sums = jnp.sum(fields, axis=(2, 3))
    square_sums = jnp.sum(fields * fields, axis=(2, 3))
    sums = jnp.concatenate(
        [
            jnp.sum(omega[:, None] * plain_sums, axis=0),
            jnp.sum(omega[:, None] * square_sums, axis=0),
            jnp.sum(omega)[None],
            jnp.sum(alive)[None],
        ]
    )
    sums = sums_y = at.round(after(sums, table_value), 1)
    for bit in range(2, at.size.bit_length() - 1):
        sums = at.round(sums, bit)
    second = swap(after(jnp.where(first, quarter_of(2), quarter_of(1)), chunk_first))
    sums = at.round(after(sums, second), 0)
    total, live_total = sums[2 * half_vars], sums[2 * half_vars + 1]
    first_moment = sums[:half_vars] / (total * rows * cols)
    second_moment = sums[half_vars : 2 * half_vars] / (total * rows * cols)
    center_new = (1.0 - MOMENTUM) * running_stats[0] + MOMENTUM * first_moment
    spread_new = (1.0 - MOMENTUM) * running_stats[1] + MOMENTUM * (
        second_moment - first_moment * first_moment
    )
    statistics = jnp.stack([center_new, spread_new])
    other_statistics = swap(statistics)
    all_statistics = jnp.concatenate(
        [
            jnp.where(first, statistics, other_statistics),
            jnp.where(first, other_statistics, statistics),
        ],
        axis=1,
    )
    center = all_statistics[0].reshape(VARS, 1)
    scale = lax.rsqrt(all_statistics[1] + EPSILON).reshape(VARS, 1)
    weight_hat = pick(omega, pipe) * live_total / total
    alive_own = pick(alive, pipe)[None]
    out_low = (pick(cotangent, pipe).astype(F32) * weight_hat).astype(BF)

    passed = [passed_on(chunk_first, (sums_y,), ())]
    passed.append(passed_on(second, (), ()))
    third = swap(after(jnp.where(first, quarter_of(0), quarter_of(2)), second))
    fourth = swap(
        after(jnp.where(first, quarter_of(1), quarter(own_merge)), third, passed[0][0])
    )
    alive_own = after(alive_own, third)

    tokens, heads, shares, pixels = aggregate(
        place,
        alive_own,
        own_fields,
        other_fields,
        center,
        scale,
        keys,
        tvt,
        position_embed,
        (own_merge, *passed[0]),
    )
    passed.append(passed_on(third, (), (tokens,)))
    heads_beside = partner(heads, "dp", 1)
    brought = [block for pair in passed for block in pair]
    pack, proj, lse = attend(place, tokens, norm_gain, norm_bias, own_attend, brought)
    passed.append(passed_on(fourth, (tokens,), (lse,)))
    brought = [block for pair in passed for block in pair]
    pack_beside = partner(pack, "dp", 1)
    units, middle, second_low, hidden_sum = expand(
        place,
        tokens,
        out_low,
        norm_gain,
        norm_bias,
        pack,
        (own_merge, *brought[6:]),
        up_weight,
        hidden_bias,
        down_weight,
        heads_beside,
    )
    units_beside = partner(units, "dp", 1)
    scalars = jnp.stack([alive_own[0], weight_hat])
    result, middle_grad, branch_low, gain_second, bias_second, output_sum = contract(
        place,
        scalars,
        units,
        up_weight,
        down_weight,
        middle,
        cotangent,
        norm_gain[1:2],
        output_bias.reshape(1, D),
    )
    ff_width = FF // (2 * at.size)
    d_width = D // at.size
    direct = 2 * at.chips == BLOCKS
    wide_place = jnp.stack([pipe * SPANS + chip if direct else 0 * chip, core]).astype(jnp.int32)
    square_place = jnp.stack([pipe, chip if direct else 0 * chip]).astype(jnp.int32)
    both_units = (units, units_beside)
    down_send, down_keep = wide_grads(
        wide_place,
        out_low,
        both_units,
        0,
        True,
        (branch_low,),
        "down_grads",
    )
    up_send, up_keep = wide_grads(
        wide_place,
        second_low,
        both_units,
        1,
        False,
        (down_keep,),
        "up_grads",
    )
    right_own, right_send, token_grad, gain_first, bias_first = attend_back(
        place,
        middle_grad,
        branch_low,
        proj,
        lse,
        tokens,
        norm_gain,
        own_attend,
        own_merge,
        brought,
        (down_keep, up_keep),
    )
    right_beside = partner(right_send, "dp", 1)
    tail_own, tail_send, field_grads = aggregate_back(
        place,
        alive_own,
        token_grad,
        pixels,
        keys,
        tvt,
        shares,
        (gain_first, gain_second, bias_first, bias_second, output_sum, hidden_sum),
        (own_merge, *passed[0]),
    )
    tail_beside = partner(tail_send, "dp", 1)

    if direct:
        groups = at.groups[1:]
        down_came, up_came = swap(down_send), partner(up_send, "dp", 2)
        down_next, up_next = first_sums(down_keep, down_came, up_keep, up_came, tail_own)
        down_brought = partner(down_next, "dp", 2)
        up_brought = swap(up_next)
        started = (down_next, up_next)
    else:
        groups = at.groups
        started = (down_keep, up_keep)

        def spread(array):
            array = array.transpose(4, 0, 1, 2, 3, 5).reshape(HALF, 2 * at.chips, -1)
            array = at.relative(array.transpose(1, 0, 2), pipe * at.chips + chip)
            array = array.reshape(2, at.chips, HALF, -1)
            total = array[0].astype(F32) + swap(array[1]).astype(F32)
            return at.grouped(total.astype(BF))

        down_wide = jnp.stack([down_keep, down_send]).transpose(0, 2, 3, 1, 4, 5)
        wide = [spread(down_wide), spread(jnp.stack([up_keep, up_send], axis=3))]

    send, keep, cross_send, cross_keep = square_grads(
        square_place,
        (tail_own, tail_beside),
        (heads, heads_beside),
        (pack, pack_beside),
        (right_own, right_beside),
        started,
    )
    if direct:
        wide = second_sums(
            down_keep, down_came, down_brought, up_keep, up_came, up_brought, send
        )
        shared = partner(after(send, wide), "dp", 2)
        crossed = swap(after(cross_send, wide))
        wide = at.last(wide, groups[0])
        cross_next = third_sums(cross_keep, crossed)
        cross_brought = partner(cross_next, "dp", 2)
        field_grads, result = after((field_grads, result), cross_next)
        came = swap(jnp.where(first, result, tokens))
        field_halves = field_grads.reshape(2, half_vars, rows, cols)
        field_came = swap(pick(field_halves, 1 - pipe).astype(BF)).astype(F32)
        square = fourth_sums(
            keep, shared, cross_keep, crossed, cross_brought, (came, field_came, wide)
        )
        square = at.last(square, groups[0])
    else:
        wide = jnp.stack([at.reduced(array, groups) for array in wide])

        def rows_of(array):
            return at.relative(array.reshape(at.chips, -1, HALF), chip)

        whole = jnp.stack([keep, send], axis=1).reshape(SPANS, PARTS, HALF)
        cross = (cross_keep.astype(F32) + swap(cross_send).astype(F32)).astype(BF)
        cross = cross.transpose(1, 0, 2, 3).reshape(SPANS, CROSS, HALF)
        square = [rows_of(whole[:, n * ROWS : (n + 1) * ROWS]) for n in range(4)]
        square.append(rows_of(cross))
        square = at.reduced(at.grouped(jnp.concatenate(square, axis=1)), groups)
        came = swap(jnp.where(first, result, tokens))
        field_halves = field_grads.reshape(2, half_vars, rows, cols)
        field_came = swap(pick(field_halves, 1 - pipe).astype(BF)).astype(F32)

    wide = wide.reshape(2, HALF, 2, ff_width)
    other = partner(pick(wide, 1 - core, 2).astype(BF), "dp", 1).astype(F32)
    own = pick(wide, core, 2)
    wide = jnp.concatenate(
        [jnp.where(core == 0, own, other), jnp.where(core == 0, other, own)], axis=1
    )
    down_part, up_part = wide[0].T, wide[1]

    lot = 2 * d_width
    part = TAIL // at.chips
    query_part = square[:lot]
    tail = square[lot : lot + part]
    merge_one = square[lot + part : 2 * lot + part]
    merge_two = square[2 * lot + part : 3 * lot + part]
    cross = square[3 * lot + part :]
    tail_came = swap(tail.astype(BF)).astype(F32)
    sent = jnp.concatenate(
        [jnp.where(first, merge_two, merge_one), query_part, cross], axis=0
    ).astype(BF)
    section_came = swap(sent).astype(F32)
    section_sum = jnp.stack(
        [
            jnp.where(first, merge_one, merge_two) + section_came[:lot],
            query_part + section_came[lot : 2 * lot],
            section_came[2 * lot :],
            cross,
        ]
    )
    tail = (tail.astype(BF).astype(F32) + tail_came).astype(BF)
    section_sum = section_sum.reshape(4, 2, d_width, HALF).transpose(1, 0, 2, 3)
    section_part = at.over_cores(section_sum)
    merge_part = section_part[0]
    second_attend = section_part[1:]

    tail = at.gather(tail)
    tail = jnp.stack([tail, partner(tail, "dp", 1)])
    spot = jnp.stack([pipe, core, side, chip, at.dp]).astype(jnp.int32)
    (
        position_sum,
        gain_sum,
        bias_sum,
        output_sum,
        hidden_sum,
        embed_grads,
        variable_grads,
        first_attend,
        query_sum,
    ) = finish(
        spot,
        tail,
        table,
        query,
        jnp.broadcast_to(given, (HEADS, D)),
        tvt,
        own_attend,
        [*passed[2], *passed[3], *passed[1]],
        at.chips,
        d_width,
    )
    attend_part = jnp.where(first, first_attend, second_attend)
    hidden_sum = hidden_sum.reshape(FF)

    outputs = jnp.stack([jnp.where(first, tokens, came), jnp.where(first, came, result)])
    field_own = pick(field_halves, pipe)
    own_scale = lax.rsqrt(spread_new + EPSILON)
    field_out = (
        jnp.stack(
            [
                jnp.where(first, field_own, field_came),
                jnp.where(first, field_came, field_own),
            ]
        )
        * own_scale[None, :, None, None]
    )
    hidden_part = lax.dynamic_slice_in_dim(
        hidden_sum, (pipe * at.size + at.dp) * ff_width, ff_width
    )
    return (
        statistics,
        outputs[None],
        field_out,
        embed_grads,
        variable_grads,
        query_sum.reshape(D),
        attend_part[None],
        merge_part[None],
        position_sum,
        gain_sum,
        bias_sum,
        up_part,
        hidden_part,
        down_part,
        output_sum.reshape(D),
    )


def solution(mesh):
    return jax.shard_map(
        on_device,
        mesh=mesh,
        in_specs=(
            P("dp", "pipe", None, None),
            P("dp"),
            P("dp"),
            P(None, "pipe"),
            P(),
            P(),
            P(),
            P("pipe", None, None, None),
            P("pipe", None, None),
            P(),
            P(),
            P(),
            P(),
            P(),
            P(),
            P(),
            P("dp", None, None),
        ),
        out_specs=(
            P(None, "pipe"),
            P("pipe", "dp", None, None),
            P("dp", "pipe", None, None),
            P(),
            P(),
            P(),
            P("pipe", None, "dp", None),
            P("pipe", "dp", None),
            P(),
            P(),
            P(),
            P(None, ("pipe", "dp")),
            P(("pipe", "dp")),
            P(("pipe", "dp"), None),
            P(),
        ),
        check_vma=False,
    )
```

```python
import functools

import jax
import jax.numpy as jnp
from jax import lax
from jax.experimental import pallas as pl
from jax.experimental.pallas import tpu as pltpu
from jax.sharding import PartitionSpec as P

D = 1024
HEADS = 16
HDIM = 64
FF = 4096
VARS = 48
PATCH = 2
PATCHES = 512
PIECES = PATCH * PATCH
ROWS_TABLE = VARS * (PIECES + 1)
HALF = D // 2
QUARTER = D // 4
TABLE_PAD = 256
FF_TILE = 1024
FF_STEPS = FF // FF_TILE
PAIRS = HEADS // 2
LANES = 2 * HDIM
CHUNK = 128
TOKENS_BACK = 2
UNROLL = 4
UNROLL_PAIR = 2

PRECISE = lax.Precision.HIGHEST
EPSILON = 1e-05
MOMENTUM = 0.1
BF = jnp.bfloat16
F32 = jnp.float32
VMEM_LIMIT = 56 * 1024 * 1024


def dot(left, right, left_dim, right_dim):
    return lax.dot_general(
        left, right, (((left_dim,), (right_dim,)), ((), ())), preferred_element_type=F32
    )


VMEM = pl.BlockSpec(memory_space=pltpu.VMEM)
SMEM = pl.BlockSpec(memory_space=pltpu.SMEM)
ANYWHERE = pl.BlockSpec(memory_space=pl.ANY)


def shape(dims, kind):
    return jax.ShapeDtypeStruct(dims, kind)


def params(grid=0):
    semantics = ("arbitrary",) * grid if grid else None
    return pltpu.CompilerParams(vmem_limit_bytes=VMEM_LIMIT, dimension_semantics=semantics)


def cost():
    return pl.CostEstimate(flops=1000, bytes_accessed=1000, transcendentals=0)


def section_copies(place_ref, section, own, brought, targets, sems):
    core, side = place_ref[1], place_ref[2]

    def rows(core, side):
        return pl.ds(pl.multiple_of((2 * core + side) * QUARTER, QUARTER), QUARTER)

    @pl.when(place_ref[0] == section)
    def _():
        for n, target in enumerate(targets):
            for quarter in range(4):
                part = pl.ds(quarter * QUARTER, QUARTER)
                pltpu.make_async_copy(
                    own[n].at[part], target.at[part], sems.at[n, quarter]
                ).start()

    @pl.when(place_ref[0] != section)
    def _():
        for n, target in enumerate(targets):
            for other in range(2):
                for turn in range(2):
                    place = rows(core + other - 2 * core * other, side + turn - 2 * side * turn)
                    pltpu.make_async_copy(
                        brought[n][other].at[turn], target.at[place], sems.at[n, 2 * other + turn]
                    ).start()

    def wait(n):
        for quarter in range(4):
            part = pl.ds(quarter * QUARTER, QUARTER)
            pltpu.make_async_copy(
                brought[n][0].at[0], targets[n].at[part], sems.at[n, quarter]
            ).wait()

    return wait


def normalized(values):
    center = values - jnp.mean(values, axis=-1, keepdims=True)
    spread = jnp.mean(center * center, axis=-1, keepdims=True)
    inverse = lax.rsqrt(spread + EPSILON)
    return center * inverse, inverse


def norm_back(xhat, inverse, gain, grad):
    scaled = grad * gain
    first = jnp.mean(scaled, axis=-1, keepdims=True)
    second = jnp.mean(scaled * xhat, axis=-1, keepdims=True)
    return (scaled - first - xhat * second) * inverse


def row_chunks(body):
    def step(i, carry):
        body(pl.ds(pl.multiple_of(i * CHUNK, CHUNK), CHUNK))
        return carry

    lax.fori_loop(0, PATCHES // CHUNK, step, 0)


def column_tiles(width, body):
    def step(i, carry):
        body(pl.ds(pl.multiple_of(i * width, width), width))
        return carry

    lax.fori_loop(0, D // width, step, 0)


def head_rows(width):
    row = lax.broadcasted_iota(jnp.int32, (HEADS, width), 0)
    column = lax.broadcasted_iota(jnp.int32, (HEADS, width), 1)
    start = row * HDIM
    return (column >= start) & (column < start + HDIM)


def tables_kernel(query_ref, table_ref, weight_ref, low_ref, keys_ref, value_ref):
    given = jnp.broadcast_to(query_ref[...], (HEADS, D)).astype(BF)
    query = dot(given, weight_ref[0], 1, 0).astype(BF).astype(F32)
    low_ref[...] = query
    spread = jnp.where(head_rows(D), query, 0.0).astype(BF)
    key_query = (dot(spread, weight_ref[1], 1, 1) * HDIM ** (-0.5)).astype(BF)
    keys_ref[...] = dot(table_ref[...], key_query, 1, 1)
    values = dot(table_ref[...], weight_ref[2], 1, 0)
    value_ref[...] = jnp.concatenate([values, key_query.astype(F32)], axis=0).T


def tables(query, table, weights):
    return pl.pallas_call(
        tables_kernel,
        out_shape=(
            shape((HEADS, D), F32),
            shape((ROWS_TABLE, HEADS), F32),
            shape((D, TABLE_PAD), F32),
        ),
        in_specs=[VMEM] * 3,
        out_specs=(VMEM,) * 3,
        compiler_params=params(),
        cost_estimate=cost(),
        name="tables",
    )(query, table, weights)


COLS = 128
STRIPES = 16


def column_order():
    row = lax.broadcasted_iota(jnp.int32, (COLS, COLS), 0)
    column = lax.broadcasted_iota(jnp.int32, (COLS, COLS), 1)
    place = jnp.where(column < COLS // 2, 2 * column, 2 * column - COLS + 1)
    return (row == place).astype(F32)


def exact(left, right, right_dim):
    return lax.dot_general(
        left,
        right,
        (((1,), (right_dim,)), ((), ())),
        precision=PRECISE,
        preferred_element_type=F32,
    )


def head_keys(keys_ref, h):
    keys = keys_ref[...]
    lane = lax.broadcasted_iota(jnp.int32, keys.shape, 1)
    return jnp.sum(jnp.where(lane == h, keys, 0.0), axis=1, keepdims=True)


def mixed_rows(shares, pixels_ref):
    return jnp.concatenate(
        [(shares * pixels_ref[k]).astype(BF) for k in range(PIECES)]
        + [shares.astype(BF), jnp.zeros((TABLE_PAD - ROWS_TABLE, PATCHES), BF)],
        axis=0,
    )


def aggregate_kernel(
    place_ref,
    alive_ref,
    own_field_ref,
    other_field_ref,
    center_ref,
    scale_ref,
    keys_ref,
    tvt_ref,
    position_ref,
    own_ref,
    brought_ref,
    beside_ref,
    tokens_ref,
    heads_ref,
    shares_ref,
    pixels_ref,
    merge_ref,
    grid_ref,
    sems,
):
    wait = section_copies(
        place_ref, 0, [own_ref], [(brought_ref, beside_ref)], [merge_ref], sems
    )
    alive = alive_ref[0]
    order = column_order()
    half = VARS // 2 * STRIPES
    own, other = own_field_ref[...], other_field_ref[...]
    grid_ref[:half] = exact(jnp.where(place_ref[0] == 0, own, other), order, 0)
    grid_ref[half:] = exact(jnp.where(place_ref[0] == 0, other, own), order, 0)
    center, scale = center_ref[...], scale_ref[...]
    low_lane = lax.broadcasted_iota(jnp.int32, (VARS, COLS), 1) < COLS // 2

    def stripe(r):
        values = grid_ref[pl.ds(r, VARS, stride=STRIPES), :]
        return ((values - center) * scale).astype(BF).astype(F32)

    for a in range(PATCH):
        for j in range(PATCHES // COLS):
            even, odd = stripe(4 * j + a), stripe(4 * j + 2 + a)
            columns = slice(j * COLS, (j + 1) * COLS)
            pixels_ref[2 * a, :, columns] = jnp.where(
                low_lane, even, pltpu.roll(odd, COLS // 2, 1)
            )
            pixels_ref[2 * a + 1, :, columns] = jnp.where(
                low_lane, pltpu.roll(even, COLS // 2, 1), odd
            )

    def head(h, carry):
        keys = head_keys(keys_ref, h)
        scores = keys[PIECES * VARS :]
        for k in range(PIECES):
            scores = scores + keys[k * VARS : (k + 1) * VARS] * pixels_ref[k]
        top = jnp.max(scores, axis=0, keepdims=True)
        powers = jnp.exp(scores - top)
        shares = powers / jnp.sum(powers, axis=0, keepdims=True)
        shares_ref[h] = shares
        rows = pl.ds(pl.multiple_of(h * HDIM, HDIM), HDIM)
        heads_ref[rows, :] = dot(tvt_ref[rows, :], mixed_rows(shares, pixels_ref), 1, 0).astype(
            BF
        )
        return carry

    lax.fori_loop(0, HEADS, head, 0, unroll=UNROLL)
    wait(0)
    heads = heads_ref[...].T

    def tile(columns):
        merged = dot(heads, merge_ref[:, columns], 1, 0)
        tokens_ref[:, columns] = (alive * (merged + position_ref[:, columns].astype(F32))).astype(
            BF
        )

    column_tiles(256, tile)


def aggregate(place, alive, own_field, other_field, center, scale, keys, tvt, position, merge):
    return pl.pallas_call(
        aggregate_kernel,
        out_shape=(
            shape((PATCHES, D), BF),
            shape((D, PATCHES), BF),
            shape((HEADS, VARS, PATCHES), F32),
            shape((PIECES, VARS, PATCHES), F32),
        ),
        in_specs=[SMEM, SMEM] + [VMEM] * 7 + [ANYWHERE] * 3,
        out_specs=(VMEM,) * 4,
        scratch_shapes=[
            pltpu.VMEM((D, D), BF),
            pltpu.VMEM((VARS * STRIPES, COLS), F32),
            pltpu.SemaphoreType.DMA((1, 4)),
        ],
        compiler_params=params(),
        cost_estimate=cost(),
        name="aggregate",
    )(place, alive, own_field, other_field, center, scale, keys, tvt, position, *merge)


def attend_kernel(place_ref, tokens_ref, gain_ref, bias_ref, attend_ref, *refs):
    brought = [(refs[2 * n], refs[2 * n + 1]) for n in range(3)]
    pack_ref, proj_ref, lse_ref, weight_ref, first_ref, sems = refs[6:]
    wait = section_copies(
        place_ref,
        1,
        [attend_ref.at[j] for j in range(3)],
        brought,
        [weight_ref.at[j] for j in range(3)],
        sems,
    )

    def first_norm(rows):
        xhat, _ = normalized(tokens_ref[rows, :].astype(F32))
        first_ref[rows, :] = (xhat * gain_ref[0:1, :] + bias_ref[0:1, :]).astype(BF)

    row_chunks(first_norm)
    pack_ref[:D, :] = first_ref[...].T
    for j in range(3):
        wait(j)
        column_tiles(
            256,
            lambda columns: proj_ref.__setitem__(
                (j, slice(None), columns),
                dot(first_ref[...], weight_ref[j, :, columns], 1, 0).astype(BF),
            ),
        )

    lane = lax.broadcasted_iota(jnp.int32, (PATCHES, LANES), 1)

    def pair(i, carry):
        columns = pl.ds(pl.multiple_of(i * LANES, LANES), LANES)
        queries = proj_ref[0, :, columns]
        keys = proj_ref[1, :, columns]
        values = proj_ref[2, :, columns].T
        for side in range(2):
            inside = (lane < HDIM) if side == 0 else (lane >= HDIM)
            key = jnp.where(inside, keys * HDIM ** (-0.5), jnp.zeros_like(keys)).astype(BF)
            scores = dot(key, queries, 1, 1)
            top = jnp.max(scores, axis=0, keepdims=True)
            powers = jnp.exp(scores - top)
            whole = jnp.sum(powers, axis=0, keepdims=True)
            probs = (powers * (1.0 / whole)).astype(BF)
            lse_ref[i, side : side + 1, :] = top + jnp.log(whole)
            value = values[side * HDIM : (side + 1) * HDIM]
            rows = pl.ds(pl.multiple_of(D + i * LANES + side * HDIM, HDIM), HDIM)
            pack_ref[rows, :] = dot(value, probs, 1, 0).astype(BF)
        return carry

    lax.fori_loop(0, PAIRS, pair, 0, unroll=UNROLL_PAIR)


def attend(place, tokens, gain, bias, own_attend, brought):
    return pl.pallas_call(
        attend_kernel,
        out_shape=(
            shape((2 * D, PATCHES), BF),
            shape((3, PATCHES, D), BF),
            shape((PAIRS, 2, PATCHES), F32),
        ),
        in_specs=[SMEM] + [VMEM] * 3 + [ANYWHERE] * 7,
        out_specs=(VMEM,) * 3,
        scratch_shapes=[
            pltpu.VMEM((3, D, D), BF),
            pltpu.VMEM((PATCHES, D), BF),
            pltpu.SemaphoreType.DMA((3, 4)),
        ],
        compiler_params=params(),
        cost_estimate=cost(),
        name="attend",
    )(place, tokens, gain, bias, own_attend, *brought)


def gelu_parts(hidden):
    inverse = 1.0 / (1.0 + 0.23164190 * jnp.abs(hidden))
    decay = jnp.exp2(hidden * hidden * (-0.72134752))
    series = 0.5 * 1.061405429
    for factor in (-1.453152027, 1.421413741, -0.284496736, 0.254829592):
        series = series * inverse + 0.5 * factor
    tail = series * inverse * decay
    cdf = jnp.where(hidden >= 0.0, 1.0 - tail, tail)
    return cdf, decay * 0.3989422804014327


FF_PART = 1024
UNITS = FF + HALF


def copy(source, target, sem):
    return pltpu.make_async_copy(source, target, sem)


def aligned(index, size):
    return pl.ds(pl.multiple_of(index * size, size), size)


def start_either(choice, source, if_true, if_false, sem):
    @pl.when(choice)
    def _():
        copy(source, if_true, sem).start()

    @pl.when(jnp.logical_not(choice))
    def _():
        copy(source, if_false, sem).start()


def expand_kernel(
    place_ref,
    tokens_ref,
    out_ref,
    gain_ref,
    norm_bias_ref,
    bias_ref,
    pack_any,
    own_any,
    brought_any,
    beside_any,
    up_any,
    down_any,
    after_any,
    units_any,
    middle_any,
    second_any,
    sum_ref,
    up_ref,
    down_ref,
    tile_ref,
    merge_ref,
    context_ref,
    middle_ref,
    second_ref,
    merge_sems,
    in_sems,
    out_sems,
):
    def fetch(j):
        part = aligned(j, FF_TILE)
        return (
            copy(up_any.at[:, part], up_ref.at[:, part], in_sems.at[j, 0]),
            copy(down_any.at[part], down_ref.at[part], in_sems.at[j, 1]),
        )

    def start(j):
        for one in fetch(j):
            one.start()

    def put(j, slot):
        return copy(
            tile_ref.at[slot], units_any.at[:, :, aligned(j, FF_TILE)], out_sems.at[slot]
        )

    context = copy(pack_any.at[pl.ds(D, D)], context_ref, in_sems.at[FF_STEPS, 0])
    context.start()
    wait = section_copies(
        place_ref, 1, [own_any], [(brought_any, beside_any)], [merge_ref], merge_sems
    )
    start(0)
    context.wait()
    turned = context_ref[...].T
    wait(0)
    column_tiles(
        512,
        lambda columns: middle_ref.__setitem__(
            (slice(None), columns),
            tokens_ref[:, columns].astype(F32) + dot(turned, merge_ref[:, columns], 1, 0),
        ),
    )
    middle_out = copy(middle_ref, middle_any, in_sems.at[FF_STEPS, 1])
    middle_out.start()
    start(1)

    def second_norm(rows):
        xhat, _ = normalized(middle_ref[rows, :])
        second_ref[rows, :] = (xhat * gain_ref[1:2, :] + norm_bias_ref[1:2, :]).astype(BF)

    row_chunks(second_norm)
    second_out = copy(second_ref, second_any, out_sems.at[2])
    second_out.start()

    def step(j, carry):
        slot = lax.rem(j, 2)

        @pl.when(j + 2 < FF_STEPS)
        def _():
            start(j + 2)

        @pl.when(j >= 2)
        def _():
            put(j - 2, slot).wait()

        for one in fetch(j):
            one.wait()
        for part in range(FF_TILE // FF_PART):
            inner = slice(part * FF_PART, (part + 1) * FF_PART)
            begin = pl.multiple_of(j * FF_TILE + part * FF_PART, FF_PART)
            columns = pl.ds(begin, FF_PART)
            hidden = dot(second_ref[...], up_ref[:, columns], 1, 0) + bias_ref[:, columns]
            grad = dot(out_ref[...], down_ref[columns, :], 1, 1)
            cdf, density = gelu_parts(hidden)
            tile_ref[slot, 0, :, inner] = (hidden * cdf).astype(BF)
            low = (grad * (cdf + hidden * density)).astype(BF)
            tile_ref[slot, 1, :, inner] = low
            sum_ref[:, columns] = jnp.sum(low.astype(F32), axis=0, keepdims=True)
        put(j, slot).start()
        return carry

    lax.fori_loop(0, FF_STEPS, step, 0)
    others = aligned(1 - place_ref[1], HALF)
    put(FF_STEPS - 2, 0).wait()
    tile_ref[0, 0, :, :HALF] = out_ref[:, others]
    tile_ref[0, 1, :, :HALF] = second_ref[:, others]
    end = copy(
        tile_ref.at[0, :, :, pl.ds(0, HALF)], units_any.at[:, :, pl.ds(FF, HALF)], out_sems.at[0]
    )
    end.start()
    middle_out.wait()
    second_out.wait()
    put(FF_STEPS - 1, 1).wait()
    end.wait()


def expand(place, tokens, out_low, gain, norm_bias, pack, merge, up, bias, down, after):
    return pl.pallas_call(
        expand_kernel,
        out_shape=(
            shape((2, PATCHES, UNITS), BF),
            shape((PATCHES, D), F32),
            shape((PATCHES, D), BF),
            shape((1, FF), F32),
        ),
        in_specs=[SMEM] + [VMEM] * 5 + [ANYWHERE] * 7,
        out_specs=(ANYWHERE, ANYWHERE, ANYWHERE, VMEM),
        scratch_shapes=[
            pltpu.VMEM((D, FF), BF),
            pltpu.VMEM((FF, D), BF),
            pltpu.VMEM((2, 2, PATCHES, FF_TILE), BF),
            pltpu.VMEM((D, D), BF),
            pltpu.VMEM((D, PATCHES), BF),
            pltpu.VMEM((PATCHES, D), F32),
            pltpu.VMEM((PATCHES, D), BF),
            pltpu.SemaphoreType.DMA((1, 4)),
            pltpu.SemaphoreType.DMA((FF_STEPS + 1, 2)),
            pltpu.SemaphoreType.DMA((3,)),
        ],
        compiler_params=params(),
        cost_estimate=cost(),
        name="expand",
    )(place, tokens, out_low, gain, norm_bias, bias.reshape(1, FF), pack, *merge, up, down, after)


DEPTHS = 4
DEPTH = FF // DEPTHS


def contract_kernel(
    place_ref,
    scalars_ref,
    gain_ref,
    bias_ref,
    units_any,
    up_any,
    down_any,
    middle_any,
    cotangent_any,
    result_ref,
    grad_ref,
    branch_ref,
    gain_grad_ref,
    bias_grad_ref,
    out_grad_ref,
    units_ref,
    up_ref,
    down_ref,
    middle_ref,
    cotangent_ref,
    total_ref,
    second_ref,
    sems,
):
    def fetch(n):
        which, c = divmod(n, DEPTHS)
        part = slice(c * DEPTH, (c + 1) * DEPTH)
        if which == 0:
            weight = copy(down_any.at[part], down_ref.at[part], sems.at[n, 1])
        else:
            weight = copy(up_any.at[:, part], up_ref.at[:, part], sems.at[n, 1])
        return (
            copy(units_any.at[which, :, part], units_ref.at[which, :, part], sems.at[n, 0]),
            weight,
        )

    rest = (
        copy(middle_any, middle_ref, sems.at[2 * DEPTHS, 0]),
        copy(cotangent_any.at[place_ref[0]], cotangent_ref, sems.at[2 * DEPTHS, 1]),
    )
    for n in range(2):
        for one in fetch(n):
            one.start()
    for n in range(2 * DEPTHS):
        which, c = divmod(n, DEPTHS)
        part = slice(c * DEPTH, (c + 1) * DEPTH)
        for one in fetch(n + 2) if n + 2 < 2 * DEPTHS else rest if n + 2 == 2 * DEPTHS else ():
            one.start()
        for one in fetch(n):
            one.wait()
        ref = second_ref if which else total_ref
        if which:
            product = dot(units_ref[1, :, part], up_ref[:, part], 1, 1)
        else:
            product = dot(units_ref[0, :, part], down_ref[part, :], 1, 0)
        if c:
            ref[...] += product
        else:
            ref[...] = product
    for one in rest:
        one.wait()
    alive, hat = scalars_ref[0], scalars_ref[1]
    gain_grad_ref[...] = jnp.zeros_like(gain_grad_ref)
    bias_grad_ref[...] = jnp.zeros_like(bias_grad_ref)
    out_grad_ref[...] = jnp.zeros_like(out_grad_ref)

    def chunk(rows):
        middle = middle_ref[rows, :]
        result_ref[rows, :] = (alive * (middle + total_ref[rows, :] + bias_ref[...])).astype(BF)
        xhat, inverse = normalized(middle)
        grad = second_ref[rows, :]
        gain_grad_ref[...] += jnp.sum(grad * xhat, axis=0, keepdims=True)
        bias_grad_ref[...] += jnp.sum(grad, axis=0, keepdims=True)
        out = cotangent_ref[rows, :].astype(F32) * hat
        out_grad_ref[...] += jnp.sum(out, axis=0, keepdims=True)
        whole = out + norm_back(xhat, inverse, gain_ref[...], grad)
        grad_ref[rows, :] = whole
        branch_ref[rows, :] = whole.astype(BF)

    row_chunks(chunk)


def contract(place, scalars, units, up, down, middle, cotangent, gain, bias):
    return pl.pallas_call(
        contract_kernel,
        out_shape=(
            shape((PATCHES, D), BF),
            shape((PATCHES, D), F32),
            shape((PATCHES, D), BF),
            shape((1, D), F32),
            shape((1, D), F32),
            shape((1, D), F32),
        ),
        in_specs=[SMEM, SMEM, VMEM, VMEM] + [ANYWHERE] * 5,
        out_specs=(VMEM,) * 6,
        scratch_shapes=[
            pltpu.VMEM((2, PATCHES, FF), BF),
            pltpu.VMEM((D, FF), BF),
            pltpu.VMEM((FF, D), BF),
            pltpu.VMEM((PATCHES, D), F32),
            pltpu.VMEM((PATCHES, D), BF),
            pltpu.VMEM((PATCHES, D), F32),
            pltpu.VMEM((PATCHES, D), F32),
            pltpu.SemaphoreType.DMA((2 * DEPTHS + 1, 2)),
        ],
        compiler_params=params(),
        cost_estimate=cost(),
        name="contract",
    )(place, scalars, gain, bias, units, up, down, middle, cotangent)


def attend_back_kernel(
    place_ref,
    grad_ref,
    branch_ref,
    proj_ref,
    lse_ref,
    tokens_ref,
    gain_ref,
    attend_ref,
    merge_ref,
    *refs,
):
    brought = [(refs[2 * n], refs[2 * n + 1]) for n in range(4)]
    outs = refs[8 + TOKENS_BACK :]
    keep_ref, send_ref, token_grad_ref, gain_grad_ref, bias_grad_ref = outs[:5]
    weight_ref, context_ref, first_ref, proj_grad_ref, sems = outs[5:]
    wait = section_copies(
        place_ref,
        1,
        [merge_ref] + [attend_ref.at[j] for j in range(3)],
        brought[3:] + brought[:3],
        [weight_ref.at[j] for j in range(4)],
        sems,
    )
    wait(0)
    branch = branch_ref[...]

    def context_tile(columns):
        context_ref[:, columns] = dot(branch, weight_ref[0, columns, :], 1, 1).astype(BF)

    column_tiles(256, context_tile)
    lane = lax.broadcasted_iota(jnp.int32, (PATCHES, LANES), 1)

    def pair(i, carry):
        columns = pl.ds(pl.multiple_of(i * LANES, LANES), LANES)
        queries = proj_ref[0, :, columns]
        keys = proj_ref[1, :, columns]
        values = proj_ref[2, :, columns]
        grads = context_ref[:, columns]
        keys_turned = keys.T
        blank = jnp.zeros_like(keys)
        query_grads, key_grads, value_grads = [], [], []
        for side in range(2):
            inside = (lane < HDIM) if side == 0 else (lane >= HDIM)
            key = jnp.where(inside, keys * HDIM ** (-0.5), blank).astype(BF)
            value = jnp.where(inside, values, blank)
            probs = jnp.exp(dot(key, queries, 1, 1) - lse_ref[i, side : side + 1, :])
            share_grad = dot(value, grads, 1, 1)
            weighted = probs * share_grad
            inner = jnp.sum(weighted, axis=0, keepdims=True)
            score_low = (weighted - probs * inner).astype(BF)
            value_grads.append(dot(probs.astype(BF), grads, 1, 0))
            key_grads.append(dot(score_low, queries, 1, 0))
            query_grads.append(
                dot(keys_turned[side * HDIM : (side + 1) * HDIM], score_low, 1, 0)
            )
        low = lane < HDIM
        query_grad = jnp.concatenate(query_grads, axis=0) * HDIM ** (-0.5)
        proj_grad_ref[0, :, columns] = query_grad.T.astype(BF)
        proj_grad_ref[1, :, columns] = (
            jnp.where(low, key_grads[0], key_grads[1]) * HDIM ** (-0.5)
        ).astype(BF)
        proj_grad_ref[2, :, columns] = jnp.where(low, value_grads[0], value_grads[1]).astype(BF)
        return carry

    lax.fori_loop(0, PAIRS, pair, 0, unroll=UNROLL_PAIR)
    core = place_ref[1]
    owns = pl.ds(pl.multiple_of(core * HALF, HALF), HALF)
    others = pl.ds(pl.multiple_of((1 - core) * HALF, HALF), HALF)
    for j in range(3):
        keep_ref[j] = proj_grad_ref[j, :, owns]
        send_ref[j] = proj_grad_ref[j, :, others]
    keep_ref[3] = branch_ref[:, owns]
    send_ref[3] = branch_ref[:, others]
    for j in range(3):
        wait(j + 1)

    def first_tile(columns):
        total = dot(proj_grad_ref[0], weight_ref[1, columns, :], 1, 1)
        for j in range(1, 3):
            total = total + dot(proj_grad_ref[j], weight_ref[j + 1, columns, :], 1, 1)
        first_ref[:, columns] = total

    column_tiles(256, first_tile)
    gain_grad_ref[...] = jnp.zeros_like(gain_grad_ref)
    bias_grad_ref[...] = jnp.zeros_like(bias_grad_ref)

    def chunk(rows):
        xhat, inverse = normalized(tokens_ref[rows, :].astype(F32))
        grad = first_ref[rows, :]
        gain_grad_ref[...] += jnp.sum(grad * xhat, axis=0, keepdims=True)
        bias_grad_ref[...] += jnp.sum(grad, axis=0, keepdims=True)
        token_grad_ref[rows, :] = (
            grad_ref[rows, :] + norm_back(xhat, inverse, gain_ref[0:1, :], grad)
        ).astype(BF)

    row_chunks(chunk)


def attend_back(
    place, grad, branch, proj, lse, tokens, gain, own_attend, own_merge, brought, after
):
    return pl.pallas_call(
        attend_back_kernel,
        out_shape=(
            shape((4, PATCHES, HALF), BF),
            shape((4, PATCHES, HALF), BF),
            shape((PATCHES, D), BF),
            shape((1, D), F32),
            shape((1, D), F32),
        ),
        in_specs=[SMEM] + [VMEM] * 6 + [ANYWHERE] * (10 + TOKENS_BACK),
        out_specs=(VMEM,) * 5,
        scratch_shapes=[
            pltpu.VMEM((4, D, D), BF),
            pltpu.VMEM((PATCHES, D), BF),
            pltpu.VMEM((PATCHES, D), F32),
            pltpu.VMEM((3, PATCHES, D), BF),
            pltpu.SemaphoreType.DMA((4, 4)),
        ],
        compiler_params=params(),
        cost_estimate=cost(),
        name="attend_back",
    )(place, grad, branch, proj, lse, tokens, gain, own_attend, own_merge, *brought, *after)


MIX_AT = PATCHES
SMALL_AT = PATCHES + TABLE_PAD
KEYS_AT = SMALL_AT + 16
TAIL = KEYS_AT + ROWS_TABLE


def aggregate_back_kernel(
    place_ref,
    alive_ref,
    token_grad_ref,
    pixels_ref,
    keys_ref,
    tvt_ref,
    shares_ref,
    gain_first_ref,
    gain_second_ref,
    bias_first_ref,
    bias_second_ref,
    output_ref,
    hidden_ref,
    own_ref,
    brought_ref,
    beside_ref,
    keep_ref,
    send_ref,
    field_ref,
    key_grad_ref,
    head_ref,
    merge_ref,
    mix_ref,
    pixel_grad_ref,
    grid_ref,
    sems,
):
    wait = section_copies(
        place_ref, 0, [own_ref], [(brought_ref, beside_ref)], [merge_ref], sems
    )
    core = place_ref[1]
    owns = pl.ds(pl.multiple_of(core * HALF, HALF), HALF)
    others = pl.ds(pl.multiple_of((1 - core) * HALF, HALF), HALF)
    alive = alive_ref[0]
    pre = (token_grad_ref[...].astype(F32) * alive).astype(BF)
    keep_ref[:PATCHES, :] = (token_grad_ref[:, owns].astype(F32) * alive).astype(BF)
    send_ref[:PATCHES, :] = (token_grad_ref[:, others].astype(F32) * alive).astype(BF)
    wait(0)

    def head_tile(rows):
        head_ref[rows, :] = dot(merge_ref[rows, :], pre, 1, 1).astype(BF)

    column_tiles(256, head_tile)
    pixel_grad_ref[...] = jnp.zeros_like(pixel_grad_ref)
    key_grad_ref[...] = jnp.zeros_like(key_grad_ref)
    lane = lax.broadcasted_iota(jnp.int32, (VARS, HEADS), 1)

    def head(h, carry):
        rows = pl.ds(pl.multiple_of(h * HDIM, HDIM), HDIM)
        keys = head_keys(keys_ref, h)
        grads = head_ref[rows, :]
        shares = shares_ref[h]
        mix_ref[rows, :] = dot(grads, mixed_rows(shares, pixels_ref), 1, 1)
        row_grads = dot(tvt_ref[rows, :], grads, 0, 0)
        share_grads = row_grads[PIECES * VARS : ROWS_TABLE]
        for k in range(PIECES):
            share_grads = share_grads + row_grads[k * VARS : (k + 1) * VARS] * pixels_ref[k]
        inner = jnp.sum(shares * share_grads, axis=0, keepdims=True)
        scores = shares * (share_grads - inner)
        for k in range(PIECES + 1):
            piece = slice(k * VARS, (k + 1) * VARS)
            if k < PIECES:
                pixel_grad_ref[k] += shares * row_grads[piece] + scores * keys[piece]
                total = jnp.sum(scores * pixels_ref[k], axis=1, keepdims=True)
            else:
                total = jnp.sum(scores, axis=1, keepdims=True)
            key_grad_ref[piece, :] += jnp.where(lane == h, total, 0.0)
        return carry

    lax.fori_loop(0, HEADS, head, 0, unroll=UNROLL)
    for ref, start in ((keep_ref, core * HALF), (send_ref, (1 - core) * HALF)):
        for part in range(2):
            rows = pl.ds(pl.multiple_of(start + part * TABLE_PAD, TABLE_PAD), TABLE_PAD)
            ref[MIX_AT:SMALL_AT, part * TABLE_PAD : (part + 1) * TABLE_PAD] = mix_ref[
                rows, :
            ].astype(BF)
        columns = pl.ds(pl.multiple_of(start, HALF), HALF)
        small = [
            one[:, columns]
            for one in (
                gain_first_ref,
                gain_second_ref,
                bias_first_ref,
                bias_second_ref,
                output_ref,
            )
        ]
        for part in range(FF // D):
            small.append(hidden_ref[:, pl.ds(pl.multiple_of(part * D + start, HALF), HALF)])
        small.append(jnp.zeros((16 - len(small), HALF), F32))
        ref[SMALL_AT:KEYS_AT, :] = jnp.concatenate(small, axis=0).astype(BF)
        ref[KEYS_AT:, :] = jnp.concatenate(
            [key_grad_ref[...], jnp.zeros((ROWS_TABLE, HALF - HEADS), F32)], axis=1
        ).astype(BF)
    low_lane = lax.broadcasted_iota(jnp.int32, (VARS, COLS), 1) < COLS // 2
    for a in range(PATCH):
        for j in range(PATCHES // COLS):
            columns = slice(j * COLS, (j + 1) * COLS)
            low, high = pixel_grad_ref[2 * a, :, columns], pixel_grad_ref[2 * a + 1, :, columns]
            even = jnp.where(low_lane, low, pltpu.roll(high, COLS // 2, 1))
            odd = jnp.where(low_lane, pltpu.roll(low, COLS // 2, 1), high)
            grid_ref[pl.ds(4 * j + a, VARS, stride=STRIPES), :] = even
            grid_ref[pl.ds(4 * j + 2 + a, VARS, stride=STRIPES), :] = odd
    field_ref[...] = exact(grid_ref[...], column_order(), 1)


def aggregate_back(place, alive, token_grad, pixels, keys, tvt, shares, small, merge):
    return pl.pallas_call(
        aggregate_back_kernel,
        out_shape=(
            shape((TAIL, HALF), BF),
            shape((TAIL, HALF), BF),
            shape((VARS * STRIPES, COLS), F32),
        ),
        in_specs=[SMEM, SMEM] + [VMEM] * 11 + [ANYWHERE] * 3,
        out_specs=(VMEM,) * 3,
        scratch_shapes=[
            pltpu.VMEM((ROWS_TABLE, HEADS), F32),
            pltpu.VMEM((D, PATCHES), BF),
            pltpu.VMEM((D, D), BF),
            pltpu.VMEM((D, TABLE_PAD), F32),
            pltpu.VMEM((PIECES, VARS, PATCHES), F32),
            pltpu.VMEM((VARS * STRIPES, COLS), F32),
            pltpu.SemaphoreType.DMA((1, 4)),
        ],
        compiler_params=params(),
        cost_estimate=cost(),
        name="aggregate_back",
    )(place, alive, token_grad, pixels, keys, tvt, shares, *small, *merge)


BLOCKS = 16
BLOCK = FF // BLOCKS
SPANS = BLOCKS // 2
SPAN = 4 * BLOCK


def wide_kernel(which, by_pipe, place_ref, left_any, own_any, beside_any, *refs):
    send_any, keep_any, left_ref, turned_ref, right_ref, product_ref, sems, out_sems = refs[-8:]
    place, core = place_ref[0], place_ref[1]
    side, z_low = jnp.bitwise_and(place, 1), jnp.bitwise_and(lax.shift_right_logical(place, 1), 1)

    def fetch(i):
        columns = aligned(jnp.bitwise_xor(3 - i, lax.shift_right_logical(place, 2)), SPAN)
        return [
            copy(
                source.at[which, :, columns],
                right_ref.at[i, pl.ds(n * PATCHES, PATCHES)],
                sems.at[i, n],
            )
            for n, source in enumerate((own_any, beside_any))
        ]

    lefts = (
        copy(left_any.at[:, aligned(core, HALF)], left_ref.at[0], sems.at[4, 0]),
        copy(beside_any.at[which, :, pl.ds(FF, HALF)], left_ref.at[1], sems.at[4, 1]),
    )
    for one in lefts:
        one.start()
    for i in range(2):
        for one in fetch(i):
            one.start()
    for n, one in enumerate(lefts):
        one.wait()
        turned_ref[:, n * PATCHES : (n + 1) * PATCHES] = left_ref[n].T

    def put(i, block):
        source = product_ref.at[i % 2, :, pl.ds(block * BLOCK, BLOCK)]
        return source, out_sems.at[i % 2, block]

    def wait(i):
        for block in range(4):
            source, sem = put(i, block)
            copy(source, send_any.at[0, 0, 0], sem).wait()

    for i in range(4):
        for one in fetch(i + 2) if i < 2 else ():
            one.start()
        for one in fetch(i):
            one.wait()
        if i >= 2:
            wait(i - 2)
        product_ref[i % 2] = dot(turned_ref[...], right_ref[i], 1, 0).astype(BF)
        pipe, z_high = divmod(3 - i, 2)
        for block in range(4):
            source, sem = put(i, block)
            to_side = jnp.bitwise_xor(block % 2, side)
            to_z = jnp.bitwise_xor(block // 2, z_low)
            if by_pipe:
                target = send_any if pipe else keep_any
                copy(source, target.at[to_side, z_high, to_z], sem).start()
            else:
                start_either(
                    to_side == 1,
                    source,
                    send_any.at[pipe, z_high, to_z],
                    keep_any.at[pipe, z_high, to_z],
                    sem,
                )
    wait(2)
    wait(3)


def wide_grads(place, left, right, which, by_pipe, after, name):
    return pl.pallas_call(
        functools.partial(wide_kernel, which, by_pipe),
        in_specs=[SMEM] + [ANYWHERE] * (3 + len(after)),
        out_specs=(ANYWHERE, ANYWHERE),
        out_shape=(shape((2, 2, 2, HALF, BLOCK), BF), shape((2, 2, 2, HALF, BLOCK), BF)),
        scratch_shapes=[
            pltpu.VMEM((2, PATCHES, HALF), BF),
            pltpu.VMEM((HALF, 2 * PATCHES), BF),
            pltpu.VMEM((4, 2 * PATCHES, SPAN), BF),
            pltpu.VMEM((2, HALF, SPAN), BF),
            pltpu.SemaphoreType.DMA((5, 2)),
            pltpu.SemaphoreType.DMA((2, 4)),
        ],
        compiler_params=params(),
        cost_estimate=cost(),
        name=name,
    )(place, left, *right, *after)


ROWS = D // SPANS
PARTS = 4 * ROWS
CROSS = ROWS


def square_kernel(
    place_ref,
    tail_own,
    tail_beside,
    heads_own,
    heads_beside,
    pack_own,
    pack_beside,
    right_own,
    right_beside,
    *refs,
):
    send_any, keep_any, cross_send_any, cross_keep_any = refs[-9:-5]
    left_ref, right_ref, product_ref, sems, out_sems = refs[-5:]
    pipe, place = place_ref[0], place_ref[1]
    side, z = jnp.bitwise_and(place, 1), lax.shift_right_logical(place, 1)
    lefts = [
        (pack_own.at[pl.ds(0, D)], pack_beside.at[pl.ds(0, D)]),
        (pack_own.at[pl.ds(D, D)], pack_beside.at[pl.ds(D, D)]),
        (heads_own, heads_beside),
    ]
    left_copies = [
        [
            copy(one, left_ref.at[n, :, pl.ds(m * PATCHES, PATCHES)], sems.at[n, m])
            for m, one in enumerate(pair)
        ]
        for n, pair in enumerate(lefts)
    ]
    right_copies = [
        [
            copy(one.at[n], right_ref.at[n, pl.ds(m * PATCHES, PATCHES)], sems.at[3 + n, m])
            for m, one in enumerate((right_own, right_beside))
        ]
        for n in range(4)
    ]
    for n in (0, 3, 1, 2):
        for one in (left_copies[n] if n < 3 else []) + right_copies[n]:
            one.start()
    right_ref[4, :PATCHES] = tail_own[:PATCHES]
    right_ref[4, PATCHES:] = tail_beside[:PATCHES]

    def put(slot, block):
        return product_ref.at[slot, pl.ds(block * ROWS, ROWS)], out_sems.at[slot, block]

    def wait(slot):
        for block in range(SPANS):
            source, sem = put(slot, block)
            copy(source, send_any.at[0, pl.ds(0, ROWS)], sem).wait()

    def share(slot, part):
        rows = pl.ds(part * ROWS, ROWS)
        for block in range(SPANS):
            source, sem = put(slot, block)
            to_z = jnp.bitwise_xor(block // 2, z)
            start_either(
                side != block % 2, source, send_any.at[to_z, rows], keep_any.at[to_z, rows], sem
            )

    def cross(slot, part, goal):
        rows = pl.ds(part * ROWS, ROWS)
        for block in range(SPANS):
            source, sem = put(slot, block)
            to_side = jnp.bitwise_xor(block % 2, side)
            to_z = jnp.bitwise_xor(block // 2, z)
            start_either(
                pipe != goal,
                source,
                cross_send_any.at[to_side, to_z, rows],
                cross_keep_any.at[to_side, to_z, rows],
                sem,
            )

    product_ref[0] = (tail_own[...].astype(F32) + tail_beside[...].astype(F32)).astype(BF)
    share(0, 1)
    for step, (left, right) in enumerate(((0, 0), (1, 3), (2, 4), (0, 1), (0, 2))):
        slot = (step + 1) % 2
        if step in (0, 1, 2):
            for one in left_copies[left]:
                one.wait()
        if right < 4:
            for one in right_copies[right]:
                one.wait()
        if step >= 1:
            wait(slot)
        for tile in range(2):
            rows = slice(tile * HALF, (tile + 1) * HALF)
            product_ref[slot, rows] = dot(left_ref[left, rows], right_ref[right], 1, 0).astype(BF)
        if step < 3:
            share(slot, (0, 3, 2)[step])
        else:
            cross(slot, 0, step - 3)
    wait(0)
    wait(1)


def square_grads(place, tail, heads, pack, right, after):
    return pl.pallas_call(
        square_kernel,
        in_specs=[SMEM, VMEM, VMEM] + [ANYWHERE] * (6 + len(after)),
        out_specs=(ANYWHERE,) * 4,
        out_shape=(
            shape((4, PARTS, HALF), BF),
            shape((4, PARTS, HALF), BF),
            shape((2, 4, CROSS, HALF), BF),
            shape((2, 4, CROSS, HALF), BF),
        ),
        scratch_shapes=[
            pltpu.VMEM((3, D, 2 * PATCHES), BF),
            pltpu.VMEM((5, 2 * PATCHES, HALF), BF),
            pltpu.VMEM((2, D, HALF), BF),
            pltpu.SemaphoreType.DMA((7, 2)),
            pltpu.SemaphoreType.DMA((2, SPANS)),
        ],
        compiler_params=params(),
        cost_estimate=cost(),
        name="square_grads",
    )(place, *tail, *heads, *pack, *right, *after)


def first_sums_kernel(down_keep, down_came, up_keep, up_came, after_any, down_ref, up_ref):
    for z in range(4):
        at = (0, z // 2, z % 2)
        down_ref[z] = (down_keep[at].astype(F32) + down_came[at].astype(F32)).astype(BF)
        up_ref[z] = (up_keep[at].astype(F32) + up_came[at].astype(F32)).astype(BF)


def first_sums(down_keep, down_came, up_keep, up_came, after):
    half = pl.BlockSpec((1, 2, 2, HALF, BLOCK), lambda i: (1, 0, 0, 0, 0))
    return pl.pallas_call(
        first_sums_kernel,
        grid=(1,),
        in_specs=[half] * 4 + [ANYWHERE],
        out_specs=(VMEM, VMEM),
        out_shape=(shape((4, HALF, BLOCK), BF), shape((4, HALF, BLOCK), BF)),
        compiler_params=params(1),
        cost_estimate=cost(),
        name="first_sums",
    )(down_keep, down_came, up_keep, up_came, after)


def second_sums_kernel(
    down_keep, down_came, down_brought, up_keep, up_came, up_brought, after_any, *outs
):
    def added(keep, came, brought, z):
        at = (0, z // 2, z % 2)
        one = (keep[at].astype(F32) + came[at].astype(F32)).astype(BF).astype(F32)
        return (one + brought[z].astype(F32)).astype(BF)

    for z in range(4):
        outs[z][0] = added(down_keep, down_came, down_brought, z)
        outs[z][1] = added(up_keep, up_came, up_brought, z)


def second_sums(down_keep, down_came, down_brought, up_keep, up_came, up_brought, after):
    half = pl.BlockSpec((1, 2, 2, HALF, BLOCK), lambda i: (0, 0, 0, 0, 0))
    return pl.pallas_call(
        second_sums_kernel,
        grid=(1,),
        in_specs=[half, half, VMEM] * 2 + [ANYWHERE],
        out_specs=(VMEM,) * 4,
        out_shape=(shape((2, HALF, BLOCK), BF),) * 4,
        compiler_params=params(1),
        cost_estimate=cost(),
        name="second_sums",
    )(down_keep, down_came, down_brought, up_keep, up_came, up_brought, after)


def third_sums_kernel(keep, came, out_ref):
    for z in range(4):
        out_ref[z] = (keep[0, z].astype(F32) + came[0, z].astype(F32)).astype(BF)


def third_sums(keep, came):
    half = pl.BlockSpec((1, 4, CROSS, HALF), lambda i: (1, 0, 0, 0))
    return pl.pallas_call(
        third_sums_kernel,
        grid=(1,),
        in_specs=[half, half],
        out_specs=VMEM,
        out_shape=shape((4, CROSS, HALF), BF),
        compiler_params=params(1),
        cost_estimate=cost(),
        name="third_sums",
    )(keep, came)


def fourth_sums_kernel(keep, came, cross_keep, cross_came, brought, *refs):
    for z in range(4):
        out_ref = refs[len(refs) - 4 + z]
        out_ref[:PARTS] = (keep[z].astype(F32) + came[z].astype(F32)).astype(BF)
        one = (cross_keep[0, z].astype(F32) + cross_came[0, z].astype(F32)).astype(BF)
        out_ref[PARTS:] = (one.astype(F32) + brought[z].astype(F32)).astype(BF)


def fourth_sums(keep, came, cross_keep, cross_came, brought, after):
    half = pl.BlockSpec((1, 4, CROSS, HALF), lambda i: (0, 0, 0, 0))
    return pl.pallas_call(
        fourth_sums_kernel,
        grid=(1,),
        in_specs=[VMEM, VMEM, half, half, VMEM] + [ANYWHERE] * len(after),
        out_specs=(VMEM,) * 4,
        out_shape=(shape((PARTS + CROSS, HALF), BF),) * 4,
        compiler_params=params(1),
        cost_estimate=cost(),
        name="fourth_sums",
    )(keep, came, cross_keep, cross_came, brought, *after)


def finish_kernel(
    chips,
    place_ref,
    tail_ref,
    table_ref,
    query_ref,
    given_ref,
    value_ref,
    attend_ref,
    *refs,
):
    brought = [(refs[2 * n], refs[2 * n + 1]) for n in range(3)]
    position_ref, gain_ref, bias_ref, output_ref, hidden_ref = refs[6:11]
    embed_ref, variable_ref, attend_grad_ref, query_grad_ref = refs[11:15]
    weight_ref, whole_ref, mix_ref, rows_ref, turned_ref, sems = refs[15:]
    core, chip, spot = place_ref[1], place_ref[3], place_ref[4]
    wait = section_copies(
        place_ref,
        0,
        [attend_ref.at[j] for j in range(3)],
        brought,
        [weight_ref.at[j] for j in range(3)],
        sems,
    )
    part = TAIL // chips
    for c in range(2):
        for n in range(chips):
            whole_ref[c, n * part : (n + 1) * part, :] = tail_ref[
                jnp.bitwise_xor(c, core), jnp.bitwise_xor(n, chip)
            ].astype(F32)
    for c in range(2):
        columns = slice(c * HALF, (c + 1) * HALF)
        position_ref[:, columns] = whole_ref[c, :PATCHES, :]
        small = whole_ref[c, SMALL_AT:KEYS_AT, :]
        gain_ref[:, columns] = small[0:2]
        bias_ref[:, columns] = small[2:4]
        output_ref[:, columns] = small[4:5]
        hidden_ref[:, columns] = small[5:9]
        for n in range(2):
            start = c * HALF + n * TABLE_PAD
            mix_ref[start : start + TABLE_PAD, :] = whole_ref[
                c, MIX_AT:SMALL_AT, n * TABLE_PAD : (n + 1) * TABLE_PAD
            ].astype(BF)
    keys = whole_ref[0, KEYS_AT:, :HEADS]
    table = table_ref[...].astype(F32)
    grads = lax.dot_general(
        keys,
        table,
        (((0,), (0,)), ((), ())),
        precision=PRECISE,
        preferred_element_type=F32,
    ).astype(BF)
    mask = head_rows(D)
    wait(1)
    low = jnp.where(mask, dot(grads, weight_ref[1], 1, 0), 0.0)
    low = jnp.sum(low, axis=0, keepdims=True) * HDIM ** (-0.5)
    low = jnp.broadcast_to(low, (HEADS, D)).astype(BF)
    wait(0)
    query_grad_ref[...] = dot(low, weight_ref[0], 1, 1)[:1]
    mixed = mix_ref[...]
    wait(2)
    key_query = value_ref[...].astype(F32)[:, ROWS_TABLE:]
    table_grad = dot(mixed, weight_ref[2], 0, 1)[:ROWS_TABLE] + lax.dot_general(
        keys,
        key_query,
        (((1,), (1,)), ((), ())),
        precision=PRECISE,
        preferred_element_type=F32,
    )
    for k in range(PIECES):
        embed_ref[:, k, :] = table_grad[k * VARS : (k + 1) * VARS]
    variable_ref[...] = table_grad[PIECES * VARS :]
    size = attend_grad_ref.shape[1]
    rows = pl.ds(pl.multiple_of(spot * size, size), size)
    rows_ref[...] = jnp.concatenate([grads.astype(F32), given_ref[...]], axis=0).T
    turned_ref[...] = table.T
    own = rows_ref[rows, :]
    low = low.astype(F32)
    spread = jnp.where(mask, query_ref[...] * HDIM ** (-0.5), 0.0)
    attend_grad_ref[0] = own[:, HEADS : HEADS + 1] * low[:1]
    attend_grad_ref[1] = lax.dot_general(
        own[:, :HEADS],
        spread,
        (((1,), (0,)), ((), ())),
        precision=PRECISE,
        preferred_element_type=F32,
    )
    left = jnp.concatenate(
        [turned_ref[rows, :], jnp.zeros((size, TABLE_PAD - ROWS_TABLE), F32)], axis=1
    ).astype(BF)
    attend_grad_ref[2] = dot(left, mixed, 1, 1)


def finish(place, tail, table, query, given, value, weights, brought, chips, size):
    return pl.pallas_call(
        functools.partial(finish_kernel, chips),
        out_shape=(
            shape((PATCHES, D), F32),
            shape((2, D), F32),
            shape((2, D), F32),
            shape((1, D), F32),
            shape((FF // D, D), F32),
            shape((VARS, PIECES, D), F32),
            shape((VARS, D), F32),
            shape((3, size, D), F32),
            shape((1, D), F32),
        ),
        in_specs=[SMEM] + [VMEM] * 5 + [ANYWHERE] * 7,
        out_specs=(VMEM,) * 9,
        scratch_shapes=[
            pltpu.VMEM((3, D, D), BF),
            pltpu.VMEM((2, TAIL, HALF), F32),
            pltpu.VMEM((D, TABLE_PAD), BF),
            pltpu.VMEM((D, 2 * HEADS), F32),
            pltpu.VMEM((D, ROWS_TABLE), F32),
            pltpu.SemaphoreType.DMA((3, 4)),
        ],
        compiler_params=params(),
        cost_estimate=cost(),
        name="finish",
    )(place, tail, table, query, given, value, weights, *brought)


def partner(block, axis, distance):
    size = lax.axis_size(axis)
    return lax.ppermute(block, axis, [(i, i ^ distance) for i in range(size)])


def swap(block):
    return partner(block, "pipe", 1)


def pick(array, index, axis=0):
    return lax.dynamic_index_in_dim(array, index, axis, keepdims=False)


def tree_sum(terms):
    while len(terms) > 1:
        terms = [terms[2 * i] + terms[2 * i + 1] for i in range(len(terms) // 2)]
    return terms[0]


class Places:
    def __init__(self):
        self.pipe = lax.axis_index("pipe")
        self.dp = lax.axis_index("dp")
        self.size = lax.axis_size("dp")
        self.core = self.dp % 2
        self.chips = self.size // 2
        bits = self.size.bit_length() - 2
        low = bits % 2 if bits % 2 else 2
        self.groups = []
        at = 1
        while bits > 0:
            width = low if at == 1 else 2
            self.groups.append((at, width))
            at += width
            bits -= width

    def relative(self, array, place):
        for bit in range(array.shape[0].bit_length() - 1):
            paired = array.reshape(-1, 2, 2**bit, *array.shape[1:])
            flipped = jnp.where((place // 2**bit) % 2 == 1, paired[:, ::-1], paired)
            array = flipped.reshape(array.shape)
        return array

    def grouped(self, array):
        counts = [2**width for _, width in reversed(self.groups)]
        dims = array.shape[1:]
        array = array.reshape(*counts, *dims)
        order = list(range(len(counts)))[::-1] + list(range(len(counts), array.ndim))
        return array.transpose(order)

    def reduced(self, array, groups):
        for n, (at, width) in enumerate(groups):
            terms = [array[0].astype(F32)]
            for distance in range(1, 2**width):
                terms.append(partner(array[distance], "dp", distance * 2**at).astype(F32))
            array = tree_sum(terms)
            if n < len(groups) - 1:
                array = array.astype(BF)
        return array

    def over_cores(self, array):
        brought = partner(pick(array, 1 - self.core).astype(BF), "dp", 1).astype(F32)
        own = pick(array, self.core)
        return jnp.concatenate(
            [jnp.where(self.core == 0, own, brought), jnp.where(self.core == 0, brought, own)],
            axis=-1,
        )

    def last(self, parts, group):
        terms = [parts[0].astype(F32)]
        for distance in range(1, 2 ** group[1]):
            terms.append(partner(parts[distance], "dp", distance * 2 ** group[0]).astype(F32))
        return tree_sum(terms)

    def gather(self, block):
        blocks = block[None]
        for at, width in reversed(self.groups):
            parts = [partner(blocks, "dp", m * 2**at) for m in range(1, 2**width)]
            blocks = jnp.stack([blocks] + parts, axis=1).reshape(-1, *block.shape)
        return blocks

    def round(self, block, bit):
        return block + partner(block, "dp", 2**bit)


def on_device(
    fields,
    item_weights,
    live_counts,
    running_stats,
    embed_weight,
    variable_embed,
    variable_query,
    attend_weight,
    merge_weight,
    position_embed,
    norm_gain,
    norm_bias,
    up_weight,
    hidden_bias,
    down_weight,
    output_bias,
    cotangent,
):
    at = Places()
    pipe, core = at.pipe, at.core
    first = pipe == 0
    side = (at.dp // 2) % 2
    chip = at.dp // 2
    place = jnp.stack([pipe, core, side]).astype(jnp.int32)
    micro, half_vars, rows, cols = fields.shape
    scale_heads = HDIM ** (-0.5)

    own_attend, own_merge = attend_weight[0], merge_weight[0]

    def quarter(weight):
        return lax.dynamic_slice_in_dim(weight, (2 * core + side) * QUARTER, QUARTER, 0)

    def quarter_of(j):
        start = (jnp.int32(j), (2 * core + side) * QUARTER, jnp.int32(0))
        return lax.dynamic_slice(own_attend, start, (1, QUARTER, D))[0]

    def after(value, *others):
        return lax.optimization_barrier((value, others))[0]

    def passed_on(block, before, behind):
        other = partner(after(block, *before), "dp", 2)
        pair = jnp.stack([block, after(other, *behind)])
        return pair, partner(pair, "dp", 1)

    chunk_first = swap(jnp.where(first, quarter(own_merge), quarter_of(0)))

    table = jnp.concatenate(
        [embed_weight.transpose(1, 0, 2).reshape(VARS * PIECES, D), variable_embed], axis=0
    )
    given = variable_query.astype(F32).reshape(1, D)
    query, table_keys, table_value = tables(given, table, own_attend)

    def from_first(block):
        return jnp.where(first, block, lax.ppermute(block, "pipe", [(0, 1)]))

    keys = from_first(table_keys)
    tvt = from_first(table_value.astype(BF))

    flat_fields = fields.reshape(micro, half_vars * rows, cols)
    other_fields = swap(pick(flat_fields, 1 - pipe))
    own_fields = pick(flat_fields, pipe)
    slots = jnp.arange(micro, dtype=jnp.int32)
    alive = (slots < live_counts[0]).astype(F32)
    omega = item_weights.astype(F32) * alive
    plain_sums = jnp.sum(fields, axis=(2, 3))
    square_sums = jnp.sum(fields * fields, axis=(2, 3))
    sums = jnp.concatenate(
        [
            jnp.sum(omega[:, None] * plain_sums, axis=0),
            jnp.sum(omega[:, None] * square_sums, axis=0),
            jnp.sum(omega)[None],
            jnp.sum(alive)[None],
        ]
    )
    sums = sums_y = at.round(after(sums, table_value), 1)
    for bit in range(2, at.size.bit_length() - 1):
        sums = at.round(sums, bit)
    second = swap(after(jnp.where(first, quarter_of(2), quarter_of(1)), chunk_first))
    sums = at.round(after(sums, second), 0)
    total, live_total = sums[2 * half_vars], sums[2 * half_vars + 1]
    first_moment = sums[:half_vars] / (total * rows * cols)
    second_moment = sums[half_vars : 2 * half_vars] / (total * rows * cols)
    center_new = (1.0 - MOMENTUM) * running_stats[0] + MOMENTUM * first_moment
    spread_new = (1.0 - MOMENTUM) * running_stats[1] + MOMENTUM * (
        second_moment - first_moment * first_moment
    )
    statistics = jnp.stack([center_new, spread_new])
    other_statistics = swap(statistics)
    all_statistics = jnp.concatenate(
        [
            jnp.where(first, statistics, other_statistics),
            jnp.where(first, other_statistics, statistics),
        ],
        axis=1,
    )
    center = all_statistics[0].reshape(VARS, 1)
    scale = lax.rsqrt(all_statistics[1] + EPSILON).reshape(VARS, 1)
    weight_hat = pick(omega, pipe) * live_total / total
    alive_own = pick(alive, pipe)[None]
    out_low = (pick(cotangent, pipe).astype(F32) * weight_hat).astype(BF)

    passed = [passed_on(chunk_first, (sums_y,), ())]
    passed.append(passed_on(second, (), ()))
    third = swap(after(jnp.where(first, quarter_of(0), quarter_of(2)), second))
    fourth = swap(
        after(jnp.where(first, quarter_of(1), quarter(own_merge)), third, passed[0][0])
    )
    alive_own = after(alive_own, third)

    tokens, heads, shares, pixels = aggregate(
        place,
        alive_own,
        own_fields,
        other_fields,
        center,
        scale,
        keys,
        tvt,
        position_embed,
        (own_merge, *passed[0]),
    )
    passed.append(passed_on(third, (), (tokens,)))
    heads_beside = partner(heads, "dp", 1)
    brought = [block for pair in passed for block in pair]
    pack, proj, lse = attend(place, tokens, norm_gain, norm_bias, own_attend, brought)
    passed.append(passed_on(fourth, (tokens,), (lse,)))
    brought = [block for pair in passed for block in pair]
    pack_beside = partner(pack, "dp", 1)
    units, middle, second_low, hidden_sum = expand(
        place,
        tokens,
        out_low,
        norm_gain,
        norm_bias,
        pack,
        (own_merge, *brought[6:]),
        up_weight,
        hidden_bias,
        down_weight,
        heads_beside,
    )
    units_beside = partner(units, "dp", 1)
    scalars = jnp.stack([alive_own[0], weight_hat])
    result, middle_grad, branch_low, gain_second, bias_second, output_sum = contract(
        place,
        scalars,
        units,
        up_weight,
        down_weight,
        middle,
        cotangent,
        norm_gain[1:2],
        output_bias.reshape(1, D),
    )
    ff_width = FF // (2 * at.size)
    d_width = D // at.size
    direct = 2 * at.chips == BLOCKS
    wide_place = jnp.stack([pipe * SPANS + chip if direct else 0 * chip, core]).astype(jnp.int32)
    square_place = jnp.stack([pipe, chip if direct else 0 * chip]).astype(jnp.int32)
    both_units = (units, units_beside)
    down_send, down_keep = wide_grads(
        wide_place,
        out_low,
        both_units,
        0,
        True,
        (branch_low,),
        "down_grads",
    )
    up_send, up_keep = wide_grads(
        wide_place,
        second_low,
        both_units,
        1,
        False,
        (down_keep,),
        "up_grads",
    )
    right_own, right_send, token_grad, gain_first, bias_first = attend_back(
        place,
        middle_grad,
        branch_low,
        proj,
        lse,
        tokens,
        norm_gain,
        own_attend,
        own_merge,
        brought,
        (down_keep, up_keep),
    )
    right_beside = partner(right_send, "dp", 1)
    tail_own, tail_send, field_grads = aggregate_back(
        place,
        alive_own,
        token_grad,
        pixels,
        keys,
        tvt,
        shares,
        (gain_first, gain_second, bias_first, bias_second, output_sum, hidden_sum),
        (own_merge, *passed[0]),
    )
    tail_beside = partner(tail_send, "dp", 1)

    if direct:
        groups = at.groups[1:]
        down_came, up_came = swap(down_send), partner(up_send, "dp", 2)
        down_next, up_next = first_sums(down_keep, down_came, up_keep, up_came, tail_own)
        down_brought = partner(down_next, "dp", 2)
        up_brought = swap(up_next)
        started = (down_next, up_next)
    else:
        groups = at.groups
        started = (down_keep, up_keep)

        def spread(array):
            array = array.transpose(4, 0, 1, 2, 3, 5).reshape(HALF, 2 * at.chips, -1)
            array = at.relative(array.transpose(1, 0, 2), pipe * at.chips + chip)
            array = array.reshape(2, at.chips, HALF, -1)
            total = array[0].astype(F32) + swap(array[1]).astype(F32)
            return at.grouped(total.astype(BF))

        down_wide = jnp.stack([down_keep, down_send]).transpose(0, 2, 3, 1, 4, 5)
        wide = [spread(down_wide), spread(jnp.stack([up_keep, up_send], axis=3))]

    send, keep, cross_send, cross_keep = square_grads(
        square_place,
        (tail_own, tail_beside),
        (heads, heads_beside),
        (pack, pack_beside),
        (right_own, right_beside),
        started,
    )
    if direct:
        wide = second_sums(
            down_keep, down_came, down_brought, up_keep, up_came, up_brought, send
        )
        shared = partner(after(send, wide), "dp", 2)
        crossed = swap(after(cross_send, wide))
        wide = at.last(wide, groups[0])
        cross_next = third_sums(cross_keep, crossed)
        cross_brought = partner(cross_next, "dp", 2)
        field_grads, result = after((field_grads, result), cross_next)
        came = swap(jnp.where(first, result, tokens))
        field_halves = field_grads.reshape(2, half_vars, rows, cols)
        field_came = swap(pick(field_halves, 1 - pipe).astype(BF)).astype(F32)
        square = fourth_sums(
            keep, shared, cross_keep, crossed, cross_brought, (came, field_came, wide)
        )
        square = at.last(square, groups[0])
    else:
        wide = jnp.stack([at.reduced(array, groups) for array in wide])

        def rows_of(array):
            return at.relative(array.reshape(at.chips, -1, HALF), chip)

        whole = jnp.stack([keep, send], axis=1).reshape(SPANS, PARTS, HALF)
        cross = (cross_keep.astype(F32) + swap(cross_send).astype(F32)).astype(BF)
        cross = cross.transpose(1, 0, 2, 3).reshape(SPANS, CROSS, HALF)
        square = [rows_of(whole[:, n * ROWS : (n + 1) * ROWS]) for n in range(4)]
        square.append(rows_of(cross))
        square = at.reduced(at.grouped(jnp.concatenate(square, axis=1)), groups)
        came = swap(jnp.where(first, result, tokens))
        field_halves = field_grads.reshape(2, half_vars, rows, cols)
        field_came = swap(pick(field_halves, 1 - pipe).astype(BF)).astype(F32)

    wide = wide.reshape(2, HALF, 2, ff_width)
    other = partner(pick(wide, 1 - core, 2).astype(BF), "dp", 1).astype(F32)
    own = pick(wide, core, 2)
    wide = jnp.concatenate(
        [jnp.where(core == 0, own, other), jnp.where(core == 0, other, own)], axis=1
    )
    down_part, up_part = wide[0].T, wide[1]

    lot = 2 * d_width
    part = TAIL // at.chips
    query_part = square[:lot]
    tail = square[lot : lot + part]
    merge_one = square[lot + part : 2 * lot + part]
    merge_two = square[2 * lot + part : 3 * lot + part]
    cross = square[3 * lot + part :]
    tail_came = swap(tail.astype(BF)).astype(F32)
    sent = jnp.concatenate(
        [jnp.where(first, merge_two, merge_one), query_part, cross], axis=0
    ).astype(BF)
    section_came = swap(sent).astype(F32)
    section_sum = jnp.stack(
        [
            jnp.where(first, merge_one, merge_two) + section_came[:lot],
            query_part + section_came[lot : 2 * lot],
            section_came[2 * lot :],
            cross,
        ]
    )
    tail = (tail.astype(BF).astype(F32) + tail_came).astype(BF)
    section_sum = section_sum.reshape(4, 2, d_width, HALF).transpose(1, 0, 2, 3)
    section_part = at.over_cores(section_sum)
    merge_part = section_part[0]
    second_attend = section_part[1:]

    tail = at.gather(tail)
    tail = jnp.stack([tail, partner(tail, "dp", 1)])
    spot = jnp.stack([pipe, core, side, chip, at.dp]).astype(jnp.int32)
    (
        position_sum,
        gain_sum,
        bias_sum,
        output_sum,
        hidden_sum,
        embed_grads,
        variable_grads,
        first_attend,
        query_sum,
    ) = finish(
        spot,
        tail,
        table,
        query,
        jnp.broadcast_to(given, (HEADS, D)),
        tvt,
        own_attend,
        [*passed[2], *passed[3], *passed[1]],
        at.chips,
        d_width,
    )
    attend_part = jnp.where(first, first_attend, second_attend)
    hidden_sum = hidden_sum.reshape(FF)

    outputs = jnp.stack([jnp.where(first, tokens, came), jnp.where(first, came, result)])
    field_own = pick(field_halves, pipe)
    own_scale = lax.rsqrt(spread_new + EPSILON)
    field_out = (
        jnp.stack(
            [
                jnp.where(first, field_own, field_came),
                jnp.where(first, field_came, field_own),
            ]
        )
        * own_scale[None, :, None, None]
    )
    hidden_part = lax.dynamic_slice_in_dim(
        hidden_sum, (pipe * at.size + at.dp) * ff_width, ff_width
    )
    return (
        statistics,
        outputs[None],
        field_out,
        embed_grads,
        variable_grads,
        query_sum.reshape(D),
        attend_part[None],
        merge_part[None],
        position_sum,
        gain_sum,
        bias_sum,
        up_part,
        hidden_part,
        down_part,
        output_sum.reshape(D),
    )


def solution(mesh):
    return jax.shard_map(
        on_device,
        mesh=mesh,
        in_specs=(
            P("dp", "pipe", None, None),
            P("dp"),
            P("dp"),
            P(None, "pipe"),
            P(),
            P(),
            P(),
            P("pipe", None, None, None),
            P("pipe", None, None),
            P(),
            P(),
            P(),
            P(),
            P(),
            P(),
            P(),
            P("dp", None, None),
        ),
        out_specs=(
            P(None, "pipe"),
            P("pipe", "dp", None, None),
            P("dp", "pipe", None, None),
            P(),
            P(),
            P(),
            P("pipe", None, "dp", None),
            P("pipe", "dp", None),
            P(),
            P(),
            P(),
            P(None, ("pipe", "dp")),
            P(("pipe", "dp")),
            P(("pipe", "dp"), None),
            P(),
        ),
        check_vma=False,
    )
```

```python
import functools

import jax
import jax.numpy as jnp
from jax import lax
from jax.experimental import pallas as pl
from jax.experimental.pallas import tpu as pltpu
from jax.sharding import PartitionSpec as P

D = 1024
HEADS = 16
HDIM = 64
FF = 4096
VARS = 48
PATCH = 2
PATCHES = 512
PIECES = PATCH * PATCH
ROWS_TABLE = VARS * (PIECES + 1)
HALF = D // 2
QUARTER = D // 4
TABLE_PAD = 256
FF_TILE = 1024
FF_STEPS = FF // FF_TILE
PAIRS = HEADS // 2
LANES = 2 * HDIM
CHUNK = 128
TOKENS_BACK = 2
UNROLL = 2
UNROLL_PAIR = 1

PRECISE = lax.Precision.HIGHEST
EPSILON = 1e-05
MOMENTUM = 0.1
BF = jnp.bfloat16
F32 = jnp.float32
VMEM_LIMIT = 56 * 1024 * 1024


def dot(left, right, left_dim, right_dim):
    return lax.dot_general(
        left, right, (((left_dim,), (right_dim,)), ((), ())), preferred_element_type=F32
    )


VMEM = pl.BlockSpec(memory_space=pltpu.VMEM)
SMEM = pl.BlockSpec(memory_space=pltpu.SMEM)
ANYWHERE = pl.BlockSpec(memory_space=pl.ANY)


def shape(dims, kind):
    return jax.ShapeDtypeStruct(dims, kind)


def params(grid=0):
    semantics = ("arbitrary",) * grid if grid else None
    return pltpu.CompilerParams(vmem_limit_bytes=VMEM_LIMIT, dimension_semantics=semantics)


def cost():
    return pl.CostEstimate(flops=1000, bytes_accessed=1000, transcendentals=0)


def section_copies(place_ref, section, own, brought, targets, sems):
    core, side = place_ref[1], place_ref[2]

    def rows(core, side):
        return pl.ds(pl.multiple_of((2 * core + side) * QUARTER, QUARTER), QUARTER)

    @pl.when(place_ref[0] == section)
    def _():
        for n, target in enumerate(targets):
            for quarter in range(4):
                part = pl.ds(quarter * QUARTER, QUARTER)
                pltpu.make_async_copy(
                    own[n].at[part], target.at[part], sems.at[n, quarter]
                ).start()

    @pl.when(place_ref[0] != section)
    def _():
        for n, target in enumerate(targets):
            for other in range(2):
                for turn in range(2):
                    place = rows(core + other - 2 * core * other, side + turn - 2 * side * turn)
                    pltpu.make_async_copy(
                        brought[n][other].at[turn], target.at[place], sems.at[n, 2 * other + turn]
                    ).start()

    def wait(n):
        for quarter in range(4):
            part = pl.ds(quarter * QUARTER, QUARTER)
            pltpu.make_async_copy(
                brought[n][0].at[0], targets[n].at[part], sems.at[n, quarter]
            ).wait()

    return wait


def normalized(values):
    center = values - jnp.mean(values, axis=-1, keepdims=True)
    spread = jnp.mean(center * center, axis=-1, keepdims=True)
    inverse = lax.rsqrt(spread + EPSILON)
    return center * inverse, inverse


def norm_back(xhat, inverse, gain, grad):
    scaled = grad * gain
    first = jnp.mean(scaled, axis=-1, keepdims=True)
    second = jnp.mean(scaled * xhat, axis=-1, keepdims=True)
    return (scaled - first - xhat * second) * inverse


def row_chunks(body):
    def step(i, carry):
        body(pl.ds(pl.multiple_of(i * CHUNK, CHUNK), CHUNK))
        return carry

    lax.fori_loop(0, PATCHES // CHUNK, step, 0)


def column_tiles(width, body):
    def step(i, carry):
        body(pl.ds(pl.multiple_of(i * width, width), width))
        return carry

    lax.fori_loop(0, D // width, step, 0)


def head_rows(width):
    row = lax.broadcasted_iota(jnp.int32, (HEADS, width), 0)
    column = lax.broadcasted_iota(jnp.int32, (HEADS, width), 1)
    start = row * HDIM
    return (column >= start) & (column < start + HDIM)


def tables_kernel(query_ref, table_ref, weight_ref, low_ref, keys_ref, value_ref):
    given = jnp.broadcast_to(query_ref[...], (HEADS, D)).astype(BF)
    query = dot(given, weight_ref[0], 1, 0).astype(BF).astype(F32)
    low_ref[...] = query
    spread = jnp.where(head_rows(D), query, 0.0).astype(BF)
    key_query = (dot(spread, weight_ref[1], 1, 1) * HDIM ** (-0.5)).astype(BF)
    keys_ref[...] = dot(table_ref[...], key_query, 1, 1)
    values = dot(table_ref[...], weight_ref[2], 1, 0)
    value_ref[...] = jnp.concatenate([values, key_query.astype(F32)], axis=0).T


def tables(query, table, weights):
    return pl.pallas_call(
        tables_kernel,
        out_shape=(
            shape((HEADS, D), F32),
            shape((ROWS_TABLE, HEADS), F32),
            shape((D, TABLE_PAD), F32),
        ),
        in_specs=[VMEM] * 3,
        out_specs=(VMEM,) * 3,
        compiler_params=params(),
        cost_estimate=cost(),
        name="tables",
    )(query, table, weights)


COLS = 128
STRIPES = 16


def column_order():
    row = lax.broadcasted_iota(jnp.int32, (COLS, COLS), 0)
    column = lax.broadcasted_iota(jnp.int32, (COLS, COLS), 1)
    place = jnp.where(column < COLS // 2, 2 * column, 2 * column - COLS + 1)
    return (row == place).astype(F32)


def exact(left, right, right_dim):
    return lax.dot_general(
        left,
        right,
        (((1,), (right_dim,)), ((), ())),
        precision=PRECISE,
        preferred_element_type=F32,
    )


def head_keys(keys_ref, h):
    keys = keys_ref[...]
    lane = lax.broadcasted_iota(jnp.int32, keys.shape, 1)
    return jnp.sum(jnp.where(lane == h, keys, 0.0), axis=1, keepdims=True)


def mixed_rows(shares, pixels_ref):
    return jnp.concatenate(
        [(shares * pixels_ref[k]).astype(BF) for k in range(PIECES)]
        + [shares.astype(BF), jnp.zeros((TABLE_PAD - ROWS_TABLE, PATCHES), BF)],
        axis=0,
    )


def aggregate_kernel(
    place_ref,
    alive_ref,
    own_field_ref,
    other_field_ref,
    center_ref,
    scale_ref,
    keys_ref,
    tvt_ref,
    position_ref,
    own_ref,
    brought_ref,
    beside_ref,
    tokens_ref,
    heads_ref,
    shares_ref,
    pixels_ref,
    merge_ref,
    grid_ref,
    sems,
):
    wait = section_copies(
        place_ref, 0, [own_ref], [(brought_ref, beside_ref)], [merge_ref], sems
    )
    alive = alive_ref[0]
    order = column_order()
    half = VARS // 2 * STRIPES
    own, other = own_field_ref[...], other_field_ref[...]
    grid_ref[:half] = exact(jnp.where(place_ref[0] == 0, own, other), order, 0)
    grid_ref[half:] = exact(jnp.where(place_ref[0] == 0, other, own), order, 0)
    center, scale = center_ref[...], scale_ref[...]
    low_lane = lax.broadcasted_iota(jnp.int32, (VARS, COLS), 1) < COLS // 2

    def stripe(r):
        values = grid_ref[pl.ds(r, VARS, stride=STRIPES), :]
        return ((values - center) * scale).astype(BF).astype(F32)

    for a in range(PATCH):
        for j in range(PATCHES // COLS):
            even, odd = stripe(4 * j + a), stripe(4 * j + 2 + a)
            columns = slice(j * COLS, (j + 1) * COLS)
            pixels_ref[2 * a, :, columns] = jnp.where(
                low_lane, even, pltpu.roll(odd, COLS // 2, 1)
            )
            pixels_ref[2 * a + 1, :, columns] = jnp.where(
                low_lane, pltpu.roll(even, COLS // 2, 1), odd
            )

    def head(h, carry):
        keys = head_keys(keys_ref, h)
        scores = keys[PIECES * VARS :]
        for k in range(PIECES):
            scores = scores + keys[k * VARS : (k + 1) * VARS] * pixels_ref[k]
        top = jnp.max(scores, axis=0, keepdims=True)
        powers = jnp.exp(scores - top)
        shares = powers / jnp.sum(powers, axis=0, keepdims=True)
        shares_ref[h] = shares
        rows = pl.ds(pl.multiple_of(h * HDIM, HDIM), HDIM)
        heads_ref[rows, :] = dot(tvt_ref[rows, :], mixed_rows(shares, pixels_ref), 1, 0).astype(
            BF
        )
        return carry

    lax.fori_loop(0, HEADS, head, 0, unroll=UNROLL)
    wait(0)
    heads = heads_ref[...].T

    def tile(columns):
        merged = dot(heads, merge_ref[:, columns], 1, 0)
        tokens_ref[:, columns] = (alive * (merged + position_ref[:, columns].astype(F32))).astype(
            BF
        )

    column_tiles(256, tile)


def aggregate(place, alive, own_field, other_field, center, scale, keys, tvt, position, merge):
    return pl.pallas_call(
        aggregate_kernel,
        out_shape=(
            shape((PATCHES, D), BF),
            shape((D, PATCHES), BF),
            shape((HEADS, VARS, PATCHES), F32),
            shape((PIECES, VARS, PATCHES), F32),
        ),
        in_specs=[SMEM, SMEM] + [VMEM] * 7 + [ANYWHERE] * 3,
        out_specs=(VMEM,) * 4,
        scratch_shapes=[
            pltpu.VMEM((D, D), BF),
            pltpu.VMEM((VARS * STRIPES, COLS), F32),
            pltpu.SemaphoreType.DMA((1, 4)),
        ],
        compiler_params=params(),
        cost_estimate=cost(),
        name="aggregate",
    )(place, alive, own_field, other_field, center, scale, keys, tvt, position, *merge)


def attend_kernel(place_ref, tokens_ref, gain_ref, bias_ref, attend_ref, *refs):
    brought = [(refs[2 * n], refs[2 * n + 1]) for n in range(3)]
    pack_ref, proj_ref, lse_ref, weight_ref, first_ref, sems = refs[6:]
    wait = section_copies(
        place_ref,
        1,
        [attend_ref.at[j] for j in range(3)],
        brought,
        [weight_ref.at[j] for j in range(3)],
        sems,
    )

    def first_norm(rows):
        xhat, _ = normalized(tokens_ref[rows, :].astype(F32))
        first_ref[rows, :] = (xhat * gain_ref[0:1, :] + bias_ref[0:1, :]).astype(BF)

    row_chunks(first_norm)
    pack_ref[:D, :] = first_ref[...].T
    for j in range(3):
        wait(j)
        column_tiles(
            256,
            lambda columns: proj_ref.__setitem__(
                (j, slice(None), columns),
                dot(first_ref[...], weight_ref[j, :, columns], 1, 0).astype(BF),
            ),
        )

    lane = lax.broadcasted_iota(jnp.int32, (PATCHES, LANES), 1)

    def pair(i, carry):
        columns = pl.ds(pl.multiple_of(i * LANES, LANES), LANES)
        queries = proj_ref[0, :, columns]
        keys = proj_ref[1, :, columns]
        values = proj_ref[2, :, columns].T
        for side in range(2):
            inside = (lane < HDIM) if side == 0 else (lane >= HDIM)
            key = jnp.where(inside, keys * HDIM ** (-0.5), jnp.zeros_like(keys)).astype(BF)
            scores = dot(key, queries, 1, 1)
            top = jnp.max(scores, axis=0, keepdims=True)
            powers = jnp.exp(scores - top)
            whole = jnp.sum(powers, axis=0, keepdims=True)
            probs = (powers * (1.0 / whole)).astype(BF)
            lse_ref[i, side : side + 1, :] = top + jnp.log(whole)
            value = values[side * HDIM : (side + 1) * HDIM]
            rows = pl.ds(pl.multiple_of(D + i * LANES + side * HDIM, HDIM), HDIM)
            pack_ref[rows, :] = dot(value, probs, 1, 0).astype(BF)
        return carry

    lax.fori_loop(0, PAIRS, pair, 0, unroll=UNROLL_PAIR)


def attend(place, tokens, gain, bias, own_attend, brought):
    return pl.pallas_call(
        attend_kernel,
        out_shape=(
            shape((2 * D, PATCHES), BF),
            shape((3, PATCHES, D), BF),
            shape((PAIRS, 2, PATCHES), F32),
        ),
        in_specs=[SMEM] + [VMEM] * 3 + [ANYWHERE] * 7,
        out_specs=(VMEM,) * 3,
        scratch_shapes=[
            pltpu.VMEM((3, D, D), BF),
            pltpu.VMEM((PATCHES, D), BF),
            pltpu.SemaphoreType.DMA((3, 4)),
        ],
        compiler_params=params(),
        cost_estimate=cost(),
        name="attend",
    )(place, tokens, gain, bias, own_attend, *brought)


def gelu_parts(hidden):
    inverse = 1.0 / (1.0 + 0.23164190 * jnp.abs(hidden))
    decay = jnp.exp2(hidden * hidden * (-0.72134752))
    series = 0.5 * 1.061405429
    for factor in (-1.453152027, 1.421413741, -0.284496736, 0.254829592):
        series = series * inverse + 0.5 * factor
    tail = series * inverse * decay
    cdf = jnp.where(hidden >= 0.0, 1.0 - tail, tail)
    return cdf, decay * 0.3989422804014327


FF_PART = 1024
UNITS = FF + HALF


def copy(source, target, sem):
    return pltpu.make_async_copy(source, target, sem)


def aligned(index, size):
    return pl.ds(pl.multiple_of(index * size, size), size)


def start_either(choice, source, if_true, if_false, sem):
    @pl.when(choice)
    def _():
        copy(source, if_true, sem).start()

    @pl.when(jnp.logical_not(choice))
    def _():
        copy(source, if_false, sem).start()


def expand_kernel(
    place_ref,
    tokens_ref,
    out_ref,
    gain_ref,
    norm_bias_ref,
    bias_ref,
    pack_any,
    own_any,
    brought_any,
    beside_any,
    up_any,
    down_any,
    after_any,
    units_any,
    middle_any,
    second_any,
    sum_ref,
    up_ref,
    down_ref,
    tile_ref,
    merge_ref,
    context_ref,
    middle_ref,
    second_ref,
    merge_sems,
    in_sems,
    out_sems,
):
    def fetch(j):
        part = aligned(j, FF_TILE)
        return (
            copy(up_any.at[:, part], up_ref.at[:, part], in_sems.at[j, 0]),
            copy(down_any.at[part], down_ref.at[part], in_sems.at[j, 1]),
        )

    def start(j):
        for one in fetch(j):
            one.start()

    def put(j, slot):
        return copy(
            tile_ref.at[slot], units_any.at[:, :, aligned(j, FF_TILE)], out_sems.at[slot]
        )

    context = copy(pack_any.at[pl.ds(D, D)], context_ref, in_sems.at[FF_STEPS, 0])
    context.start()
    wait = section_copies(
        place_ref, 1, [own_any], [(brought_any, beside_any)], [merge_ref], merge_sems
    )
    start(0)
    context.wait()
    turned = context_ref[...].T
    wait(0)
    column_tiles(
        512,
        lambda columns: middle_ref.__setitem__(
            (slice(None), columns),
            tokens_ref[:, columns].astype(F32) + dot(turned, merge_ref[:, columns], 1, 0),
        ),
    )
    middle_out = copy(middle_ref, middle_any, in_sems.at[FF_STEPS, 1])
    middle_out.start()
    start(1)

    def second_norm(rows):
        xhat, _ = normalized(middle_ref[rows, :])
        second_ref[rows, :] = (xhat * gain_ref[1:2, :] + norm_bias_ref[1:2, :]).astype(BF)

    row_chunks(second_norm)
    second_out = copy(second_ref, second_any, out_sems.at[2])
    second_out.start()

    def step(j, carry):
        slot = lax.rem(j, 2)

        @pl.when(j + 2 < FF_STEPS)
        def _():
            start(j + 2)

        @pl.when(j >= 2)
        def _():
            put(j - 2, slot).wait()

        for one in fetch(j):
            one.wait()
        for part in range(FF_TILE // FF_PART):
            inner = slice(part * FF_PART, (part + 1) * FF_PART)
            begin = pl.multiple_of(j * FF_TILE + part * FF_PART, FF_PART)
            columns = pl.ds(begin, FF_PART)
            hidden = dot(second_ref[...], up_ref[:, columns], 1, 0) + bias_ref[:, columns]
            grad = dot(out_ref[...], down_ref[columns, :], 1, 1)
            cdf, density = gelu_parts(hidden)
            tile_ref[slot, 0, :, inner] = (hidden * cdf).astype(BF)
            low = (grad * (cdf + hidden * density)).astype(BF)
            tile_ref[slot, 1, :, inner] = low
            sum_ref[:, columns] = jnp.sum(low.astype(F32), axis=0, keepdims=True)
        put(j, slot).start()
        return carry

    lax.fori_loop(0, FF_STEPS, step, 0)
    others = aligned(1 - place_ref[1], HALF)
    put(FF_STEPS - 2, 0).wait()
    tile_ref[0, 0, :, :HALF] = out_ref[:, others]
    tile_ref[0, 1, :, :HALF] = second_ref[:, others]
    end = copy(
        tile_ref.at[0, :, :, pl.ds(0, HALF)], units_any.at[:, :, pl.ds(FF, HALF)], out_sems.at[0]
    )
    end.start()
    middle_out.wait()
    second_out.wait()
    put(FF_STEPS - 1, 1).wait()
    end.wait()


def expand(place, tokens, out_low, gain, norm_bias, pack, merge, up, bias, down, after):
    return pl.pallas_call(
        expand_kernel,
        out_shape=(
            shape((2, PATCHES, UNITS), BF),
            shape((PATCHES, D), F32),
            shape((PATCHES, D), BF),
            shape((1, FF), F32),
        ),
        in_specs=[SMEM] + [VMEM] * 5 + [ANYWHERE] * 7,
        out_specs=(ANYWHERE, ANYWHERE, ANYWHERE, VMEM),
        scratch_shapes=[
            pltpu.VMEM((D, FF), BF),
            pltpu.VMEM((FF, D), BF),
            pltpu.VMEM((2, 2, PATCHES, FF_TILE), BF),
            pltpu.VMEM((D, D), BF),
            pltpu.VMEM((D, PATCHES), BF),
            pltpu.VMEM((PATCHES, D), F32),
            pltpu.VMEM((PATCHES, D), BF),
            pltpu.SemaphoreType.DMA((1, 4)),
            pltpu.SemaphoreType.DMA((FF_STEPS + 1, 2)),
            pltpu.SemaphoreType.DMA((3,)),
        ],
        compiler_params=params(),
        cost_estimate=cost(),
        name="expand",
    )(place, tokens, out_low, gain, norm_bias, bias.reshape(1, FF), pack, *merge, up, down, after)


DEPTHS = 4
DEPTH = FF // DEPTHS


def contract_kernel(
    place_ref,
    scalars_ref,
    gain_ref,
    bias_ref,
    units_any,
    up_any,
    down_any,
    middle_any,
    cotangent_any,
    result_ref,
    grad_ref,
    branch_ref,
    gain_grad_ref,
    bias_grad_ref,
    out_grad_ref,
    units_ref,
    up_ref,
    down_ref,
    middle_ref,
    cotangent_ref,
    total_ref,
    second_ref,
    sems,
):
    def fetch(n):
        which, c = divmod(n, DEPTHS)
        part = slice(c * DEPTH, (c + 1) * DEPTH)
        if which == 0:
            weight = copy(down_any.at[part], down_ref.at[part], sems.at[n, 1])
        else:
            weight = copy(up_any.at[:, part], up_ref.at[:, part], sems.at[n, 1])
        return (
            copy(units_any.at[which, :, part], units_ref.at[which, :, part], sems.at[n, 0]),
            weight,
        )

    rest = (
        copy(middle_any, middle_ref, sems.at[2 * DEPTHS, 0]),
        copy(cotangent_any.at[place_ref[0]], cotangent_ref, sems.at[2 * DEPTHS, 1]),
    )
    for n in range(2):
        for one in fetch(n):
            one.start()
    for n in range(2 * DEPTHS):
        which, c = divmod(n, DEPTHS)
        part = slice(c * DEPTH, (c + 1) * DEPTH)
        for one in fetch(n + 2) if n + 2 < 2 * DEPTHS else rest if n + 2 == 2 * DEPTHS else ():
            one.start()
        for one in fetch(n):
            one.wait()
        ref = second_ref if which else total_ref
        if which:
            product = dot(units_ref[1, :, part], up_ref[:, part], 1, 1)
        else:
            product = dot(units_ref[0, :, part], down_ref[part, :], 1, 0)
        if c:
            ref[...] += product
        else:
            ref[...] = product
    for one in rest:
        one.wait()
    alive, hat = scalars_ref[0], scalars_ref[1]
    gain_grad_ref[...] = jnp.zeros_like(gain_grad_ref)
    bias_grad_ref[...] = jnp.zeros_like(bias_grad_ref)
    out_grad_ref[...] = jnp.zeros_like(out_grad_ref)

    def chunk(rows):
        middle = middle_ref[rows, :]
        result_ref[rows, :] = (alive * (middle + total_ref[rows, :] + bias_ref[...])).astype(BF)
        xhat, inverse = normalized(middle)
        grad = second_ref[rows, :]
        gain_grad_ref[...] += jnp.sum(grad * xhat, axis=0, keepdims=True)
        bias_grad_ref[...] += jnp.sum(grad, axis=0, keepdims=True)
        out = cotangent_ref[rows, :].astype(F32) * hat
        out_grad_ref[...] += jnp.sum(out, axis=0, keepdims=True)
        whole = out + norm_back(xhat, inverse, gain_ref[...], grad)
        grad_ref[rows, :] = whole
        branch_ref[rows, :] = whole.astype(BF)

    row_chunks(chunk)


def contract(place, scalars, units, up, down, middle, cotangent, gain, bias):
    return pl.pallas_call(
        contract_kernel,
        out_shape=(
            shape((PATCHES, D), BF),
            shape((PATCHES, D), F32),
            shape((PATCHES, D), BF),
            shape((1, D), F32),
            shape((1, D), F32),
            shape((1, D), F32),
        ),
        in_specs=[SMEM, SMEM, VMEM, VMEM] + [ANYWHERE] * 5,
        out_specs=(VMEM,) * 6,
        scratch_shapes=[
            pltpu.VMEM((2, PATCHES, FF), BF),
            pltpu.VMEM((D, FF), BF),
            pltpu.VMEM((FF, D), BF),
            pltpu.VMEM((PATCHES, D), F32),
            pltpu.VMEM((PATCHES, D), BF),
            pltpu.VMEM((PATCHES, D), F32),
            pltpu.VMEM((PATCHES, D), F32),
            pltpu.SemaphoreType.DMA((2 * DEPTHS + 1, 2)),
        ],
        compiler_params=params(),
        cost_estimate=cost(),
        name="contract",
    )(place, scalars, gain, bias, units, up, down, middle, cotangent)


def attend_back_kernel(
    place_ref,
    grad_ref,
    branch_ref,
    proj_ref,
    lse_ref,
    tokens_ref,
    gain_ref,
    attend_ref,
    merge_ref,
    *refs,
):
    brought = [(refs[2 * n], refs[2 * n + 1]) for n in range(4)]
    outs = refs[8 + TOKENS_BACK :]
    keep_ref, send_ref, token_grad_ref, gain_grad_ref, bias_grad_ref = outs[:5]
    weight_ref, context_ref, first_ref, proj_grad_ref, sems = outs[5:]
    wait = section_copies(
        place_ref,
        1,
        [merge_ref] + [attend_ref.at[j] for j in range(3)],
        brought[3:] + brought[:3],
        [weight_ref.at[j] for j in range(4)],
        sems,
    )
    wait(0)
    branch = branch_ref[...]

    def context_tile(columns):
        context_ref[:, columns] = dot(branch, weight_ref[0, columns, :], 1, 1).astype(BF)

    column_tiles(256, context_tile)
    lane = lax.broadcasted_iota(jnp.int32, (PATCHES, LANES), 1)

    def pair(i, carry):
        columns = pl.ds(pl.multiple_of(i * LANES, LANES), LANES)
        queries = proj_ref[0, :, columns]
        keys = proj_ref[1, :, columns]
        values = proj_ref[2, :, columns]
        grads = context_ref[:, columns]
        keys_turned = keys.T
        blank = jnp.zeros_like(keys)
        query_grads, key_grads, value_grads = [], [], []
        for side in range(2):
            inside = (lane < HDIM) if side == 0 else (lane >= HDIM)
            key = jnp.where(inside, keys * HDIM ** (-0.5), blank).astype(BF)
            value = jnp.where(inside, values, blank)
            probs = jnp.exp(dot(key, queries, 1, 1) - lse_ref[i, side : side + 1, :])
            share_grad = dot(value, grads, 1, 1)
            weighted = probs * share_grad
            inner = jnp.sum(weighted, axis=0, keepdims=True)
            score_low = (weighted - probs * inner).astype(BF)
            value_grads.append(dot(probs.astype(BF), grads, 1, 0))
            key_grads.append(dot(score_low, queries, 1, 0))
            query_grads.append(
                dot(keys_turned[side * HDIM : (side + 1) * HDIM], score_low, 1, 0)
            )
        low = lane < HDIM
        query_grad = jnp.concatenate(query_grads, axis=0) * HDIM ** (-0.5)
        proj_grad_ref[0, :, columns] = query_grad.T.astype(BF)
        proj_grad_ref[1, :, columns] = (
            jnp.where(low, key_grads[0], key_grads[1]) * HDIM ** (-0.5)
        ).astype(BF)
        proj_grad_ref[2, :, columns] = jnp.where(low, value_grads[0], value_grads[1]).astype(BF)
        return carry

    lax.fori_loop(0, PAIRS, pair, 0, unroll=UNROLL_PAIR)
    core = place_ref[1]
    owns = pl.ds(pl.multiple_of(core * HALF, HALF), HALF)
    others = pl.ds(pl.multiple_of((1 - core) * HALF, HALF), HALF)
    for j in range(3):
        keep_ref[j] = proj_grad_ref[j, :, owns]
        send_ref[j] = proj_grad_ref[j, :, others]
    keep_ref[3] = branch_ref[:, owns]
    send_ref[3] = branch_ref[:, others]
    for j in range(3):
        wait(j + 1)

    def first_tile(columns):
        total = dot(proj_grad_ref[0], weight_ref[1, columns, :], 1, 1)
        for j in range(1, 3):
            total = total + dot(proj_grad_ref[j], weight_ref[j + 1, columns, :], 1, 1)
        first_ref[:, columns] = total

    column_tiles(256, first_tile)
    gain_grad_ref[...] = jnp.zeros_like(gain_grad_ref)
    bias_grad_ref[...] = jnp.zeros_like(bias_grad_ref)

    def chunk(rows):
        xhat, inverse = normalized(tokens_ref[rows, :].astype(F32))
        grad = first_ref[rows, :]
        gain_grad_ref[...] += jnp.sum(grad * xhat, axis=0, keepdims=True)
        bias_grad_ref[...] += jnp.sum(grad, axis=0, keepdims=True)
        token_grad_ref[rows, :] = (
            grad_ref[rows, :] + norm_back(xhat, inverse, gain_ref[0:1, :], grad)
        ).astype(BF)

    row_chunks(chunk)


def attend_back(
    place, grad, branch, proj, lse, tokens, gain, own_attend, own_merge, brought, after
):
    return pl.pallas_call(
        attend_back_kernel,
        out_shape=(
            shape((4, PATCHES, HALF), BF),
            shape((4, PATCHES, HALF), BF),
            shape((PATCHES, D), BF),
            shape((1, D), F32),
            shape((1, D), F32),
        ),
        in_specs=[SMEM] + [VMEM] * 6 + [ANYWHERE] * (10 + TOKENS_BACK),
        out_specs=(VMEM,) * 5,
        scratch_shapes=[
            pltpu.VMEM((4, D, D), BF),
            pltpu.VMEM((PATCHES, D), BF),
            pltpu.VMEM((PATCHES, D), F32),
            pltpu.VMEM((3, PATCHES, D), BF),
            pltpu.SemaphoreType.DMA((4, 4)),
        ],
        compiler_params=params(),
        cost_estimate=cost(),
        name="attend_back",
    )(place, grad, branch, proj, lse, tokens, gain, own_attend, own_merge, *brought, *after)


MIX_AT = PATCHES
SMALL_AT = PATCHES + TABLE_PAD
KEYS_AT = SMALL_AT + 16
TAIL = KEYS_AT + ROWS_TABLE


def aggregate_back_kernel(
    place_ref,
    alive_ref,
    token_grad_ref,
    pixels_ref,
    keys_ref,
    tvt_ref,
    shares_ref,
    gain_first_ref,
    gain_second_ref,
    bias_first_ref,
    bias_second_ref,
    output_ref,
    hidden_ref,
    own_ref,
    brought_ref,
    beside_ref,
    keep_ref,
    send_ref,
    field_ref,
    key_grad_ref,
    head_ref,
    merge_ref,
    mix_ref,
    pixel_grad_ref,
    grid_ref,
    sems,
):
    wait = section_copies(
        place_ref, 0, [own_ref], [(brought_ref, beside_ref)], [merge_ref], sems
    )
    core = place_ref[1]
    owns = pl.ds(pl.multiple_of(core * HALF, HALF), HALF)
    others = pl.ds(pl.multiple_of((1 - core) * HALF, HALF), HALF)
    alive = alive_ref[0]
    pre = (token_grad_ref[...].astype(F32) * alive).astype(BF)
    keep_ref[:PATCHES, :] = (token_grad_ref[:, owns].astype(F32) * alive).astype(BF)
    send_ref[:PATCHES, :] = (token_grad_ref[:, others].astype(F32) * alive).astype(BF)
    wait(0)

    def head_tile(rows):
        head_ref[rows, :] = dot(merge_ref[rows, :], pre, 1, 1).astype(BF)

    column_tiles(256, head_tile)
    pixel_grad_ref[...] = jnp.zeros_like(pixel_grad_ref)
    key_grad_ref[...] = jnp.zeros_like(key_grad_ref)
    lane = lax.broadcasted_iota(jnp.int32, (VARS, HEADS), 1)

    def head(h, carry):
        rows = pl.ds(pl.multiple_of(h * HDIM, HDIM), HDIM)
        keys = head_keys(keys_ref, h)
        grads = head_ref[rows, :]
        shares = shares_ref[h]
        mix_ref[rows, :] = dot(grads, mixed_rows(shares, pixels_ref), 1, 1)
        row_grads = dot(tvt_ref[rows, :], grads, 0, 0)
        share_grads = row_grads[PIECES * VARS : ROWS_TABLE]
        for k in range(PIECES):
            share_grads = share_grads + row_grads[k * VARS : (k + 1) * VARS] * pixels_ref[k]
        inner = jnp.sum(shares * share_grads, axis=0, keepdims=True)
        scores = shares * (share_grads - inner)
        for k in range(PIECES + 1):
            piece = slice(k * VARS, (k + 1) * VARS)
            if k < PIECES:
                pixel_grad_ref[k] += shares * row_grads[piece] + scores * keys[piece]
                total = jnp.sum(scores * pixels_ref[k], axis=1, keepdims=True)
            else:
                total = jnp.sum(scores, axis=1, keepdims=True)
            key_grad_ref[piece, :] += jnp.where(lane == h, total, 0.0)
        return carry

    lax.fori_loop(0, HEADS, head, 0, unroll=UNROLL)
    for ref, start in ((keep_ref, core * HALF), (send_ref, (1 - core) * HALF)):
        for part in range(2):
            rows = pl.ds(pl.multiple_of(start + part * TABLE_PAD, TABLE_PAD), TABLE_PAD)
            ref[MIX_AT:SMALL_AT, part * TABLE_PAD : (part + 1) * TABLE_PAD] = mix_ref[
                rows, :
            ].astype(BF)
        columns = pl.ds(pl.multiple_of(start, HALF), HALF)
        small = [
            one[:, columns]
            for one in (
                gain_first_ref,
                gain_second_ref,
                bias_first_ref,
                bias_second_ref,
                output_ref,
            )
        ]
        for part in range(FF // D):
            small.append(hidden_ref[:, pl.ds(pl.multiple_of(part * D + start, HALF), HALF)])
        small.append(jnp.zeros((16 - len(small), HALF), F32))
        ref[SMALL_AT:KEYS_AT, :] = jnp.concatenate(small, axis=0).astype(BF)
        ref[KEYS_AT:, :] = jnp.concatenate(
            [key_grad_ref[...], jnp.zeros((ROWS_TABLE, HALF - HEADS), F32)], axis=1
        ).astype(BF)
    low_lane = lax.broadcasted_iota(jnp.int32, (VARS, COLS), 1) < COLS // 2
    for a in range(PATCH):
        for j in range(PATCHES // COLS):
            columns = slice(j * COLS, (j + 1) * COLS)
            low, high = pixel_grad_ref[2 * a, :, columns], pixel_grad_ref[2 * a + 1, :, columns]
            even = jnp.where(low_lane, low, pltpu.roll(high, COLS // 2, 1))
            odd = jnp.where(low_lane, pltpu.roll(low, COLS // 2, 1), high)
            grid_ref[pl.ds(4 * j + a, VARS, stride=STRIPES), :] = even
            grid_ref[pl.ds(4 * j + 2 + a, VARS, stride=STRIPES), :] = odd
    field_ref[...] = exact(grid_ref[...], column_order(), 1)


def aggregate_back(place, alive, token_grad, pixels, keys, tvt, shares, small, merge):
    return pl.pallas_call(
        aggregate_back_kernel,
        out_shape=(
            shape((TAIL, HALF), BF),
            shape((TAIL, HALF), BF),
            shape((VARS * STRIPES, COLS), F32),
        ),
        in_specs=[SMEM, SMEM] + [VMEM] * 11 + [ANYWHERE] * 3,
        out_specs=(VMEM,) * 3,
        scratch_shapes=[
            pltpu.VMEM((ROWS_TABLE, HEADS), F32),
            pltpu.VMEM((D, PATCHES), BF),
            pltpu.VMEM((D, D), BF),
            pltpu.VMEM((D, TABLE_PAD), F32),
            pltpu.VMEM((PIECES, VARS, PATCHES), F32),
            pltpu.VMEM((VARS * STRIPES, COLS), F32),
            pltpu.SemaphoreType.DMA((1, 4)),
        ],
        compiler_params=params(),
        cost_estimate=cost(),
        name="aggregate_back",
    )(place, alive, token_grad, pixels, keys, tvt, shares, *small, *merge)


BLOCKS = 16
BLOCK = FF // BLOCKS
SPANS = BLOCKS // 2
SPAN = 4 * BLOCK


def wide_kernel(which, by_pipe, place_ref, left_any, own_any, beside_any, *refs):
    send_any, keep_any, left_ref, turned_ref, right_ref, product_ref, sems, out_sems = refs[-8:]
    place, core = place_ref[0], place_ref[1]
    side, z_low = jnp.bitwise_and(place, 1), jnp.bitwise_and(lax.shift_right_logical(place, 1), 1)

    def fetch(i):
        columns = aligned(jnp.bitwise_xor(3 - i, lax.shift_right_logical(place, 2)), SPAN)
        return [
            copy(
                source.at[which, :, columns],
                right_ref.at[i, pl.ds(n * PATCHES, PATCHES)],
                sems.at[i, n],
            )
            for n, source in enumerate((own_any, beside_any))
        ]

    lefts = (
        copy(left_any.at[:, aligned(core, HALF)], left_ref.at[0], sems.at[4, 0]),
        copy(beside_any.at[which, :, pl.ds(FF, HALF)], left_ref.at[1], sems.at[4, 1]),
    )
    for one in lefts:
        one.start()
    for i in range(2):
        for one in fetch(i):
            one.start()
    for n, one in enumerate(lefts):
        one.wait()
        turned_ref[:, n * PATCHES : (n + 1) * PATCHES] = left_ref[n].T

    def put(i, block):
        source = product_ref.at[i % 2, :, pl.ds(block * BLOCK, BLOCK)]
        return source, out_sems.at[i % 2, block]

    def wait(i):
        for block in range(4):
            source, sem = put(i, block)
            copy(source, send_any.at[0, 0, 0], sem).wait()

    for i in range(4):
        for one in fetch(i + 2) if i < 2 else ():
            one.start()
        for one in fetch(i):
            one.wait()
        if i >= 2:
            wait(i - 2)
        product_ref[i % 2] = dot(turned_ref[...], right_ref[i], 1, 0).astype(BF)
        pipe, z_high = divmod(3 - i, 2)
        for block in range(4):
            source, sem = put(i, block)
            to_side = jnp.bitwise_xor(block % 2, side)
            to_z = jnp.bitwise_xor(block // 2, z_low)
            if by_pipe:
                target = send_any if pipe else keep_any
                copy(source, target.at[to_side, z_high, to_z], sem).start()
            else:
                start_either(
                    to_side == 1,
                    source,
                    send_any.at[pipe, z_high, to_z],
                    keep_any.at[pipe, z_high, to_z],
                    sem,
                )
    wait(2)
    wait(3)


def wide_grads(place, left, right, which, by_pipe, after, name):
    return pl.pallas_call(
        functools.partial(wide_kernel, which, by_pipe),
        in_specs=[SMEM] + [ANYWHERE] * (3 + len(after)),
        out_specs=(ANYWHERE, ANYWHERE),
        out_shape=(shape((2, 2, 2, HALF, BLOCK), BF), shape((2, 2, 2, HALF, BLOCK), BF)),
        scratch_shapes=[
            pltpu.VMEM((2, PATCHES, HALF), BF),
            pltpu.VMEM((HALF, 2 * PATCHES), BF),
            pltpu.VMEM((4, 2 * PATCHES, SPAN), BF),
            pltpu.VMEM((2, HALF, SPAN), BF),
            pltpu.SemaphoreType.DMA((5, 2)),
            pltpu.SemaphoreType.DMA((2, 4)),
        ],
        compiler_params=params(),
        cost_estimate=cost(),
        name=name,
    )(place, left, *right, *after)


ROWS = D // SPANS
PARTS = 4 * ROWS
CROSS = ROWS


def square_kernel(
    place_ref,
    tail_own,
    tail_beside,
    heads_own,
    heads_beside,
    pack_own,
    pack_beside,
    right_own,
    right_beside,
    *refs,
):
    send_any, keep_any, cross_send_any, cross_keep_any = refs[-9:-5]
    left_ref, right_ref, product_ref, sems, out_sems = refs[-5:]
    pipe, place = place_ref[0], place_ref[1]
    side, z = jnp.bitwise_and(place, 1), lax.shift_right_logical(place, 1)
    lefts = [
        (pack_own.at[pl.ds(0, D)], pack_beside.at[pl.ds(0, D)]),
        (pack_own.at[pl.ds(D, D)], pack_beside.at[pl.ds(D, D)]),
        (heads_own, heads_beside),
    ]
    left_copies = [
        [
            copy(one, left_ref.at[n, :, pl.ds(m * PATCHES, PATCHES)], sems.at[n, m])
            for m, one in enumerate(pair)
        ]
        for n, pair in enumerate(lefts)
    ]
    right_copies = [
        [
            copy(one.at[n], right_ref.at[n, pl.ds(m * PATCHES, PATCHES)], sems.at[3 + n, m])
            for m, one in enumerate((right_own, right_beside))
        ]
        for n in range(4)
    ]
    for n in (0, 3, 1, 2):
        for one in (left_copies[n] if n < 3 else []) + right_copies[n]:
            one.start()
    right_ref[4, :PATCHES] = tail_own[:PATCHES]
    right_ref[4, PATCHES:] = tail_beside[:PATCHES]

    def put(slot, block):
        return product_ref.at[slot, pl.ds(block * ROWS, ROWS)], out_sems.at[slot, block]

    def wait(slot):
        for block in range(SPANS):
            source, sem = put(slot, block)
            copy(source, send_any.at[0, pl.ds(0, ROWS)], sem).wait()

    def share(slot, part):
        rows = pl.ds(part * ROWS, ROWS)
        for block in range(SPANS):
            source, sem = put(slot, block)
            to_z = jnp.bitwise_xor(block // 2, z)
            start_either(
                side != block % 2, source, send_any.at[to_z, rows], keep_any.at[to_z, rows], sem
            )

    def cross(slot, part, goal):
        rows = pl.ds(part * ROWS, ROWS)
        for block in range(SPANS):
            source, sem = put(slot, block)
            to_side = jnp.bitwise_xor(block % 2, side)
            to_z = jnp.bitwise_xor(block // 2, z)
            start_either(
                pipe != goal,
                source,
                cross_send_any.at[to_side, to_z, rows],
                cross_keep_any.at[to_side, to_z, rows],
                sem,
            )

    product_ref[0] = (tail_own[...].astype(F32) + tail_beside[...].astype(F32)).astype(BF)
    share(0, 1)
    for step, (left, right) in enumerate(((0, 0), (1, 3), (2, 4), (0, 1), (0, 2))):
        slot = (step + 1) % 2
        if step in (0, 1, 2):
            for one in left_copies[left]:
                one.wait()
        if right < 4:
            for one in right_copies[right]:
                one.wait()
        if step >= 1:
            wait(slot)
        for tile in range(2):
            rows = slice(tile * HALF, (tile + 1) * HALF)
            product_ref[slot, rows] = dot(left_ref[left, rows], right_ref[right], 1, 0).astype(BF)
        if step < 3:
            share(slot, (0, 3, 2)[step])
        else:
            cross(slot, 0, step - 3)
    wait(0)
    wait(1)


def square_grads(place, tail, heads, pack, right, after):
    return pl.pallas_call(
        square_kernel,
        in_specs=[SMEM, VMEM, VMEM] + [ANYWHERE] * (6 + len(after)),
        out_specs=(ANYWHERE,) * 4,
        out_shape=(
            shape((4, PARTS, HALF), BF),
            shape((4, PARTS, HALF), BF),
            shape((2, 4, CROSS, HALF), BF),
            shape((2, 4, CROSS, HALF), BF),
        ),
        scratch_shapes=[
            pltpu.VMEM((3, D, 2 * PATCHES), BF),
            pltpu.VMEM((5, 2 * PATCHES, HALF), BF),
            pltpu.VMEM((2, D, HALF), BF),
            pltpu.SemaphoreType.DMA((7, 2)),
            pltpu.SemaphoreType.DMA((2, SPANS)),
        ],
        compiler_params=params(),
        cost_estimate=cost(),
        name="square_grads",
    )(place, *tail, *heads, *pack, *right, *after)


def first_sums_kernel(down_keep, down_came, up_keep, up_came, after_any, down_ref, up_ref):
    for z in range(4):
        at = (0, z // 2, z % 2)
        down_ref[z] = (down_keep[at].astype(F32) + down_came[at].astype(F32)).astype(BF)
        up_ref[z] = (up_keep[at].astype(F32) + up_came[at].astype(F32)).astype(BF)


def first_sums(down_keep, down_came, up_keep, up_came, after):
    half = pl.BlockSpec((1, 2, 2, HALF, BLOCK), lambda i: (1, 0, 0, 0, 0))
    return pl.pallas_call(
        first_sums_kernel,
        grid=(1,),
        in_specs=[half] * 4 + [ANYWHERE],
        out_specs=(VMEM, VMEM),
        out_shape=(shape((4, HALF, BLOCK), BF), shape((4, HALF, BLOCK), BF)),
        compiler_params=params(1),
        cost_estimate=cost(),
        name="first_sums",
    )(down_keep, down_came, up_keep, up_came, after)


def second_sums_kernel(
    down_keep, down_came, down_brought, up_keep, up_came, up_brought, after_any, *outs
):
    def added(keep, came, brought, z):
        at = (0, z // 2, z % 2)
        one = (keep[at].astype(F32) + came[at].astype(F32)).astype(BF).astype(F32)
        return (one + brought[z].astype(F32)).astype(BF)

    for z in range(4):
        outs[z][0] = added(down_keep, down_came, down_brought, z)
        outs[z][1] = added(up_keep, up_came, up_brought, z)


def second_sums(down_keep, down_came, down_brought, up_keep, up_came, up_brought, after):
    half = pl.BlockSpec((1, 2, 2, HALF, BLOCK), lambda i: (0, 0, 0, 0, 0))
    return pl.pallas_call(
        second_sums_kernel,
        grid=(1,),
        in_specs=[half, half, VMEM] * 2 + [ANYWHERE],
        out_specs=(VMEM,) * 4,
        out_shape=(shape((2, HALF, BLOCK), BF),) * 4,
        compiler_params=params(1),
        cost_estimate=cost(),
        name="second_sums",
    )(down_keep, down_came, down_brought, up_keep, up_came, up_brought, after)


def third_sums_kernel(keep, came, out_ref):
    for z in range(4):
        out_ref[z] = (keep[0, z].astype(F32) + came[0, z].astype(F32)).astype(BF)


def third_sums(keep, came):
    half = pl.BlockSpec((1, 4, CROSS, HALF), lambda i: (1, 0, 0, 0))
    return pl.pallas_call(
        third_sums_kernel,
        grid=(1,),
        in_specs=[half, half],
        out_specs=VMEM,
        out_shape=shape((4, CROSS, HALF), BF),
        compiler_params=params(1),
        cost_estimate=cost(),
        name="third_sums",
    )(keep, came)


def fourth_sums_kernel(keep, came, cross_keep, cross_came, brought, *refs):
    for z in range(4):
        out_ref = refs[len(refs) - 4 + z]
        out_ref[:PARTS] = (keep[z].astype(F32) + came[z].astype(F32)).astype(BF)
        one = (cross_keep[0, z].astype(F32) + cross_came[0, z].astype(F32)).astype(BF)
        out_ref[PARTS:] = (one.astype(F32) + brought[z].astype(F32)).astype(BF)


def fourth_sums(keep, came, cross_keep, cross_came, brought, after):
    half = pl.BlockSpec((1, 4, CROSS, HALF), lambda i: (0, 0, 0, 0))
    return pl.pallas_call(
        fourth_sums_kernel,
        grid=(1,),
        in_specs=[VMEM, VMEM, half, half, VMEM] + [ANYWHERE] * len(after),
        out_specs=(VMEM,) * 4,
        out_shape=(shape((PARTS + CROSS, HALF), BF),) * 4,
        compiler_params=params(1),
        cost_estimate=cost(),
        name="fourth_sums",
    )(keep, came, cross_keep, cross_came, brought, *after)


def finish_kernel(
    chips,
    place_ref,
    tail_ref,
    table_ref,
    query_ref,
    given_ref,
    value_ref,
    attend_ref,
    *refs,
):
    brought = [(refs[2 * n], refs[2 * n + 1]) for n in range(3)]
    position_ref, gain_ref, bias_ref, output_ref, hidden_ref = refs[6:11]
    embed_ref, variable_ref, attend_grad_ref, query_grad_ref = refs[11:15]
    weight_ref, whole_ref, mix_ref, rows_ref, turned_ref, sems = refs[15:]
    core, chip, spot = place_ref[1], place_ref[3], place_ref[4]
    wait = section_copies(
        place_ref,
        0,
        [attend_ref.at[j] for j in range(3)],
        brought,
        [weight_ref.at[j] for j in range(3)],
        sems,
    )
    part = TAIL // chips
    for c in range(2):
        for n in range(chips):
            whole_ref[c, n * part : (n + 1) * part, :] = tail_ref[
                jnp.bitwise_xor(c, core), jnp.bitwise_xor(n, chip)
            ].astype(F32)
    for c in range(2):
        columns = slice(c * HALF, (c + 1) * HALF)
        position_ref[:, columns] = whole_ref[c, :PATCHES, :]
        small = whole_ref[c, SMALL_AT:KEYS_AT, :]
        gain_ref[:, columns] = small[0:2]
        bias_ref[:, columns] = small[2:4]
        output_ref[:, columns] = small[4:5]
        hidden_ref[:, columns] = small[5:9]
        for n in range(2):
            start = c * HALF + n * TABLE_PAD
            mix_ref[start : start + TABLE_PAD, :] = whole_ref[
                c, MIX_AT:SMALL_AT, n * TABLE_PAD : (n + 1) * TABLE_PAD
            ].astype(BF)
    keys = whole_ref[0, KEYS_AT:, :HEADS]
    table = table_ref[...].astype(F32)
    grads = lax.dot_general(
        keys,
        table,
        (((0,), (0,)), ((), ())),
        precision=PRECISE,
        preferred_element_type=F32,
    ).astype(BF)
    mask = head_rows(D)
    wait(1)
    low = jnp.where(mask, dot(grads, weight_ref[1], 1, 0), 0.0)
    low = jnp.sum(low, axis=0, keepdims=True) * HDIM ** (-0.5)
    low = jnp.broadcast_to(low, (HEADS, D)).astype(BF)
    wait(0)
    query_grad_ref[...] = dot(low, weight_ref[0], 1, 1)[:1]
    mixed = mix_ref[...]
    wait(2)
    key_query = value_ref[...].astype(F32)[:, ROWS_TABLE:]
    table_grad = dot(mixed, weight_ref[2], 0, 1)[:ROWS_TABLE] + lax.dot_general(
        keys,
        key_query,
        (((1,), (1,)), ((), ())),
        precision=PRECISE,
        preferred_element_type=F32,
    )
    for k in range(PIECES):
        embed_ref[:, k, :] = table_grad[k * VARS : (k + 1) * VARS]
    variable_ref[...] = table_grad[PIECES * VARS :]
    size = attend_grad_ref.shape[1]
    rows = pl.ds(pl.multiple_of(spot * size, size), size)
    rows_ref[...] = jnp.concatenate([grads.astype(F32), given_ref[...]], axis=0).T
    turned_ref[...] = table.T
    own = rows_ref[rows, :]
    low = low.astype(F32)
    spread = jnp.where(mask, query_ref[...] * HDIM ** (-0.5), 0.0)
    attend_grad_ref[0] = own[:, HEADS : HEADS + 1] * low[:1]
    attend_grad_ref[1] = lax.dot_general(
        own[:, :HEADS],
        spread,
        (((1,), (0,)), ((), ())),
        precision=PRECISE,
        preferred_element_type=F32,
    )
    left = jnp.concatenate(
        [turned_ref[rows, :], jnp.zeros((size, TABLE_PAD - ROWS_TABLE), F32)], axis=1
    ).astype(BF)
    attend_grad_ref[2] = dot(left, mixed, 1, 1)


def finish(place, tail, table, query, given, value, weights, brought, chips, size):
    return pl.pallas_call(
        functools.partial(finish_kernel, chips),
        out_shape=(
            shape((PATCHES, D), F32),
            shape((2, D), F32),
            shape((2, D), F32),
            shape((1, D), F32),
            shape((FF // D, D), F32),
            shape((VARS, PIECES, D), F32),
            shape((VARS, D), F32),
            shape((3, size, D), F32),
            shape((1, D), F32),
        ),
        in_specs=[SMEM] + [VMEM] * 5 + [ANYWHERE] * 7,
        out_specs=(VMEM,) * 9,
        scratch_shapes=[
            pltpu.VMEM((3, D, D), BF),
            pltpu.VMEM((2, TAIL, HALF), F32),
            pltpu.VMEM((D, TABLE_PAD), BF),
            pltpu.VMEM((D, 2 * HEADS), F32),
            pltpu.VMEM((D, ROWS_TABLE), F32),
            pltpu.SemaphoreType.DMA((3, 4)),
        ],
        compiler_params=params(),
        cost_estimate=cost(),
        name="finish",
    )(place, tail, table, query, given, value, weights, *brought)


def partner(block, axis, distance):
    size = lax.axis_size(axis)
    return lax.ppermute(block, axis, [(i, i ^ distance) for i in range(size)])


def swap(block):
    return partner(block, "pipe", 1)


def pick(array, index, axis=0):
    return lax.dynamic_index_in_dim(array, index, axis, keepdims=False)


def tree_sum(terms):
    while len(terms) > 1:
        terms = [terms[2 * i] + terms[2 * i + 1] for i in range(len(terms) // 2)]
    return terms[0]


class Places:
    def __init__(self):
        self.pipe = lax.axis_index("pipe")
        self.dp = lax.axis_index("dp")
        self.size = lax.axis_size("dp")
        self.core = self.dp % 2
        self.chips = self.size // 2
        bits = self.size.bit_length() - 2
        low = bits % 2 if bits % 2 else 2
        self.groups = []
        at = 1
        while bits > 0:
            width = low if at == 1 else 2
            self.groups.append((at, width))
            at += width
            bits -= width

    def relative(self, array, place):
        for bit in range(array.shape[0].bit_length() - 1):
            paired = array.reshape(-1, 2, 2**bit, *array.shape[1:])
            flipped = jnp.where((place // 2**bit) % 2 == 1, paired[:, ::-1], paired)
            array = flipped.reshape(array.shape)
        return array

    def grouped(self, array):
        counts = [2**width for _, width in reversed(self.groups)]
        dims = array.shape[1:]
        array = array.reshape(*counts, *dims)
        order = list(range(len(counts)))[::-1] + list(range(len(counts), array.ndim))
        return array.transpose(order)

    def reduced(self, array, groups):
        for n, (at, width) in enumerate(groups):
            terms = [array[0].astype(F32)]
            for distance in range(1, 2**width):
                terms.append(partner(array[distance], "dp", distance * 2**at).astype(F32))
            array = tree_sum(terms)
            if n < len(groups) - 1:
                array = array.astype(BF)
        return array

    def over_cores(self, array):
        brought = partner(pick(array, 1 - self.core).astype(BF), "dp", 1).astype(F32)
        own = pick(array, self.core)
        return jnp.concatenate(
            [jnp.where(self.core == 0, own, brought), jnp.where(self.core == 0, brought, own)],
            axis=-1,
        )

    def last(self, parts, group):
        terms = [parts[0].astype(F32)]
        for distance in range(1, 2 ** group[1]):
            terms.append(partner(parts[distance], "dp", distance * 2 ** group[0]).astype(F32))
        return tree_sum(terms)

    def gather(self, block):
        blocks = block[None]
        for at, width in reversed(self.groups):
            parts = [partner(blocks, "dp", m * 2**at) for m in range(1, 2**width)]
            blocks = jnp.stack([blocks] + parts, axis=1).reshape(-1, *block.shape)
        return blocks

    def round(self, block, bit):
        return block + partner(block, "dp", 2**bit)


def on_device(
    fields,
    item_weights,
    live_counts,
    running_stats,
    embed_weight,
    variable_embed,
    variable_query,
    attend_weight,
    merge_weight,
    position_embed,
    norm_gain,
    norm_bias,
    up_weight,
    hidden_bias,
    down_weight,
    output_bias,
    cotangent,
):
    at = Places()
    pipe, core = at.pipe, at.core
    first = pipe == 0
    side = (at.dp // 2) % 2
    chip = at.dp // 2
    place = jnp.stack([pipe, core, side]).astype(jnp.int32)
    micro, half_vars, rows, cols = fields.shape
    scale_heads = HDIM ** (-0.5)

    own_attend, own_merge = attend_weight[0], merge_weight[0]

    def quarter(weight):
        return lax.dynamic_slice_in_dim(weight, (2 * core + side) * QUARTER, QUARTER, 0)

    def quarter_of(j):
        start = (jnp.int32(j), (2 * core + side) * QUARTER, jnp.int32(0))
        return lax.dynamic_slice(own_attend, start, (1, QUARTER, D))[0]

    def after(value, *others):
        return lax.optimization_barrier((value, others))[0]

    def passed_on(block, before, behind):
        other = partner(after(block, *before), "dp", 2)
        pair = jnp.stack([block, after(other, *behind)])
        return pair, partner(pair, "dp", 1)

    chunk_first = swap(jnp.where(first, quarter(own_merge), quarter_of(0)))

    table = jnp.concatenate(
        [embed_weight.transpose(1, 0, 2).reshape(VARS * PIECES, D), variable_embed], axis=0
    )
    given = variable_query.astype(F32).reshape(1, D)
    query, table_keys, table_value = tables(given, table, own_attend)

    def from_first(block):
        return jnp.where(first, block, lax.ppermute(block, "pipe", [(0, 1)]))

    keys = from_first(table_keys)
    tvt = from_first(table_value.astype(BF))

    flat_fields = fields.reshape(micro, half_vars * rows, cols)
    other_fields = swap(pick(flat_fields, 1 - pipe))
    own_fields = pick(flat_fields, pipe)
    slots = jnp.arange(micro, dtype=jnp.int32)
    alive = (slots < live_counts[0]).astype(F32)
    omega = item_weights.astype(F32) * alive
    plain_sums = jnp.sum(fields, axis=(2, 3))
    square_sums = jnp.sum(fields * fields, axis=(2, 3))
    sums = jnp.concatenate(
        [
            jnp.sum(omega[:, None] * plain_sums, axis=0),
            jnp.sum(omega[:, None] * square_sums, axis=0),
            jnp.sum(omega)[None],
            jnp.sum(alive)[None],
        ]
    )
    sums = sums_y = at.round(after(sums, table_value), 1)
    for bit in range(2, at.size.bit_length() - 1):
        sums = at.round(sums, bit)
    second = swap(after(jnp.where(first, quarter_of(2), quarter_of(1)), chunk_first))
    sums = at.round(after(sums, second), 0)
    total, live_total = sums[2 * half_vars], sums[2 * half_vars + 1]
    first_moment = sums[:half_vars] / (total * rows * cols)
    second_moment = sums[half_vars : 2 * half_vars] / (total * rows * cols)
    center_new = (1.0 - MOMENTUM) * running_stats[0] + MOMENTUM * first_moment
    spread_new = (1.0 - MOMENTUM) * running_stats[1] + MOMENTUM * (
        second_moment - first_moment * first_moment
    )
    statistics = jnp.stack([center_new, spread_new])
    other_statistics = swap(statistics)
    all_statistics = jnp.concatenate(
        [
            jnp.where(first, statistics, other_statistics),
            jnp.where(first, other_statistics, statistics),
        ],
        axis=1,
    )
    center = all_statistics[0].reshape(VARS, 1)
    scale = lax.rsqrt(all_statistics[1] + EPSILON).reshape(VARS, 1)
    weight_hat = pick(omega, pipe) * live_total / total
    alive_own = pick(alive, pipe)[None]
    out_low = (pick(cotangent, pipe).astype(F32) * weight_hat).astype(BF)

    passed = [passed_on(chunk_first, (sums_y,), ())]
    passed.append(passed_on(second, (), ()))
    third = swap(after(jnp.where(first, quarter_of(0), quarter_of(2)), second))
    fourth = swap(
        after(jnp.where(first, quarter_of(1), quarter(own_merge)), third, passed[0][0])
    )
    alive_own = after(alive_own, third)

    tokens, heads, shares, pixels = aggregate(
        place,
        alive_own,
        own_fields,
        other_fields,
        center,
        scale,
        keys,
        tvt,
        position_embed,
        (own_merge, *passed[0]),
    )
    passed.append(passed_on(third, (), (tokens,)))
    heads_beside = partner(heads, "dp", 1)
    brought = [block for pair in passed for block in pair]
    pack, proj, lse = attend(place, tokens, norm_gain, norm_bias, own_attend, brought)
    passed.append(passed_on(fourth, (tokens,), (lse,)))
    brought = [block for pair in passed for block in pair]
    pack_beside = partner(pack, "dp", 1)
    units, middle, second_low, hidden_sum = expand(
        place,
        tokens,
        out_low,
        norm_gain,
        norm_bias,
        pack,
        (own_merge, *brought[6:]),
        up_weight,
        hidden_bias,
        down_weight,
        heads_beside,
    )
    units_beside = partner(units, "dp", 1)
    scalars = jnp.stack([alive_own[0], weight_hat])
    result, middle_grad, branch_low, gain_second, bias_second, output_sum = contract(
        place,
        scalars,
        units,
        up_weight,
        down_weight,
        middle,
        cotangent,
        norm_gain[1:2],
        output_bias.reshape(1, D),
    )
    ff_width = FF // (2 * at.size)
    d_width = D // at.size
    direct = 2 * at.chips == BLOCKS
    wide_place = jnp.stack([pipe * SPANS + chip if direct else 0 * chip, core]).astype(jnp.int32)
    square_place = jnp.stack([pipe, chip if direct else 0 * chip]).astype(jnp.int32)
    both_units = (units, units_beside)
    down_send, down_keep = wide_grads(
        wide_place,
        out_low,
        both_units,
        0,
        True,
        (branch_low,),
        "down_grads",
    )
    up_send, up_keep = wide_grads(
        wide_place,
        second_low,
        both_units,
        1,
        False,
        (down_keep,),
        "up_grads",
    )
    right_own, right_send, token_grad, gain_first, bias_first = attend_back(
        place,
        middle_grad,
        branch_low,
        proj,
        lse,
        tokens,
        norm_gain,
        own_attend,
        own_merge,
        brought,
        (down_keep, up_keep),
    )
    right_beside = partner(right_send, "dp", 1)
    tail_own, tail_send, field_grads = aggregate_back(
        place,
        alive_own,
        token_grad,
        pixels,
        keys,
        tvt,
        shares,
        (gain_first, gain_second, bias_first, bias_second, output_sum, hidden_sum),
        (own_merge, *passed[0]),
    )
    tail_beside = partner(tail_send, "dp", 1)

    if direct:
        groups = at.groups[1:]
        down_came, up_came = swap(down_send), partner(up_send, "dp", 2)
        down_next, up_next = first_sums(down_keep, down_came, up_keep, up_came, tail_own)
        down_brought = partner(down_next, "dp", 2)
        up_brought = swap(up_next)
        started = (down_next, up_next)
    else:
        groups = at.groups
        started = (down_keep, up_keep)

        def spread(array):
            array = array.transpose(4, 0, 1, 2, 3, 5).reshape(HALF, 2 * at.chips, -1)
            array = at.relative(array.transpose(1, 0, 2), pipe * at.chips + chip)
            array = array.reshape(2, at.chips, HALF, -1)
            total = array[0].astype(F32) + swap(array[1]).astype(F32)
            return at.grouped(total.astype(BF))

        down_wide = jnp.stack([down_keep, down_send]).transpose(0, 2, 3, 1, 4, 5)
        wide = [spread(down_wide), spread(jnp.stack([up_keep, up_send], axis=3))]

    send, keep, cross_send, cross_keep = square_grads(
        square_place,
        (tail_own, tail_beside),
        (heads, heads_beside),
        (pack, pack_beside),
        (right_own, right_beside),
        started,
    )
    if direct:
        wide = second_sums(
            down_keep, down_came, down_brought, up_keep, up_came, up_brought, send
        )
        shared = partner(after(send, wide), "dp", 2)
        crossed = swap(after(cross_send, wide))
        wide = at.last(wide, groups[0])
        cross_next = third_sums(cross_keep, crossed)
        cross_brought = partner(cross_next, "dp", 2)
        field_grads, result = after((field_grads, result), cross_next)
        came = swap(jnp.where(first, result, tokens))
        field_halves = field_grads.reshape(2, half_vars, rows, cols)
        field_came = swap(pick(field_halves, 1 - pipe).astype(BF)).astype(F32)
        square = fourth_sums(
            keep, shared, cross_keep, crossed, cross_brought, (came, field_came, wide)
        )
        square = at.last(square, groups[0])
    else:
        wide = jnp.stack([at.reduced(array, groups) for array in wide])

        def rows_of(array):
            return at.relative(array.reshape(at.chips, -1, HALF), chip)

        whole = jnp.stack([keep, send], axis=1).reshape(SPANS, PARTS, HALF)
        cross = (cross_keep.astype(F32) + swap(cross_send).astype(F32)).astype(BF)
        cross = cross.transpose(1, 0, 2, 3).reshape(SPANS, CROSS, HALF)
        square = [rows_of(whole[:, n * ROWS : (n + 1) * ROWS]) for n in range(4)]
        square.append(rows_of(cross))
        square = at.reduced(at.grouped(jnp.concatenate(square, axis=1)), groups)
        came = swap(jnp.where(first, result, tokens))
        field_halves = field_grads.reshape(2, half_vars, rows, cols)
        field_came = swap(pick(field_halves, 1 - pipe).astype(BF)).astype(F32)

    wide = wide.reshape(2, HALF, 2, ff_width)
    other = partner(pick(wide, 1 - core, 2).astype(BF), "dp", 1).astype(F32)
    own = pick(wide, core, 2)
    wide = jnp.concatenate(
        [jnp.where(core == 0, own, other), jnp.where(core == 0, other, own)], axis=1
    )
    down_part, up_part = wide[0].T, wide[1]

    lot = 2 * d_width
    part = TAIL // at.chips
    query_part = square[:lot]
    tail = square[lot : lot + part]
    merge_one = square[lot + part : 2 * lot + part]
    merge_two = square[2 * lot + part : 3 * lot + part]
    cross = square[3 * lot + part :]
    tail_came = swap(tail.astype(BF)).astype(F32)
    sent = jnp.concatenate(
        [jnp.where(first, merge_two, merge_one), query_part, cross], axis=0
    ).astype(BF)
    section_came = swap(sent).astype(F32)
    section_sum = jnp.stack(
        [
            jnp.where(first, merge_one, merge_two) + section_came[:lot],
            query_part + section_came[lot : 2 * lot],
            section_came[2 * lot :],
            cross,
        ]
    )
    tail = (tail.astype(BF).astype(F32) + tail_came).astype(BF)
    section_sum = section_sum.reshape(4, 2, d_width, HALF).transpose(1, 0, 2, 3)
    section_part = at.over_cores(section_sum)
    merge_part = section_part[0]
    second_attend = section_part[1:]

    tail = at.gather(tail)
    tail = jnp.stack([tail, partner(tail, "dp", 1)])
    spot = jnp.stack([pipe, core, side, chip, at.dp]).astype(jnp.int32)
    (
        position_sum,
        gain_sum,
        bias_sum,
        output_sum,
        hidden_sum,
        embed_grads,
        variable_grads,
        first_attend,
        query_sum,
    ) = finish(
        spot,
        tail,
        table,
        query,
        jnp.broadcast_to(given, (HEADS, D)),
        tvt,
        own_attend,
        [*passed[2], *passed[3], *passed[1]],
        at.chips,
        d_width,
    )
    attend_part = jnp.where(first, first_attend, second_attend)
    hidden_sum = hidden_sum.reshape(FF)

    outputs = jnp.stack([jnp.where(first, tokens, came), jnp.where(first, came, result)])
    field_own = pick(field_halves, pipe)
    own_scale = lax.rsqrt(spread_new + EPSILON)
    field_out = (
        jnp.stack(
            [
                jnp.where(first, field_own, field_came),
                jnp.where(first, field_came, field_own),
            ]
        )
        * own_scale[None, :, None, None]
    )
    hidden_part = lax.dynamic_slice_in_dim(
        hidden_sum, (pipe * at.size + at.dp) * ff_width, ff_width
    )
    return (
        statistics,
        outputs[None],
        field_out,
        embed_grads,
        variable_grads,
        query_sum.reshape(D),
        attend_part[None],
        merge_part[None],
        position_sum,
        gain_sum,
        bias_sum,
        up_part,
        hidden_part,
        down_part,
        output_sum.reshape(D),
    )


def solution(mesh):
    return jax.shard_map(
        on_device,
        mesh=mesh,
        in_specs=(
            P("dp", "pipe", None, None),
            P("dp"),
            P("dp"),
            P(None, "pipe"),
            P(),
            P(),
            P(),
            P("pipe", None, None, None),
            P("pipe", None, None),
            P(),
            P(),
            P(),
            P(),
            P(),
            P(),
            P(),
            P("dp", None, None),
        ),
        out_specs=(
            P(None, "pipe"),
            P("pipe", "dp", None, None),
            P("dp", "pipe", None, None),
            P(),
            P(),
            P(),
            P("pipe", None, "dp", None),
            P("pipe", "dp", None),
            P(),
            P(),
            P(),
            P(None, ("pipe", "dp")),
            P(("pipe", "dp")),
            P(("pipe", "dp"), None),
            P(),
        ),
        check_vma=False,
    )
```
